128 devices in a mesh: group: 8 (over x_hi, y), tp: 16 (over x_lo, z, core).
Axes of the slice: x: 4 (x_hi: 2, x_lo: 2; x = x_hi * 2 + x_lo), y: 4, z: 4, core: 2. Of those that a mesh axis runs over, the one named last changes fastest.
Arguments:
- master: float32 [8192, 32768], P(None, ('group', 'tp')), may hold values from -0.5524272 to 0.5524272
- activations: bfloat16 [2048, 8192], P('group', 'tp'), may hold values from -6 to 6
- owner: int32 [8], replicated, may hold values from 0 to 7, each once
Outputs:
- hidden: bfloat16 [2048, 32768], P('group', 'tp')
The draws below stay inside these ranges and needn't reach their ends.
Inputs may be any that keep to these rules, and one draw needn't show every extreme that they name: `owner`: every section owns exactly one span.
All inputs are finite; a program needn't handle non-finite values.
Results may differ from the reference program's by a relative error of at most 0.022.
Values may be sent and summed in bfloat16 or wider, within the bound.
No kernel may reach another device: no remote copies, remote signals or barrier semaphores. Data moves between devices by JAX's collectives and lax.ppermute only.
A program may use at most 320 MiB of HBM per device.

```python
import math
import jax
import jax.numpy as jnp
from jax import lax

D = 8192
FF = 32768
BLOCK = 128
TOKENS = 2048
SPAN = 4096
N_GROUP = 8
N_TP = 16


def draw_master(key, part):
    key = jax.random.fold_in(key, 7)
    keys = jax.random.split(key, 5)
    base = jnp.clip(jax.random.normal(keys[0], (D, FF), jnp.float32), -6.0, 6.0)
    top = 10.0
    row_block = jnp.exp(jax.random.uniform(keys[1], (D // BLOCK,), jnp.float32, 0.0, math.log(top)))
    col_block = jnp.exp(jax.random.uniform(keys[2], (FF // BLOCK,), jnp.float32, 0.0, math.log(top)))
    row_jitter = jax.random.uniform(keys[3], (D,), jnp.float32, 0.5, 1.0)
    col_jitter = jax.random.uniform(keys[4], (FF,), jnp.float32, 0.5, 1.0)
    rows = jnp.repeat(row_block, BLOCK) * row_jitter
    cols = jnp.repeat(col_block, BLOCK) * col_jitter
    return base * rows[:, None] * cols[None, :] * (1.0 / (12.0 * math.sqrt(D)))


def block_levels(key, dims, cuts, smallest, top_value):
    gain = 1.0
    for axis_at, blocks in cuts:
        steps = jax.random.uniform(jax.random.fold_in(jax.random.fold_in(key, 6), axis_at), (blocks,), jnp.float32, smallest / len(cuts), top_value / len(cuts))
        gain = gain * jnp.repeat(jnp.exp(steps), dims[axis_at] // blocks).reshape((-1,) + (1,) * (len(dims) - 1 - axis_at))
    return gain


def scatter_about(rng, shape, spread, most, pieces=(), held_as=jnp.bfloat16):
    array = spread * jax.random.normal(rng, shape, jnp.float32)
    if pieces:
        array = array * block_levels(rng, shape, pieces, -0.22, 0.18)
    return jnp.clip(array, -most, most).astype(held_as)


def setup_inputs(seed: int = 0) -> dict:
    streams_of = jax.random.split(jax.random.key(seed), 4)
    master = draw_master(jax.random.fold_in(streams_of[3], 71), 0)
    activations = scatter_about(streams_of[1], (TOKENS, D), 1.0, 6.0, ((0, 8), (1, 16)))
    owner = jax.random.permutation(streams_of[2], N_GROUP).astype(jnp.int32)
    return {"master": master, "activations": activations, "owner": owner}


def quantize(master, block):
    rows, cols = master.shape
    tiles = master.reshape(rows // block, block, cols // block, block)
    amax = jnp.max(jnp.abs(tiles), axis=(1, 3))
    scales = ((amax + 1e-6) / 448.0).astype(jnp.bfloat16)
    coded = (tiles / scales.astype(jnp.float32)[:, None, :, None]).astype(jnp.bfloat16)
    return coded.reshape(rows, cols), scales


def scaled_product(acts, coded, scales, block):
    count = acts.shape[0]
    cols = coded.shape[1]

    def step(index, total):
        start = index * block
        left = lax.dynamic_slice_in_dim(acts, start, block, 1)
        right = lax.dynamic_slice_in_dim(coded, start, block, 0)
        scale_row = lax.dynamic_slice_in_dim(scales, index, 1, 0)[0].astype(jnp.float32)
        product = jnp.dot(left, right, preferred_element_type=jnp.float32)
        return total + product.reshape(count, cols // block, block) * scale_row[None, :, None]

    start_total = jnp.zeros((count, cols // block, block), jnp.float32)
    total = lax.fori_loop(0, coded.shape[0] // block, step, start_total)
    return total.reshape(count, cols)


def grouped_sum(acts, coded, scales, groups, block):
    share = coded.shape[0] // groups

    def step(index, total):
        left = lax.dynamic_slice_in_dim(acts, index * share, share, 1)
        right = lax.dynamic_slice_in_dim(coded, index * share, share, 0)
        scale_rows = lax.dynamic_slice_in_dim(scales, index * (share // block), share // block, 0)
        term = lax.optimization_barrier(scaled_product(left, right, scale_rows, block).astype(jnp.bfloat16))
        return total + term.astype(jnp.float32)

    start_total = jnp.zeros((acts.shape[0], coded.shape[1]), jnp.float32)
    return lax.fori_loop(0, groups, step, start_total)


def reference(master, activations, owner):
    coded, scales = quantize(master, BLOCK)
    served = jnp.take(coded.reshape(D, N_GROUP, SPAN), owner, axis=1).reshape(D, FF)
    served_scales = jnp.take(scales.reshape(D // BLOCK, N_GROUP, SPAN // BLOCK), owner, axis=1).reshape(D // BLOCK, FF // BLOCK)
    total = grouped_sum(activations, served, served_scales, N_TP, BLOCK)
    return total.astype(jnp.bfloat16)
```

```python
import functools

import jax
import jax.numpy as jnp
from jax import lax
from jax.experimental import pallas as pl
from jax.experimental.pallas import tpu as pltpu
from jax.sharding import PartitionSpec as P

BLOCK = 128
AXES = ("group", "tp")
N_DEV = 128
PARTS = {"z": (0, 96), "y": (96, 80), "x": (176, 80)}
ORDER = {"z": "xyz", "y": "zxy", "x": "yzx"}
SLOTS = 4


def coords(i):
    xh, y, xl, z, core = i // 64, i // 16 % 4, i // 8 % 2, i // 2 % 4, i % 2
    return xh * 2 + xl, y, z, core


def linear(x, y, z, core):
    return (x // 2) * 64 + (y % 4) * 16 + (x % 2) * 8 + (z % 4) * 2 + core


def permute(value, move):
    return lax.ppermute(value, AXES, [(i, move(*coords(i))) for i in range(N_DEV)])


def along(axis, sign):
    def move(x, y, z, core):
        step = sign if core == 0 else -sign
        x, y, z = (x + step) % 4 if axis == "x" else x, y + step if axis == "y" else y, z + step if axis == "z" else z
        return linear(x, y, z, core)

    return move


def offset(slot, core):
    return (0, 1 if core else 3, 3 if core else 1, 2)[slot]


def ring(block, axis):
    first = permute(block, along(axis, 1))
    second = permute(block, along(axis, -1))
    relayed = permute(first, along(axis, 1))
    return [block, first, second, relayed]


def gather(block, order):
    for axis in order[:2]:
        block = jnp.concatenate(ring(block, axis), axis=0)
    return ring(block, order[2])


def refit_kernel(table, master, out):
    for r in range(master.shape[0] // BLOCK):
        for c in range(master.shape[1] // BLOCK):
            at = (pl.ds(r * BLOCK, BLOCK), pl.ds(c * BLOCK, BLOCK))
            tile = master[at]
            amax = jnp.max(jnp.abs(tile), axis=(0, 1), keepdims=True)
            scale = ((amax + 1e-6) / 448.0).astype(jnp.bfloat16).astype(jnp.float32)
            coded = (tile * (1.0 / scale)).astype(jnp.bfloat16)
            out[at] = (coded.astype(jnp.float32) * scale).astype(jnp.bfloat16)


def refit(master, chunks, share):
    cols = master.shape[1]
    return pl.pallas_call(
        refit_kernel,
        grid_spec=pltpu.PrefetchScalarGridSpec(
            num_scalar_prefetch=1,
            grid=(8,),
            in_specs=[pl.BlockSpec((share, cols), lambda i, t: (t[i], 0))],
            out_specs=pl.BlockSpec((share, cols), lambda i, t: (i, 0)),
        ),
        out_shape=jax.ShapeDtypeStruct((8 * share, cols), jnp.bfloat16),
        cost_estimate=pl.CostEstimate(flops=8 * share * cols * 6, bytes_accessed=8 * share * cols * 6, transcendentals=0),
    )(chunks, master)


def product_kernel(where, mine, theirs, *refs):
    blocks, (out_mine, out_theirs, held, sems) = refs[:12], refs[12:]
    z_part, y_part, x_part = blocks[0:4], blocks[4:8], blocks[8:12]
    core, swap = where[0], where[1]

    def source_slot(xh, xl):
        if xl == 0:
            return 2 + 1 if xh else 0
        return jnp.where(swap == xh, 1, 2)

    def copies(n, go):
        xl, zs = n // 4, n % 4
        buf = n % 2
        sem = sems.at[buf]
        z0, zn = PARTS["z"]
        y0, yn = PARTS["y"]
        x0, xn = PARTS["x"]
        for xh in range(2):
            sx = source_slot(xh, xl)
            for ys in range(4):
                go(z_part[zs].at[ys * 4 + sx], held.at[buf, xh, ys, pl.ds(z0, zn)], sem)
                go(y_part[ys].at[sx * 4 + zs], held.at[buf, xh, ys, pl.ds(y0, yn)], sem)
            dst = held.at[buf, xh, :, pl.ds(x0, xn)]
            if xl == 0:
                go(x_part[sx].at[pl.ds(zs * 4, 4)], dst, sem)
            else:

                @pl.when(swap == xh)
                def _():
                    go(x_part[1].at[pl.ds(zs * 4, 4)], dst, sem)

                @pl.when(swap != xh)
                def _():
                    go(x_part[2].at[pl.ds(zs * 4, 4)], dst, sem)

    def start(src, dst, sem):
        pltpu.make_async_copy(src, dst, sem).start()

    copies(0, start)
    total_refs = (out_mine, out_theirs)
    for n in range(8):
        buf = n % 2
        pltpu.make_async_copy(held.at[buf], held.at[buf], sems.at[buf]).wait()
        if n < 7:
            copies(n + 1, start)
        rows = pl.ds(n * 512, 512)

        def body(g, _):
            xh, ys = g // 4, g % 4
            dy = jnp.where(ys == 0, 0, jnp.where(ys == 3, 2, jnp.where((ys == 1) == (core == 1), 1, 3)))
            acts = held[buf, xh, ys]
            for weight, total in ((mine, out_mine), (theirs, out_theirs)):
                product = jnp.dot(acts, weight[rows, :], preferred_element_type=jnp.float32)
                if n == 0:
                    total[xh, dy] = product
                else:
                    total[xh, dy] += product
            return 0

        lax.fori_loop(0, 8, body, 0)


def product(where, mine, theirs, blocks):
    out = jax.ShapeDtypeStruct((2, 4, 256, 256), jnp.float32)
    vmem = pl.BlockSpec(memory_space=pltpu.VMEM)
    return pl.pallas_call(
        product_kernel,
        in_specs=[pl.BlockSpec(memory_space=pltpu.SMEM), vmem, vmem] + [pl.BlockSpec(memory_space=pl.ANY)] * 12,
        out_specs=[vmem, vmem],
        out_shape=[out, out],
        scratch_shapes=[pltpu.VMEM((2, 2, 4, 256, 512), jnp.bfloat16), pltpu.SemaphoreType.DMA((2,))],
        compiler_params=pltpu.CompilerParams(vmem_limit_bytes=48 * 1024 * 1024),
        cost_estimate=pl.CostEstimate(flops=2 * 2048 * 4096 * 512, bytes_accessed=30 * 1024 * 1024, transcendentals=0),
    )(where, mine, theirs, *blocks)


def shards(master, activations, owner):
    group, tp = lax.axis_index("group"), lax.axis_index("tp")
    xh, y = group // 4, group % 4
    xl, z, core = tp // 8, tp // 2 % 4, tp % 2
    share = activations.shape[1]

    def chunks(c):
        table = []
        for n in range(8):
            zs = n % 4
            dz = jnp.where(c == 1, offset(zs, 1), offset(zs, 0))
            table.append((xl ^ (n // 4)) * 8 + (z + dz) % 4 * 2 + c)
        return jnp.stack(table).astype(jnp.int32)

    sent = refit(master, chunks(1 - core), share)
    mine = refit(master, chunks(core), share)
    theirs = permute(sent, lambda x, y, z, c: linear(x, y, z, 1 - c))

    blocks = []
    for axis in "zyx":
        at, count = PARTS[axis]
        blocks += gather(activations[None, at : at + count], ORDER[axis])

    where = jnp.stack([core, (xl == core).astype(jnp.int32)]).astype(jnp.int32)
    kept, passed = product(where, mine, theirs, blocks)
    passed = permute(passed.astype(jnp.bfloat16), lambda x, y, z, c: linear(x, y, z, 1 - c))
    total = (kept + passed.astype(jnp.float32)).astype(jnp.bfloat16)

    parts = []
    for eh in range(2):
        for dy in range(4):
            part = total[eh, dy]
            if eh or dy:
                part = permute(part, lambda x, y, z, c: linear((x + 2 * eh) % 4, y + dy, z, c))
            parts.append(part)
    parts = jnp.stack(parts)

    out = {}
    for dz in range(4):
        for cross in range(2):

            def move(x, y, z, c):
                return linear(x ^ (c ^ cross), y, z + dz, x % 2)

            dest = (xl ^ core ^ cross) * 4 + (z + dz) % 4
            section = owner[dest]
            index = ((section // 4) ^ xh) * 4 + (y - section % 4) % 4
            value = lax.dynamic_index_in_dim(parts, index, 0, keepdims=False)
            out[dz, cross] = permute(value, move)
    stacked = jnp.stack([out[dz, cross] for dz in range(4) for cross in range(2)])
    columns = []
    for zs in range(4):
        for c in range(2):
            cross = (xl ^ core) ^ c
            columns.append(lax.dynamic_index_in_dim(stacked, (z - zs) % 4 * 2 + cross, 0, keepdims=False))
    return jnp.concatenate(columns, axis=1)


def solution(mesh):
    in_specs = (P(None, ("group", "tp")), P("group", "tp"), P())
    out_specs = P("group", "tp")
    return jax.shard_map(shards, mesh=mesh, in_specs=in_specs, out_specs=out_specs, check_vma=False)
```

```python
import functools

import jax
import jax.numpy as jnp
import numpy as np
from jax import lax
from jax.experimental import pallas as pl
from jax.experimental.pallas import tpu as pltpu
from jax.sharding import PartitionSpec as P

BLOCK = 128
AXES = ("group", "tp")
N_DEV = 128
SHARE = 512
COLS = 256
PARTS = {"z": (0, 96), "y": (96, 80), "x": (176, 80)}
ORDER = {"z": "xyz", "y": "zxy", "x": "yzx"}
MIB = 1024 * 1024


def coords(i):
    return i // 64 * 2 + i // 8 % 2, i // 16 % 4, i // 2 % 4, i % 2


def linear(x, y, z, core):
    x, y, z = x % 4, y % 4, z % 4
    return x // 2 * 64 + y * 16 + x % 2 * 8 + z * 2 + core


def permute(value, move):
    return lax.ppermute(value, AXES, [(i, move(*coords(i))) for i in range(N_DEV)])


def offset(slot, at, core):
    step = -1 if (at + core) % 2 else 1
    return (0, step, -step, 2)[slot] % 4


def exchange(value, axis, which):
    def move(x, y, z, core):
        at = {"x": x, "y": y, "z": z}
        at[axis] += offset(which, at[axis], core)
        return linear(at["x"], at["y"], at["z"], core)

    return permute(value, move)


def gather(block, order):
    for axis in order[:2]:
        for which in (1, 2):
            block = jnp.concatenate([block, exchange(block, axis, which)], axis=0)
    axis = order[2]
    first = exchange(block, axis, 1)
    second = exchange(block, axis, 2)
    relayed = exchange(first, axis, 2)
    return [v.reshape(4, 4, *v.shape[1:]) for v in (block, first, second, relayed)]


MINE, THEIRS, CORE, SLOT_OFFSET, XH, Y, DEST, SOURCE, WIDTH = 0, 8, 16, 17, 21, 22, 23, 31, 39


def device_row(i):
    x, y, z, core = coords(i)
    xh, xl = x // 2, x % 2

    def chunks(c):
        return [(xl ^ n // 4) * 8 + (z + offset(n % 4, z, c)) % 4 * 2 + c for n in range(8)]

    dest, source = [], []
    for dz in range(4):
        for cross in range(2):
            dest.append((xl ^ core ^ cross) * 4 + (z + dz) % 4)
    for zs in range(4):
        for c in range(2):
            source.append((z - zs) % 4 * 2 + (xl ^ core ^ c))
    row = chunks(core) + chunks(1 - core) + [core] + [offset(s, y, core) for s in range(4)] + [xh, y] + dest + source
    assert len(row) == WIDTH
    return row


def refit_kernel(table, master, out):
    for r in range(master.shape[0] // BLOCK):
        for c in range(master.shape[1] // BLOCK):
            at = (pl.ds(r * BLOCK, BLOCK), pl.ds(c * BLOCK, BLOCK))
            tile = master[at]
            amax = jnp.max(jnp.max(jnp.abs(tile), axis=0, keepdims=True), axis=1, keepdims=True)
            scale = ((amax + 1e-6) / 448.0).astype(jnp.bfloat16).astype(jnp.float32)
            coded = (tile * (1.0 / scale)).astype(jnp.bfloat16)
            out[at] = (coded.astype(jnp.float32) * scale).astype(jnp.bfloat16)


def refit(table, master, first):
    size = 8 * SHARE * COLS
    return pl.pallas_call(
        refit_kernel,
        grid_spec=pltpu.PrefetchScalarGridSpec(
            num_scalar_prefetch=1,
            grid=(8,),
            in_specs=[pl.BlockSpec((SHARE, COLS), lambda i, t: (t[first + i], 0))],
            out_specs=pl.BlockSpec((SHARE, COLS), lambda i, t: (i, 0)),
        ),
        out_shape=jax.ShapeDtypeStruct((8 * SHARE, COLS), jnp.bfloat16),
        cost_estimate=pl.CostEstimate(flops=size * 6, bytes_accessed=size * 6, transcendentals=0),
    )(table, master)


def rows_of(axis):
    at, count = PARTS[axis]
    return pl.ds(at, count)


def product_kernel(slots, n_weights, first, table, *refs):
    refs = list(refs)

    def take(count):
        got = refs[:count]
        del refs[:count]
        return got

    n = len(slots)
    weights = take(n_weights)
    z_part, y_part, x_part = take(n), take(n), take(n)
    before = [None] * n_weights if first else take(n_weights)
    outs = take(n_weights)
    z_held, y_held, x_held, sems = refs
    core = table[CORE]
    halves = ((0, 0), (core, 1), (1 - core, 1), (1, 0))
    zn, yn, xn = (PARTS[a][1] for a in "zyx")

    for i in range(n):
        for sx, (eh, el) in enumerate(halves):
            pltpu.make_async_copy(
                z_part[i].at[:, sx], z_held.at[i, pl.ds(eh * 4, 4), :, pl.ds(el * SHARE, SHARE)], sems.at[i, 0]
            ).start()
            for zs in range(4):
                pltpu.make_async_copy(
                    y_part[i].at[sx, zs], y_held.at[i, eh, :, pl.ds((el * 4 + zs) * SHARE, SHARE)], sems.at[i, 1]
                ).start()
        for zs in range(4):
            pltpu.make_async_copy(
                x_part[i].at[zs], x_held.at[i, :, :, pl.ds(zs * SHARE, SHARE)], sems.at[i, 2]
            ).start()

    def dot(a, b):
        return jnp.dot(a, b, preferred_element_type=jnp.float32)

    def ready(held, i, which):
        pltpu.make_async_copy(held.at[i], held.at[i], sems.at[i, which]).wait()

    z_rows, y_rows, x_rows = rows_of("z"), rows_of("y"), rows_of("x")
    for i, slot in enumerate(slots):
        ready(z_held, i, 0)
        for weight, out, old in zip(weights, outs, before):
            for eh in range(2):
                acts = z_held[i, pl.ds(eh * 4, 4)].reshape(4 * zn, 2 * SHARE)
                got = dot(acts[:, :SHARE], weight[pl.ds(slot * SHARE, SHARE), :])
                got += dot(acts[:, SHARE:], weight[pl.ds((4 + slot) * SHARE, SHARE), :])
                got = got.reshape(4, zn, COLS)
                if first:
                    if i == 0:
                        out[eh, :, z_rows, :] = got
                    else:
                        out[eh, :, z_rows, :] += got
                else:
                    for ys in range(4):
                        value = old[eh, ys, z_rows, :] + got[ys]
                        out[eh, table[SLOT_OFFSET + ys], z_rows, :] = value.astype(out.dtype)
        ready(y_held, i, 1)
        acts = y_held[i].reshape(2 * yn, 8 * SHARE)
        for weight, out, old in zip(weights, outs, before):
            got = dot(acts, weight[...]).reshape(2, yn, COLS)
            if first:
                out[:, slot, y_rows, :] = got
            else:
                for eh in range(2):
                    for ys in range(4):
                        value = got[eh] if ys == slot else old[eh, ys, y_rows, :]
                        out[eh, table[SLOT_OFFSET + ys], y_rows, :] = value.astype(out.dtype)
        ready(x_held, i, 2)
        acts = x_held[i].reshape(4 * xn, 4 * SHARE)
        eh, el = halves[slot]
        for weight, out, old in zip(weights, outs, before):
            got = dot(acts, weight[pl.ds(el * 4 * SHARE, 4 * SHARE), :]).reshape(4, xn, COLS)
            if first:
                if slot == 0:
                    out[0, :, x_rows, :] = got
                    out[1, :, x_rows, :] = jnp.zeros_like(got)
                else:
                    out[eh, :, x_rows, :] += got
            else:
                for ys in range(4):
                    to = table[SLOT_OFFSET + ys]
                    out[0, to, x_rows, :] = old[0, ys, x_rows, :].astype(out.dtype)
                    out[1, to, x_rows, :] = (old[1, ys, x_rows, :] + got[ys]).astype(out.dtype)


def product(table, weights, blocks, slots, before, types):
    first = before is None
    vmem = pl.BlockSpec(memory_space=pltpu.VMEM)
    n, n_weights = len(slots), len(weights)
    zn, yn, xn = (PARTS[a][1] for a in "zyx")
    parts = [blocks[axis][s] for axis in "zyx" for s in slots]
    share = n * n_weights
    before = [] if first else before
    return pl.pallas_call(
        functools.partial(product_kernel, slots, n_weights, first),
        in_specs=[pl.BlockSpec(memory_space=pltpu.SMEM)]
        + [vmem] * n_weights
        + [pl.BlockSpec(memory_space=pl.ANY)] * (3 * n)
        + [vmem] * len(before),
        out_specs=[vmem] * n_weights,
        out_shape=[jax.ShapeDtypeStruct((2, 4, 256, COLS), t) for t in types],
        scratch_shapes=[
            pltpu.VMEM((n, 8, zn, 2 * SHARE), jnp.bfloat16),
            pltpu.VMEM((n, 2, yn, 8 * SHARE), jnp.bfloat16),
            pltpu.VMEM((n, 4, xn, 4 * SHARE), jnp.bfloat16),
            pltpu.SemaphoreType.DMA((n, 3)),
        ],
        compiler_params=pltpu.CompilerParams(vmem_limit_bytes=40 * MIB),
        cost_estimate=pl.CostEstimate(
            flops=share * 2 * 512 * 4096 * COLS, bytes_accessed=n * 4 * MIB + n_weights * 6 * MIB, transcendentals=0
        ),
    )(table, *weights, *parts, *before)


def spread_kernel(table, owner, parts, out):
    for k in range(8):
        section = owner[table[DEST + k]]
        half = jnp.where(section >= 4, 1, 0)
        far = jnp.where(half == table[XH], 0, 4)
        out[k] = parts[far + ((table[Y] + 8 - section) & 3)]


def arrange_kernel(table, parts, out):
    for k in range(8):
        out[:, k * COLS : (k + 1) * COLS] = parts[table[SOURCE + k]]


def small_call(kernel, scalars, parts, shape):
    smem, vmem = pl.BlockSpec(memory_space=pltpu.SMEM), pl.BlockSpec(memory_space=pltpu.VMEM)
    return pl.pallas_call(
        kernel,
        in_specs=[smem] * len(scalars) + [vmem],
        out_specs=vmem,
        out_shape=jax.ShapeDtypeStruct(shape, jnp.bfloat16),
        cost_estimate=pl.CostEstimate(flops=0, bytes_accessed=2 * MIB, transcendentals=0),
    )(*scalars, parts)


def shards(master, activations, owner):
    rows = jnp.asarray(np.array([device_row(i) for i in range(N_DEV)], np.int32))
    me = lax.axis_index("group") * 16 + lax.axis_index("tp")
    table = lax.dynamic_index_in_dim(rows, me, 0, keepdims=False)

    sent = refit(table, master, THEIRS)
    mine = refit(table, master, MINE)
    theirs = permute(sent, lambda x, y, z, c: linear(x, y, z, 1 - c))

    blocks = {}
    for axis in "zyx":
        at, count = PARTS[axis]
        blocks[axis] = gather(activations[None, at : at + count], ORDER[axis])

    f32, bf16 = jnp.float32, jnp.bfloat16
    kept, passed = product(table, [mine, theirs], blocks, (0, 1, 2), None, [f32, f32])
    (passed,) = product(table, [theirs], blocks, (3,), [passed], [bf16])
    passed = permute(passed, lambda x, y, z, c: linear(x, y, z, 1 - c))
    (kept,) = product(table, [mine], blocks, (3,), [kept], [f32])
    total = (kept + passed.astype(f32)).astype(bf16)

    parts = []
    for eh in range(2):
        for dy in range(4):
            part = total[eh, dy]
            if eh or dy:
                part = permute(part, lambda x, y, z, c: linear(x + 2 * eh, y + dy, z, c))
            parts.append(part)

    picked = small_call(spread_kernel, [table, owner], jnp.stack(parts), (8, 256, COLS))
    out = []
    for dz in range(4):
        for cross in range(2):
            move = lambda x, y, z, c: linear(x ^ (c ^ cross), y, z + dz, x % 2)
            out.append(permute(picked[dz * 2 + cross], move))
    return small_call(arrange_kernel, [table], jnp.stack(out), (256, 8 * COLS))


def solution(mesh):
    in_specs = (P(None, ("group", "tp")), P("group", "tp"), P())
    out_specs = P("group", "tp")
    return jax.shard_map(shards, mesh=mesh, in_specs=in_specs, out_specs=out_specs, check_vma=False)
```

```python
import functools

import jax
import jax.numpy as jnp
import numpy as np
from jax import lax
from jax.experimental import pallas as pl
from jax.experimental.pallas import tpu as pltpu
from jax.sharding import PartitionSpec as P

BLOCK = 128
AXES = ("group", "tp")
N_DEV = 128
SHARE = 512
COLS = 256
PARTS = {"z": (0, 96), "y": (96, 80), "x": (176, 80)}
ORDER = {"z": "xyz", "y": "zxy", "x": "yzx"}
MIB = 1024 * 1024


def coords(i):
    return i // 64 * 2 + i // 8 % 2, i // 16 % 4, i // 2 % 4, i % 2


def linear(x, y, z, core):
    x, y, z = x % 4, y % 4, z % 4
    return x // 2 * 64 + y * 16 + x % 2 * 8 + z * 2 + core


def permute(value, move):
    return lax.ppermute(value, AXES, [(i, move(*coords(i))) for i in range(N_DEV)])


def offset(slot, at, core):
    step = -1 if (at + core) % 2 else 1
    return (0, step, -step, 2)[slot] % 4


def exchange(value, axis, which):
    def move(x, y, z, core):
        at = {"x": x, "y": y, "z": z}
        at[axis] += offset(which, at[axis], core)
        return linear(at["x"], at["y"], at["z"], core)

    return permute(value, move)


def gather_plane(block, order):
    for axis in order[:2]:
        for which in (1, 2):
            block = jnp.concatenate([block, exchange(block, axis, which)], axis=0)
    return block


def gather_last(block, axis):
    first = exchange(block, axis, 1)
    second = exchange(block, axis, 2)
    relayed = exchange(first, axis, 2)
    return [v.reshape(4, 4, *v.shape[1:]) for v in (block, first, second, relayed)]


MINE, THEIRS, CORE, SLOT_OFFSET, XH, Y, Z, DEST, WIDTH = 0, 8, 16, 17, 21, 22, 23, 24, 28


def device_row(i):
    x, y, z, core = coords(i)
    xh, xl = x // 2, x % 2

    def chunks(c):
        return [(xl ^ n // 4) * 8 + (z + offset(n % 4, z, c)) % 4 * 2 + c for n in range(8)]

    dest = [(xl ^ core) * 4 + (z + dz) % 4 for dz in range(4)]
    row = chunks(core) + chunks(1 - core) + [core] + [offset(s, y, core) for s in range(4)] + [xh, y, z] + dest
    assert len(row) == WIDTH
    return row


def refit_kernel(table, master, out):
    for r in range(master.shape[0] // BLOCK):
        for c in range(master.shape[1] // BLOCK):
            at = (pl.ds(r * BLOCK, BLOCK), pl.ds(c * BLOCK, BLOCK))
            tile = master[at]
            amax = jnp.max(jnp.max(jnp.abs(tile), axis=0, keepdims=True), axis=1, keepdims=True)
            scale = ((amax + 1e-6) / 448.0).astype(jnp.bfloat16).astype(jnp.float32)
            coded = (tile * (1.0 / scale)).astype(jnp.bfloat16)
            out[at] = (coded.astype(jnp.float32) * scale).astype(jnp.bfloat16)


def refit(table, master, first):
    size = 8 * SHARE * COLS
    return pl.pallas_call(
        refit_kernel,
        grid_spec=pltpu.PrefetchScalarGridSpec(
            num_scalar_prefetch=1,
            grid=(8,),
            in_specs=[pl.BlockSpec((SHARE, COLS), lambda i, t: (t[first + i], 0))],
            out_specs=pl.BlockSpec((SHARE, COLS), lambda i, t: (i, 0)),
        ),
        out_shape=jax.ShapeDtypeStruct((8 * SHARE, COLS), jnp.bfloat16),
        cost_estimate=pl.CostEstimate(flops=size * 6, bytes_accessed=size * 6, transcendentals=0),
    )(table, master)


def rows_of(axis):
    at, count = PARTS[axis]
    return pl.ds(at, count)


def dot(a, b):
    return jnp.dot(a, b, preferred_element_type=jnp.float32)


def halves(core):
    return ((0, 0), (core, 1), (1 - core, 1), (1, 0))


def column_slices(core):
    return [pl.ds(pl.multiple_of(c * COLS, COLS), COLS) for c in (core, 1 - core)]


def early_kernel(table, mine, theirs, z0, z1, y0, y1, x0, x1, out, z_held, y_held, x_held, sems):
    core = table[CORE]
    zn, yn, xn = (PARTS[a][1] for a in "zyx")
    for i, (z_part, y_part, x_part) in enumerate(((z0, y0, x0), (z1, y1, x1))):
        for sx, (eh, el) in enumerate(halves(core)):
            cols = pl.ds(el * SHARE, SHARE)
            pltpu.make_async_copy(z_part.at[:, sx], z_held.at[i, pl.ds(eh * 4, 4), :, cols], sems.at[i, 0]).start()
            for zs in range(4):
                cols = pl.ds((el * 4 + zs) * SHARE, SHARE)
                pltpu.make_async_copy(y_part.at[sx, zs], y_held.at[i, eh, :, cols], sems.at[i, 1]).start()
        for zs in range(4):
            cols = pl.ds(zs * SHARE, SHARE)
            pltpu.make_async_copy(x_part.at[zs], x_held.at[i, :, :, cols], sems.at[i, 2]).start()

    z_rows, y_rows, x_rows = rows_of("z"), rows_of("y"), rows_of("x")
    weights = list(zip((mine, theirs), column_slices(core)))
    for i in range(2):
        for which, held in enumerate((z_held, y_held, x_held)):
            pltpu.make_async_copy(held.at[i], held.at[i], sems.at[i, which]).wait()
        for weight, cols in weights:
            for eh in range(2):
                acts = z_held[i, pl.ds(eh * 4, 4)].reshape(4 * zn, 2 * SHARE)
                got = dot(acts[:, :SHARE], weight[pl.ds(i * SHARE, SHARE), :])
                got += dot(acts[:, SHARE:], weight[pl.ds((4 + i) * SHARE, SHARE), :])
                got = got.reshape(4, zn, COLS)
                if i == 0:
                    out[eh, :, z_rows, cols] = got
                else:
                    out[eh, :, z_rows, cols] += got
            acts = y_held[i].reshape(2 * yn, 8 * SHARE)
            out[:, i, y_rows, cols] = dot(acts, weight[...]).reshape(2, yn, COLS)
            eh, el = halves(core)[i]
            acts = x_held[i].reshape(4 * xn, 4 * SHARE)
            got = dot(acts, weight[pl.ds(el * 4 * SHARE, 4 * SHARE), :]).reshape(4, xn, COLS)
            if i == 0:
                out[0, :, x_rows, cols] = got
                out[1, :, x_rows, cols] = jnp.zeros_like(got)
            else:
                out[eh, :, x_rows, cols] += got


def late_kernel(keep, table, mine, theirs, z2, z3, y2, y3, x2, x3, early, out, z_held, y_held, x_held, total, sems):
    core = table[CORE]
    half = core if keep else 1 - core
    near = jnp.where(half == 0, 0, 3)
    sources = ((near, 0), (1 if keep else 2, 1))
    zn, yn, xn = (PARTS[a][1] for a in "zyx")
    pltpu.make_async_copy(early.at[half], total, sems.at[3]).start()
    for i, (z_part, y_part, x_part) in enumerate(((z2, y2, x2), (z3, y3, x3))):
        for sx, el in sources:
            cols = pl.ds(el * SHARE, SHARE)
            pltpu.make_async_copy(z_part.at[:, sx], z_held.at[i, :, :, cols], sems.at[0]).start()
            for zs in range(4):
                cols = pl.ds((el * 4 + zs) * SHARE, SHARE)
                pltpu.make_async_copy(y_part.at[sx, zs], y_held.at[i, :, cols], sems.at[1]).start()
        for zs in range(4):
            cols = pl.ds(zs * SHARE, SHARE)
            pltpu.make_async_copy(x_part.at[zs], x_held.at[i, :, :, cols], sems.at[2]).start()
    for which, held in enumerate((z_held, y_held, x_held, total)):
        pltpu.make_async_copy(held, held, sems.at[which]).wait()

    z_rows, y_rows, x_rows = rows_of("z"), rows_of("y"), rows_of("x")
    for weight, cols in zip((mine, theirs), column_slices(core)):
        got = None
        for i in range(2):
            acts = z_held[i].reshape(4 * zn, 2 * SHARE)
            term = dot(acts[:, :SHARE], weight[pl.ds((2 + i) * SHARE, SHARE), :])
            term += dot(acts[:, SHARE:], weight[pl.ds((6 + i) * SHARE, SHARE), :])
            got = term if got is None else got + term
        total[:, z_rows, cols] += got.reshape(4, zn, COLS)
        acts = y_held[...].reshape(2 * yn, 8 * SHARE)
        total[2:4, y_rows, cols] = dot(acts, weight[...]).reshape(2, yn, COLS)

        def add(i, el):
            acts = x_held[i].reshape(4 * xn, 4 * SHARE)
            total[:, x_rows, cols] += dot(acts, weight[pl.ds(el * 4 * SHARE, 4 * SHARE), :]).reshape(4, xn, COLS)

        if not keep:
            add(0, 1)

        @pl.when(half == 1)
        def _():
            add(1, 0)

    for ys in range(4):
        out[table[SLOT_OFFSET + ys]] = total[ys].astype(out.dtype)


def product(kernel, table, weights, blocks, slots, held, out, more=()):
    vmem, anywhere = pl.BlockSpec(memory_space=pltpu.VMEM), pl.BlockSpec(memory_space=pl.ANY)
    parts = [blocks[axis][s] for axis in "zyx" for s in slots] + list(more)
    work = 2 * out.shape[0] * (2 if out.ndim == 4 else 1)
    return pl.pallas_call(
        kernel,
        in_specs=[pl.BlockSpec(memory_space=pltpu.SMEM)] + [vmem] * 2 + [anywhere] * len(parts),
        out_specs=vmem,
        out_shape=out,
        scratch_shapes=held,
        compiler_params=pltpu.CompilerParams(vmem_limit_bytes=32 * MIB),
        cost_estimate=pl.CostEstimate(
            flops=work * 512 * 4096 * 256, bytes_accessed=(6 + work) * MIB, transcendentals=0
        ),
    )(table, *weights, *parts)


def spread_kernel(table, owner, own, other, out):
    for k in range(4):
        section = owner[table[DEST + k]]
        half = jnp.where(section >= 4, 1, 0)
        far = jnp.where(half == table[XH], 0, 1)
        at = (table[Y] + 8 - section) & 3

        @pl.when(far == table[CORE])
        def _():
            out[k] = own[at]

        @pl.when(far != table[CORE])
        def _():
            out[k] = other[at]


def arrange_kernel(table, parts, out):
    for k in range(4):
        out[:, k * 2 * COLS : (k + 1) * 2 * COLS] = parts[(table[Z] + 4 - k) & 3]


def small_call(kernel, scalars, parts, shape):
    smem, vmem = pl.BlockSpec(memory_space=pltpu.SMEM), pl.BlockSpec(memory_space=pltpu.VMEM)
    return pl.pallas_call(
        kernel,
        in_specs=[smem] * len(scalars) + [vmem] * len(parts),
        out_specs=vmem,
        out_shape=jax.ShapeDtypeStruct(shape, jnp.bfloat16),
        cost_estimate=pl.CostEstimate(flops=0, bytes_accessed=2 * MIB, transcendentals=0),
    )(*scalars, *parts)


def other_core(x, y, z, core):
    return linear(x, y, z, 1 - core)


def shards(master, activations, owner):
    f32, bf16 = jnp.float32, jnp.bfloat16
    rows = jnp.asarray(np.array([device_row(i) for i in range(N_DEV)], np.int32))
    me = lax.axis_index("group") * 16 + lax.axis_index("tp")
    table = lax.dynamic_index_in_dim(rows, me, 0, keepdims=False)

    planes = {}
    for axis in "zyx":
        at, count = PARTS[axis]
        planes[axis] = gather_plane(activations[None, at : at + count], ORDER[axis])
    late_table, *held = lax.optimization_barrier((table, *planes.values()))
    blocks = {axis: gather_last(v, axis) for axis, v in zip("zyx", held)}

    theirs = permute(refit(late_table, master, THEIRS), other_core)
    mine = refit(late_table, master, MINE)
    weights = [mine, theirs]

    zn, yn, xn = (PARTS[a][1] for a in "zyx")
    early = product(
        early_kernel,
        table,
        weights,
        blocks,
        (0, 1),
        [
            pltpu.VMEM((2, 8, zn, 2 * SHARE), bf16),
            pltpu.VMEM((2, 2, yn, 8 * SHARE), bf16),
            pltpu.VMEM((2, 4, xn, 4 * SHARE), bf16),
            pltpu.SemaphoreType.DMA((2, 3)),
        ],
        jax.ShapeDtypeStruct((2, 4, 256, 2 * COLS), f32),
    )
    late = [
        pltpu.VMEM((2, 4, zn, 2 * SHARE), bf16),
        pltpu.VMEM((2, yn, 8 * SHARE), bf16),
        pltpu.VMEM((2, 4, xn, 4 * SHARE), bf16),
        pltpu.VMEM((4, 256, 2 * COLS), f32),
        pltpu.SemaphoreType.DMA((4,)),
    ]
    passed, kept = (
        product(
            functools.partial(late_kernel, keep),
            table,
            weights,
            blocks,
            (2, 3),
            late,
            jax.ShapeDtypeStruct((4, 256, 2 * COLS), f32 if keep else bf16),
            (early,),
        )
        for keep in (False, True)
    )
    total = (kept + permute(passed, other_core).astype(f32)).astype(bf16)

    got = {}
    for dy in (2, 1, 3, 0):
        got[dy] = permute(total[dy], lambda x, y, z, c: linear(x + 2 * c, y + dy, z, c))
    own = jnp.stack([got[dy] for dy in range(4)])
    other = permute(own, other_core)

    picked = small_call(spread_kernel, [table, owner], [own, other], (4, 256, 2 * COLS))
    got = {}
    for dz in (2, 1, 3, 0):
        got[dz] = permute(picked[dz], lambda x, y, z, c: linear(x ^ c, y, z + dz, x % 2))
    return small_call(arrange_kernel, [table], [jnp.stack([got[dz] for dz in range(4)])], (256, 8 * COLS))


def solution(mesh):
    in_specs = (P(None, ("group", "tp")), P("group", "tp"), P())
    out_specs = P("group", "tp")
    return jax.shard_map(shards, mesh=mesh, in_specs=in_specs, out_specs=out_specs, check_vma=False)
```

```python
import functools

import jax
import jax.numpy as jnp
import numpy as np
from jax import lax
from jax.experimental import pallas as pl
from jax.experimental.pallas import tpu as pltpu
from jax.sharding import PartitionSpec as P

BLOCK = 128
AXES = ("group", "tp")
N_DEV = 128
SHARE = 512
COLS = 256
PARTS = {"z": (0, 96), "y": (96, 80), "x": (176, 80)}
ORDER = {"z": "xyz", "y": "zxy", "x": "yzx"}
MIB = 1024 * 1024


def coords(i):
    return i // 64 * 2 + i // 8 % 2, i // 16 % 4, i // 2 % 4, i % 2


def linear(x, y, z, core):
    x, y, z = x % 4, y % 4, z % 4
    return x // 2 * 64 + y * 16 + x % 2 * 8 + z * 2 + core


def permute(value, move):
    return lax.ppermute(value, AXES, [(i, move(*coords(i))) for i in range(N_DEV)])


def offset(slot, at, core):
    step = -1 if (at + core) % 2 else 1
    return (0, step, -step, 2)[slot] % 4


def exchange(value, axis, which):
    def move(x, y, z, core):
        at = {"x": x, "y": y, "z": z}
        at[axis] += offset(which, at[axis], core)
        return linear(at["x"], at["y"], at["z"], core)

    return permute(value, move)


def gather_planes(blocks):
    for level in range(2):
        for which in (1, 2):
            blocks = {
                part: jnp.concatenate([block, exchange(block, ORDER[part][level], which)], axis=0)
                for part, block in blocks.items()
            }
            blocks = lax.optimization_barrier(blocks)
    return blocks


def gather_last(block, axis):
    first = exchange(block, axis, 1)
    second = exchange(block, axis, 2)
    relayed = exchange(first, axis, 2)
    return [v.reshape(4, 4, *v.shape[1:]) for v in (block, first, second, relayed)]


MINE, THEIRS, CORE, SLOT_OFFSET, XH, Y, Z, DEST, WIDTH = 0, 8, 16, 17, 21, 22, 23, 24, 28


def device_row(i):
    x, y, z, core = coords(i)
    xh, xl = x // 2, x % 2

    def chunks(c):
        return [(xl ^ n // 4) * 8 + (z + offset(n % 4, z, c)) % 4 * 2 + c for n in range(8)]

    dest = [(xl ^ core) * 4 + (z + dz) % 4 for dz in range(4)]
    row = chunks(core) + chunks(1 - core) + [core] + [offset(s, y, core) for s in range(4)] + [xh, y, z] + dest
    assert len(row) == WIDTH
    return row


def refit_kernel(table, master, out):
    tiles = master.shape[0] // BLOCK
    amax = jnp.max(jnp.abs(master[...]).reshape(tiles, BLOCK, COLS), axis=1)
    for c in range(COLS // BLOCK):
        cols = slice(c * BLOCK, (c + 1) * BLOCK)
        top = jnp.max(amax[:, cols], axis=1, keepdims=True)
        scales = ((top + 1e-6) / 448.0).astype(jnp.bfloat16).astype(jnp.float32)
        inverses = 1.0 / scales
        for r in range(tiles):
            at = (slice(r * BLOCK, (r + 1) * BLOCK), cols)
            coded = (master[at] * inverses[r : r + 1]).astype(jnp.bfloat16)
            out[at] = (coded.astype(jnp.float32) * scales[r : r + 1]).astype(jnp.bfloat16)


def refit(table, master, first):
    size = 8 * SHARE * COLS
    return pl.pallas_call(
        refit_kernel,
        grid_spec=pltpu.PrefetchScalarGridSpec(
            num_scalar_prefetch=1,
            grid=(8,),
            in_specs=[pl.BlockSpec((SHARE, COLS), lambda i, t: (t[first + i], 0))],
            out_specs=pl.BlockSpec((SHARE, COLS), lambda i, t: (i, 0)),
        ),
        out_shape=jax.ShapeDtypeStruct((8 * SHARE, COLS), jnp.bfloat16),
        compiler_params=pltpu.CompilerParams(vmem_limit_bytes=60 * MIB),
        cost_estimate=pl.CostEstimate(flops=size * 6, bytes_accessed=size * 6, transcendentals=0),
    )(table, master)


def rows_of(axis):
    at, count = PARTS[axis]
    return pl.ds(at, count)


def dot(a, b):
    return jnp.dot(a, b, preferred_element_type=jnp.float32)


def halves(core):
    return ((0, 0), (core, 1), (1 - core, 1), (1, 0))


def column_slices(core):
    return [pl.ds(pl.multiple_of(c * COLS, COLS), COLS) for c in (core, 1 - core)]


def early_kernel(table, mine, theirs, z0, z1, y0, y1, x0, x1, out, z_held, y_held, x_held, sems):
    core = table[CORE]
    zn, yn, xn = (PARTS[a][1] for a in "zyx")
    for i, (z_part, y_part, x_part) in enumerate(((z0, y0, x0), (z1, y1, x1))):
        for sx, (eh, el) in enumerate(halves(core)):
            cols = pl.ds(el * SHARE, SHARE)
            pltpu.make_async_copy(z_part.at[:, sx], z_held.at[i, pl.ds(eh * 4, 4), :, cols], sems.at[i, 0]).start()
            for zs in range(4):
                cols = pl.ds((el * 4 + zs) * SHARE, SHARE)
                pltpu.make_async_copy(y_part.at[sx, zs], y_held.at[i, eh, :, cols], sems.at[i, 1]).start()
        for zs in range(4):
            cols = pl.ds(zs * SHARE, SHARE)
            pltpu.make_async_copy(x_part.at[zs], x_held.at[i, :, :, cols], sems.at[i, 2]).start()

    z_rows, y_rows, x_rows = rows_of("z"), rows_of("y"), rows_of("x")
    weights = list(zip((mine, theirs), column_slices(core)))
    for i in range(2):
        for which, held in enumerate((z_held, y_held, x_held)):
            pltpu.make_async_copy(held.at[i], held.at[i], sems.at[i, which]).wait()
        for weight, cols in weights:
            for eh in range(2):
                acts = z_held[i, pl.ds(eh * 4, 4)].reshape(4 * zn, 2 * SHARE)
                got = dot(acts[:, :SHARE], weight[pl.ds(i * SHARE, SHARE), :])
                got += dot(acts[:, SHARE:], weight[pl.ds((4 + i) * SHARE, SHARE), :])
                got = got.reshape(4, zn, COLS)
                if i == 0:
                    out[eh, :, z_rows, cols] = got
                else:
                    out[eh, :, z_rows, cols] += got
            acts = y_held[i].reshape(2 * yn, 8 * SHARE)
            out[:, i, y_rows, cols] = dot(acts, weight[...]).reshape(2, yn, COLS)
            eh, el = halves(core)[i]
            acts = x_held[i].reshape(4 * xn, 4 * SHARE)
            got = dot(acts, weight[pl.ds(el * 4 * SHARE, 4 * SHARE), :]).reshape(4, xn, COLS)
            if i == 0:
                out[0, :, x_rows, cols] = got
                out[1, :, x_rows, cols] = jnp.zeros_like(got)
            else:
                out[eh, :, x_rows, cols] += got


def late_kernel(keep, table, mine, theirs, z2, z3, y2, y3, x2, x3, early, out, z_held, y_held, x_held, total, sems):
    core = table[CORE]
    half = core if keep else 1 - core
    near = jnp.where(half == 0, 0, 3)
    sources = ((near, 0), (1 if keep else 2, 1))
    zn, yn, xn = (PARTS[a][1] for a in "zyx")

    def start(src, dst, which):
        pltpu.make_async_copy(src, dst, sems.at[which]).start()

    def ready(held, which):
        pltpu.make_async_copy(held, held, sems.at[which]).wait()

    for i, part in enumerate((z2, z3)):
        for sx, el in sources:
            start(part.at[:, sx], z_held.at[i, :, :, pl.ds(el * SHARE, SHARE)], 0)
    start(early.at[half], total, 1)
    for i, part in enumerate((y2, y3)):
        for sx, el in sources:
            for zs in range(4):
                start(part.at[sx, zs], y_held.at[i, :, pl.ds((el * 4 + zs) * SHARE, SHARE)], 2)
    for i, part in enumerate((x2, x3)):
        for zs in range(4):
            start(part.at[zs], x_held.at[i, :, :, pl.ds(zs * SHARE, SHARE)], 3)

    z_rows, y_rows, x_rows = rows_of("z"), rows_of("y"), rows_of("x")
    weights = list(zip((mine, theirs), column_slices(core)))
    ready(z_held, 0)
    ready(total, 1)
    for weight, cols in weights:
        got = None
        for i in range(2):
            acts = z_held[i].reshape(4 * zn, 2 * SHARE)
            term = dot(acts[:, :SHARE], weight[pl.ds((2 + i) * SHARE, SHARE), :])
            term += dot(acts[:, SHARE:], weight[pl.ds((6 + i) * SHARE, SHARE), :])
            got = term if got is None else got + term
        total[:, z_rows, cols] += got.reshape(4, zn, COLS)
    ready(y_held, 2)
    for weight, cols in weights:
        acts = y_held[...].reshape(2 * yn, 8 * SHARE)
        total[2:4, y_rows, cols] = dot(acts, weight[...]).reshape(2, yn, COLS)
    ready(x_held, 3)
    for weight, cols in weights:

        def add(i, el):
            acts = x_held[i].reshape(4 * xn, 4 * SHARE)
            total[:, x_rows, cols] += dot(acts, weight[pl.ds(el * 4 * SHARE, 4 * SHARE), :]).reshape(4, xn, COLS)

        if not keep:
            add(0, 1)

        @pl.when(half == 1)
        def _():
            add(1, 0)

    for ys in range(4):
        out[table[SLOT_OFFSET + ys]] = total[ys].astype(out.dtype)


def product(kernel, table, weights, blocks, slots, held, out, more=()):
    vmem, anywhere = pl.BlockSpec(memory_space=pltpu.VMEM), pl.BlockSpec(memory_space=pl.ANY)
    parts = [blocks[axis][s] for axis in "zyx" for s in slots] + list(more)
    work = 2 * out.shape[0] * (2 if out.ndim == 4 else 1)
    return pl.pallas_call(
        kernel,
        in_specs=[pl.BlockSpec(memory_space=pltpu.SMEM)] + [vmem] * 2 + [anywhere] * len(parts),
        out_specs=vmem,
        out_shape=out,
        scratch_shapes=held,
        compiler_params=pltpu.CompilerParams(vmem_limit_bytes=32 * MIB),
        cost_estimate=pl.CostEstimate(
            flops=work * 512 * 4096 * 256, bytes_accessed=(6 + work) * MIB, transcendentals=0
        ),
    )(table, *weights, *parts)


def spread_kernel(table, owner, own, other, *refs):
    outs, sems = refs[:4], refs[4]
    for k, out in enumerate(outs):
        section = owner[table[DEST + k]]
        half = jnp.where(section >= 4, 1, 0)
        far = jnp.where(half == table[XH], 0, 1)
        at = (table[Y] + 8 - section) & 3

        @pl.when(far == table[CORE])
        def _():
            pltpu.make_async_copy(own.at[at], out, sems.at[k]).start()

        @pl.when(far != table[CORE])
        def _():
            pltpu.make_async_copy(other.at[at], out, sems.at[k]).start()

    for k, out in enumerate(outs):
        pltpu.make_async_copy(out, out, sems.at[k]).wait()


def arrange_kernel(table, *refs):
    parts, out, sems = refs[:4], refs[4], refs[5]
    copies = []
    for dz, part in enumerate(parts):
        at = pl.multiple_of(((table[Z] + 4 - dz) & 3) * (2 * COLS), 2 * COLS)
        copies.append(pltpu.make_async_copy(part, out.at[:, pl.ds(at, 2 * COLS)], sems.at[dz]))
        copies[-1].start()
    for copy in copies:
        copy.wait()


def small_call(kernel, scalars, parts, shapes):
    smem, anywhere = pl.BlockSpec(memory_space=pltpu.SMEM), pl.BlockSpec(memory_space=pl.ANY)
    return pl.pallas_call(
        kernel,
        in_specs=[smem] * len(scalars) + [anywhere] * len(parts),
        out_specs=[anywhere] * len(shapes),
        out_shape=[jax.ShapeDtypeStruct(shape, jnp.bfloat16) for shape in shapes],
        scratch_shapes=[pltpu.SemaphoreType.DMA((4,))],
        cost_estimate=pl.CostEstimate(flops=0, bytes_accessed=2 * MIB, transcendentals=0),
    )(*scalars, *parts)


def other_core(x, y, z, core):
    return linear(x, y, z, 1 - core)


def shards(master, activations, owner):
    f32, bf16 = jnp.float32, jnp.bfloat16
    rows = jnp.asarray(np.array([device_row(i) for i in range(N_DEV)], np.int32))
    me = lax.axis_index("group") * 16 + lax.axis_index("tp")
    table = lax.dynamic_index_in_dim(rows, me, 0, keepdims=False)

    planes = gather_planes({part: activations[None, at : at + n] for part, (at, n) in PARTS.items()})
    blocks = {axis: gather_last(planes[axis], axis) for axis in "zyx"}

    theirs = permute(refit(table, master, THEIRS), other_core)
    mine = refit(table, master, MINE)
    weights = [mine, theirs]

    zn, yn, xn = (PARTS[a][1] for a in "zyx")
    early = product(
        early_kernel,
        table,
        weights,
        blocks,
        (0, 1),
        [
            pltpu.VMEM((2, 8, zn, 2 * SHARE), bf16),
            pltpu.VMEM((2, 2, yn, 8 * SHARE), bf16),
            pltpu.VMEM((2, 4, xn, 4 * SHARE), bf16),
            pltpu.SemaphoreType.DMA((2, 3)),
        ],
        jax.ShapeDtypeStruct((2, 4, 256, 2 * COLS), f32),
    )
    late = [
        pltpu.VMEM((2, 4, zn, 2 * SHARE), bf16),
        pltpu.VMEM((2, yn, 8 * SHARE), bf16),
        pltpu.VMEM((2, 4, xn, 4 * SHARE), bf16),
        pltpu.VMEM((4, 256, 2 * COLS), f32),
        pltpu.SemaphoreType.DMA((4,)),
    ]
    passed, kept = (
        product(
            functools.partial(late_kernel, keep),
            table,
            weights,
            blocks,
            (2, 3),
            late,
            jax.ShapeDtypeStruct((4, 256, 2 * COLS), f32 if keep else bf16),
            (early,),
        )
        for keep in (False, True)
    )
    total = (kept + permute(passed, other_core).astype(f32)).astype(bf16)

    got = {}
    for dy in (2, 1, 3, 0):
        got[dy] = permute(total[dy], lambda x, y, z, c: linear(x + 2 * c, y + dy, z, c))
    own = jnp.stack([got[dy] for dy in range(4)])
    other = permute(own, other_core)

    picked = small_call(spread_kernel, [table, owner], [own, other], [(256, 2 * COLS)] * 4)
    got = {}
    for dz in (2, 1, 3, 0):
        got[dz] = permute(picked[dz], lambda x, y, z, c: linear(x ^ c, y, z + dz, x % 2))
    return small_call(arrange_kernel, [table], [got[dz] for dz in range(4)], [(256, 8 * COLS)])[0]


def solution(mesh):
    in_specs = (P(None, ("group", "tp")), P("group", "tp"), P())
    out_specs = P("group", "tp")
    return jax.shard_map(shards, mesh=mesh, in_specs=in_specs, out_specs=out_specs, check_vma=False)
```

```python
import functools

import jax
import jax.numpy as jnp
import numpy as np
from jax import lax
from jax.experimental import pallas as pl
from jax.experimental.pallas import tpu as pltpu
from jax.sharding import PartitionSpec as P

BLOCK = 128
AXES = ("group", "tp")
N_DEV = 128
SHARE = 512
COLS = 256
PARTS = {"z": (0, 96), "y": (96, 80), "x": (176, 80)}
ORDER = {"z": "xyz", "y": "zxy", "x": "yzx"}
MIB = 1024 * 1024


def coords(i):
    return i // 64 * 2 + i // 8 % 2, i // 16 % 4, i // 2 % 4, i % 2


def linear(x, y, z, core):
    x, y, z = x % 4, y % 4, z % 4
    return x // 2 * 64 + y * 16 + x % 2 * 8 + z * 2 + core


def permute(value, move):
    return lax.ppermute(value, AXES, [(i, move(*coords(i))) for i in range(N_DEV)])


def offset(slot, at, core):
    step = -1 if (at + core) % 2 else 1
    return (0, step, -step, 2)[slot] % 4


def exchange(value, axis, which):
    def move(x, y, z, core):
        at = {"x": x, "y": y, "z": z}
        at[axis] += offset(which, at[axis], core)
        return linear(at["x"], at["y"], at["z"], core)

    return permute(value, move)


def gather_planes(blocks):
    for level in range(2):
        for which in (1, 2):
            blocks = {
                part: jnp.concatenate([block, exchange(block, ORDER[part][level], which)], axis=0)
                for part, block in blocks.items()
            }
            blocks = lax.optimization_barrier(blocks)
    return blocks


def gather_last(block, axis):
    first = exchange(block, axis, 1)
    if axis == "z":
        first, block = lax.optimization_barrier((first, block))
    second = exchange(block, axis, 2)
    relayed = exchange(first, axis, 2)
    return [v.reshape(4, 4, *v.shape[1:]) for v in (block, first, second, relayed)]


MINE, THEIRS, CORE, SLOT_OFFSET, XH, Y, Z, DEST, WIDTH = 0, 8, 16, 17, 21, 22, 23, 24, 28


def device_row(i):
    x, y, z, core = coords(i)
    xh, xl = x // 2, x % 2

    def chunks(c):
        return [(xl ^ n // 4) * 8 + (z + offset(n % 4, z, c)) % 4 * 2 + c for n in range(8)]

    dest = [(xl ^ core) * 4 + (z + dz) % 4 for dz in range(4)]
    row = chunks(core) + chunks(1 - core) + [core] + [offset(s, y, core) for s in range(4)] + [xh, y, z] + dest
    assert len(row) == WIDTH
    return row


def refit_kernel(first, table, master, out, held, sems):
    copies = []
    for n in range(8):
        at = pl.multiple_of(table[first + n] * SHARE, SHARE)
        copies.append(pltpu.make_async_copy(master.at[pl.ds(at, SHARE)], held.at[n], sems.at[n]))
        copies[-1].start()
    tiles = SHARE // BLOCK
    for n in range(8):
        copies[n].wait()
        amax = jnp.max(jnp.abs(held[n]).reshape(tiles, BLOCK, COLS), axis=1)
        for c in range(COLS // BLOCK):
            cols = slice(c * BLOCK, (c + 1) * BLOCK)
            top = jnp.max(amax[:, cols], axis=1, keepdims=True)
            scales = ((top + 1e-6) / 448.0).astype(jnp.bfloat16).astype(jnp.float32)
            inverses = 1.0 / scales
            for r in range(tiles):
                tile = held[n, r * BLOCK : (r + 1) * BLOCK, cols]
                coded = (tile * inverses[r : r + 1]).astype(jnp.bfloat16)
                value = (coded.astype(jnp.float32) * scales[r : r + 1]).astype(jnp.bfloat16)
                out[n * SHARE + r * BLOCK : n * SHARE + (r + 1) * BLOCK, cols] = value


def refit(table, master, first):
    size = 8 * SHARE * COLS
    return pl.pallas_call(
        functools.partial(refit_kernel, first),
        in_specs=[pl.BlockSpec(memory_space=pltpu.SMEM), pl.BlockSpec(memory_space=pltpu.HBM)],
        out_specs=pl.BlockSpec(memory_space=pltpu.VMEM),
        out_shape=jax.ShapeDtypeStruct((8 * SHARE, COLS), jnp.bfloat16),
        scratch_shapes=[pltpu.VMEM((8, SHARE, COLS), jnp.float32), pltpu.SemaphoreType.DMA((8,))],
        compiler_params=pltpu.CompilerParams(vmem_limit_bytes=48 * MIB),
        cost_estimate=pl.CostEstimate(flops=size * 6, bytes_accessed=size * 6, transcendentals=0),
    )(table, master)


def rows_of(axis):
    at, count = PARTS[axis]
    return pl.ds(at, count)


def dot(a, b):
    return jnp.dot(a, b, preferred_element_type=jnp.float32)


def halves(core):
    return ((0, 0), (core, 1), (1 - core, 1), (1, 0))


def column_slices(core):
    return [pl.ds(pl.multiple_of(c * COLS, COLS), COLS) for c in (core, 1 - core)]


def early_kernel(table, mine, theirs, z0, z1, y0, y1, x0, x1, out, z_held, y_held, x_held, sems):
    core = table[CORE]
    zn, yn, xn = (PARTS[a][1] for a in "zyx")
    for i, (z_part, y_part, x_part) in enumerate(((z0, y0, x0), (z1, y1, x1))):
        for sx, (eh, el) in enumerate(halves(core)):
            cols = pl.ds(el * SHARE, SHARE)
            pltpu.make_async_copy(z_part.at[:, sx], z_held.at[i, pl.ds(eh * 4, 4), :, cols], sems.at[i, 0]).start()
            for zs in range(4):
                cols = pl.ds((el * 4 + zs) * SHARE, SHARE)
                pltpu.make_async_copy(y_part.at[sx, zs], y_held.at[i, eh, :, cols], sems.at[i, 1]).start()
        for zs in range(4):
            cols = pl.ds(zs * SHARE, SHARE)
            pltpu.make_async_copy(x_part.at[zs], x_held.at[i, :, :, cols], sems.at[i, 2]).start()

    z_rows, y_rows, x_rows = rows_of("z"), rows_of("y"), rows_of("x")
    weights = list(zip((mine, theirs), column_slices(core)))
    for i in range(2):
        for which, held in enumerate((z_held, y_held, x_held)):
            pltpu.make_async_copy(held.at[i], held.at[i], sems.at[i, which]).wait()
        for weight, cols in weights:
            for eh in range(2):
                acts = z_held[i, pl.ds(eh * 4, 4)].reshape(4 * zn, 2 * SHARE)
                got = dot(acts[:, :SHARE], weight[pl.ds(i * SHARE, SHARE), :])
                got += dot(acts[:, SHARE:], weight[pl.ds((4 + i) * SHARE, SHARE), :])
                got = got.reshape(4, zn, COLS)
                if i == 0:
                    out[eh, :, z_rows, cols] = got
                else:
                    out[eh, :, z_rows, cols] += got
            acts = y_held[i].reshape(2 * yn, 8 * SHARE)
            out[:, i, y_rows, cols] = dot(acts, weight[...]).reshape(2, yn, COLS)
            eh, el = halves(core)[i]
            acts = x_held[i].reshape(4 * xn, 4 * SHARE)
            got = dot(acts, weight[pl.ds(el * 4 * SHARE, 4 * SHARE), :]).reshape(4, xn, COLS)
            if i == 0:
                out[0, :, x_rows, cols] = got
                out[1, :, x_rows, cols] = jnp.zeros_like(got)
            else:
                out[eh, :, x_rows, cols] += got


def late_kernel(keep, table, mine, theirs, z2, z3, y2, y3, x2, x3, early, out, z_held, y_held, x_held, total, sems):
    core = table[CORE]
    half = core if keep else 1 - core
    near = jnp.where(half == 0, 0, 3)
    sources = ((near, 0), (1 if keep else 2, 1))
    zn, yn, xn = (PARTS[a][1] for a in "zyx")

    def start(src, dst, which):
        pltpu.make_async_copy(src, dst, sems.at[which]).start()

    def ready(held, which):
        pltpu.make_async_copy(held, held, sems.at[which]).wait()

    for i, part in enumerate((z2, z3)):
        for sx, el in sources:
            start(part.at[:, sx], z_held.at[i, :, :, pl.ds(el * SHARE, SHARE)], 0)
    start(early.at[half], total, 1)
    for i, part in enumerate((y2, y3)):
        for sx, el in sources:
            for zs in range(4):
                start(part.at[sx, zs], y_held.at[i, :, pl.ds((el * 4 + zs) * SHARE, SHARE)], 2)
    for i, part in enumerate((x2, x3)):
        for zs in range(4):
            start(part.at[zs], x_held.at[i, :, :, pl.ds(zs * SHARE, SHARE)], 3)

    z_rows, y_rows, x_rows = rows_of("z"), rows_of("y"), rows_of("x")
    weights = list(zip((mine, theirs), column_slices(core)))
    ready(z_held, 0)
    ready(total, 1)
    for weight, cols in weights:
        got = None
        for i in range(2):
            acts = z_held[i].reshape(4 * zn, 2 * SHARE)
            term = dot(acts[:, :SHARE], weight[pl.ds((2 + i) * SHARE, SHARE), :])
            term += dot(acts[:, SHARE:], weight[pl.ds((6 + i) * SHARE, SHARE), :])
            got = term if got is None else got + term
        total[:, z_rows, cols] += got.reshape(4, zn, COLS)
    ready(y_held, 2)
    for weight, cols in weights:
        acts = y_held[...].reshape(2 * yn, 8 * SHARE)
        total[2:4, y_rows, cols] = dot(acts, weight[...]).reshape(2, yn, COLS)
    ready(x_held, 3)
    for weight, cols in weights:

        def add(i, el):
            acts = x_held[i].reshape(4 * xn, 4 * SHARE)
            total[:, x_rows, cols] += dot(acts, weight[pl.ds(el * 4 * SHARE, 4 * SHARE), :]).reshape(4, xn, COLS)

        if not keep:
            add(0, 1)

        @pl.when(half == 1)
        def _():
            add(1, 0)

    for ys in range(4):
        out[table[SLOT_OFFSET + ys]] = total[ys].astype(out.dtype)


def product(kernel, table, weights, blocks, slots, held, out, more=()):
    vmem, anywhere = pl.BlockSpec(memory_space=pltpu.VMEM), pl.BlockSpec(memory_space=pl.ANY)
    parts = [blocks[axis][s] for axis in "zyx" for s in slots] + list(more)
    work = 2 * out.shape[0] * (2 if out.ndim == 4 else 1)
    return pl.pallas_call(
        kernel,
        in_specs=[pl.BlockSpec(memory_space=pltpu.SMEM)] + [vmem] * 2 + [anywhere] * len(parts),
        out_specs=vmem,
        out_shape=out,
        scratch_shapes=held,
        compiler_params=pltpu.CompilerParams(vmem_limit_bytes=32 * MIB),
        cost_estimate=pl.CostEstimate(
            flops=work * 512 * 4096 * 256, bytes_accessed=(6 + work) * MIB, transcendentals=0
        ),
    )(table, *weights, *parts)


def spread_kernel(table, owner, own, other, *outs):
    for k, out in enumerate(outs):
        section = owner[table[DEST + k]]
        half = jnp.where(section >= 4, 1, 0)
        far = jnp.where(half == table[XH], 0, 1)
        at = (table[Y] + 8 - section) & 3

        @pl.when(far == table[CORE])
        def _():
            out[...] = own[at]

        @pl.when(far != table[CORE])
        def _():
            out[...] = other[at]


def arrange_kernel(table, *refs):
    parts, out, sems = refs[:4], refs[4], refs[5]
    copies = []
    for dz, part in enumerate(parts):
        at = pl.multiple_of(((table[Z] + 4 - dz) & 3) * (2 * COLS), 2 * COLS)
        copies.append(pltpu.make_async_copy(part, out.at[:, pl.ds(at, 2 * COLS)], sems.at[dz]))
        copies[-1].start()
    for copy in copies:
        copy.wait()


def small_call(kernel, scalars, parts, shapes, out_space, scratch=()):
    smem, vmem = pl.BlockSpec(memory_space=pltpu.SMEM), pl.BlockSpec(memory_space=pltpu.VMEM)
    return pl.pallas_call(
        kernel,
        in_specs=[smem] * len(scalars) + [vmem] * len(parts),
        out_specs=[pl.BlockSpec(memory_space=out_space)] * len(shapes),
        out_shape=[jax.ShapeDtypeStruct(shape, jnp.bfloat16) for shape in shapes],
        scratch_shapes=scratch,
        compiler_params=pltpu.CompilerParams(vmem_limit_bytes=16 * MIB),
        cost_estimate=pl.CostEstimate(flops=0, bytes_accessed=2 * MIB, transcendentals=0),
    )(*scalars, *parts)


def other_core(x, y, z, core):
    return linear(x, y, z, 1 - core)


def shards(master, activations, owner):
    f32, bf16 = jnp.float32, jnp.bfloat16
    rows = jnp.asarray(np.array([device_row(i) for i in range(N_DEV)], np.int32))
    me = lax.axis_index("group") * 16 + lax.axis_index("tp")
    table = lax.dynamic_index_in_dim(rows, me, 0, keepdims=False)

    planes = gather_planes({part: activations[None, at : at + n] for part, (at, n) in PARTS.items()})
    blocks = {axis: gather_last(planes[axis], axis) for axis in "zyx"}

    theirs = permute(refit(table, master, THEIRS), other_core)
    mine = refit(table, master, MINE)
    weights = [mine, theirs]

    zn, yn, xn = (PARTS[a][1] for a in "zyx")
    early = product(
        early_kernel,
        table,
        weights,
        blocks,
        (0, 1),
        [
            pltpu.VMEM((2, 8, zn, 2 * SHARE), bf16),
            pltpu.VMEM((2, 2, yn, 8 * SHARE), bf16),
            pltpu.VMEM((2, 4, xn, 4 * SHARE), bf16),
            pltpu.SemaphoreType.DMA((2, 3)),
        ],
        jax.ShapeDtypeStruct((2, 4, 256, 2 * COLS), f32),
    )
    late = [
        pltpu.VMEM((2, 4, zn, 2 * SHARE), bf16),
        pltpu.VMEM((2, yn, 8 * SHARE), bf16),
        pltpu.VMEM((2, 4, xn, 4 * SHARE), bf16),
        pltpu.VMEM((4, 256, 2 * COLS), f32),
        pltpu.SemaphoreType.DMA((4,)),
    ]
    passed, kept = (
        product(
            functools.partial(late_kernel, keep),
            table,
            weights,
            blocks,
            (2, 3),
            late,
            jax.ShapeDtypeStruct((4, 256, 2 * COLS), f32 if keep else bf16),
            (early,),
        )
        for keep in (False, True)
    )
    total = (kept + permute(passed, other_core).astype(f32)).astype(bf16)

    got = {}
    for dy in (2, 1, 3, 0):
        got[dy] = permute(total[dy], lambda x, y, z, c: linear(x + 2 * c, y + dy, z, c))
    own = jnp.stack([got[dy] for dy in range(4)])
    other = permute(own, other_core)

    picked = small_call(spread_kernel, [table, owner], [own, other], [(256, 2 * COLS)] * 4, pltpu.VMEM)
    got = {}
    for dz in (2, 1, 3, 0):
        got[dz] = permute(picked[dz], lambda x, y, z, c: linear(x ^ c, y, z + dz, x % 2))
    got = [got[dz] for dz in range(4)]
    return small_call(arrange_kernel, [table], got, [(256, 8 * COLS)], pltpu.HBM, [pltpu.SemaphoreType.DMA((4,))])[0]


def solution(mesh):
    in_specs = (P(None, ("group", "tp")), P("group", "tp"), P())
    out_specs = P("group", "tp")
    return jax.shard_map(shards, mesh=mesh, in_specs=in_specs, out_specs=out_specs, check_vma=False)
```

```python
import functools

import jax
import jax.numpy as jnp
import numpy as np
from jax import lax
from jax.experimental import pallas as pl
from jax.experimental.pallas import tpu as pltpu
from jax.sharding import PartitionSpec as P

BLOCK = 128
AXES = ("group", "tp")
N_DEV = 128
SHARE = 512
COLS = 256
PARTS = {"z": (0, 96), "y": (96, 80), "x": (176, 80)}
ORDER = {"z": "xyz", "y": "zxy", "x": "yzx"}
MIB = 1024 * 1024


def coords(i):
    return i // 64 * 2 + i // 8 % 2, i // 16 % 4, i // 2 % 4, i % 2


def linear(x, y, z, core):
    x, y, z = x % 4, y % 4, z % 4
    return x // 2 * 64 + y * 16 + x % 2 * 8 + z * 2 + core


def permute(value, move):
    return lax.ppermute(value, AXES, [(i, move(*coords(i))) for i in range(N_DEV)])


def offset(slot, at, core):
    step = -1 if (at + core) % 2 else 1
    return (0, step, -step, 2)[slot] % 4


def exchange(value, axis, which):
    def move(x, y, z, core):
        at = {"x": x, "y": y, "z": z}
        at[axis] += offset(which, at[axis], core)
        return linear(at["x"], at["y"], at["z"], core)

    return permute(value, move)


def join_kernel(*refs):
    pairs, outs = refs[:6], refs[6:]
    for i, out in enumerate(outs):
        left, right = pairs[2 * i], pairs[2 * i + 1]
        n = left.shape[0]
        out[:n] = left[...]
        out[n:] = right[...]


def join(pairs):
    vmem = pl.BlockSpec(memory_space=pltpu.VMEM)
    shapes = [(2 * left.shape[0], *left.shape[1:]) for left, _ in pairs]
    size = sum(left.size for left, _ in pairs)
    return pl.pallas_call(
        join_kernel,
        in_specs=[vmem] * 6,
        out_specs=[vmem] * 3,
        out_shape=[jax.ShapeDtypeStruct(shape, jnp.bfloat16) for shape in shapes],
        compiler_params=pltpu.CompilerParams(vmem_limit_bytes=16 * MIB),
        cost_estimate=pl.CostEstimate(flops=0, bytes_accessed=8 * size, transcendentals=0),
    )(*[v for pair in pairs for v in pair])


def gather_planes(blocks):
    for level in range(2):
        for which in (1, 2):
            pairs = {part: (block, exchange(block, ORDER[part][level], which)) for part, block in blocks.items()}
            if level == 0:
                blocks = lax.optimization_barrier({part: jnp.concatenate(pair) for part, pair in pairs.items()})
            else:
                blocks = dict(zip(pairs, join(list(pairs.values()))))
    return blocks


def gather_last(block, axis):
    first = exchange(block, axis, 1)
    if axis != "y":
        first, block = lax.optimization_barrier((first, block))
    second = exchange(block, axis, 2)
    relayed = exchange(first, axis, 2)
    return [v.reshape(4, 4, *v.shape[1:]) for v in (block, first, second, relayed)]


MINE, THEIRS, CORE, SLOT_OFFSET, XH, Y, Z, DEST, WIDTH = 0, 8, 16, 17, 21, 22, 23, 24, 28


def device_row(i):
    x, y, z, core = coords(i)
    xh, xl = x // 2, x % 2

    def chunks(c):
        return [(xl ^ n // 4) * 8 + (z + offset(n % 4, z, c)) % 4 * 2 + c for n in range(8)]

    dest = [(xl ^ core) * 4 + (z + dz) % 4 for dz in range(4)]
    row = chunks(core) + chunks(1 - core) + [core] + [offset(s, y, core) for s in range(4)] + [xh, y, z] + dest
    assert len(row) == WIDTH
    return row


def refit_kernel(first, table, master, out, held, sems):
    copies = []
    for n in range(8):
        at = pl.multiple_of(table[first + n] * SHARE, SHARE)
        copies.append(pltpu.make_async_copy(master.at[pl.ds(at, SHARE)], held.at[n], sems.at[n]))
        copies[-1].start()
    tiles = SHARE // BLOCK
    for n in range(8):
        copies[n].wait()
        amax = jnp.max(jnp.abs(held[n]).reshape(tiles, BLOCK, COLS), axis=1)
        for c in range(COLS // BLOCK):
            cols = slice(c * BLOCK, (c + 1) * BLOCK)
            top = jnp.max(amax[:, cols], axis=1, keepdims=True)
            scales = ((top + 1e-6) / 448.0).astype(jnp.bfloat16).astype(jnp.float32)
            inverses = 1.0 / scales
            for r in range(tiles):
                tile = held[n, r * BLOCK : (r + 1) * BLOCK, cols]
                coded = (tile * inverses[r : r + 1]).astype(jnp.bfloat16)
                value = (coded.astype(jnp.float32) * scales[r : r + 1]).astype(jnp.bfloat16)
                out[n * SHARE + r * BLOCK : n * SHARE + (r + 1) * BLOCK, cols] = value


def refit(table, master, first):
    size = 8 * SHARE * COLS
    return pl.pallas_call(
        functools.partial(refit_kernel, first),
        in_specs=[pl.BlockSpec(memory_space=pltpu.SMEM), pl.BlockSpec(memory_space=pltpu.HBM)],
        out_specs=pl.BlockSpec(memory_space=pltpu.VMEM),
        out_shape=jax.ShapeDtypeStruct((8 * SHARE, COLS), jnp.bfloat16),
        scratch_shapes=[pltpu.VMEM((8, SHARE, COLS), jnp.float32), pltpu.SemaphoreType.DMA((8,))],
        compiler_params=pltpu.CompilerParams(vmem_limit_bytes=44 * MIB),
        cost_estimate=pl.CostEstimate(flops=size * 6, bytes_accessed=size * 6, transcendentals=0),
    )(table, master)


def rows_of(axis):
    at, count = PARTS[axis]
    return pl.ds(at, count)


def dot(a, b):
    return jnp.dot(a, b, preferred_element_type=jnp.float32)


def halves(core):
    return ((0, 0), (core, 1), (1 - core, 1), (1, 0))


def column_slices(core):
    return [pl.ds(pl.multiple_of(c * COLS, COLS), COLS) for c in (core, 1 - core)]


def early_kernel(table, mine, theirs, z0, z1, y0, y1, x0, x1, out, z_held, y_held, x_held, sems):
    core = table[CORE]
    zn, yn, xn = (PARTS[a][1] for a in "zyx")
    for i, (z_part, y_part, x_part) in enumerate(((z0, y0, x0), (z1, y1, x1))):
        for sx, (eh, el) in enumerate(halves(core)):
            cols = pl.ds(el * SHARE, SHARE)
            pltpu.make_async_copy(z_part.at[:, sx], z_held.at[i, pl.ds(eh * 4, 4), :, cols], sems.at[i, 0]).start()
            for zs in range(4):
                cols = pl.ds((el * 4 + zs) * SHARE, SHARE)
                pltpu.make_async_copy(y_part.at[sx, zs], y_held.at[i, eh, :, cols], sems.at[i, 1]).start()
        for zs in range(4):
            cols = pl.ds(zs * SHARE, SHARE)
            pltpu.make_async_copy(x_part.at[zs], x_held.at[i, :, :, cols], sems.at[i, 2]).start()

    z_rows, y_rows, x_rows = rows_of("z"), rows_of("y"), rows_of("x")
    weights = list(zip((mine, theirs), column_slices(core)))
    for i in range(2):
        for which, held in enumerate((z_held, y_held, x_held)):
            pltpu.make_async_copy(held.at[i], held.at[i], sems.at[i, which]).wait()
        for weight, cols in weights:
            for eh in range(2):
                acts = z_held[i, pl.ds(eh * 4, 4)].reshape(4 * zn, 2 * SHARE)
                got = dot(acts[:, :SHARE], weight[pl.ds(i * SHARE, SHARE), :])
                got += dot(acts[:, SHARE:], weight[pl.ds((4 + i) * SHARE, SHARE), :])
                got = got.reshape(4, zn, COLS)
                if i == 0:
                    out[eh, :, z_rows, cols] = got
                else:
                    out[eh, :, z_rows, cols] += got
            acts = y_held[i].reshape(2 * yn, 8 * SHARE)
            out[:, i, y_rows, cols] = dot(acts, weight[...]).reshape(2, yn, COLS)
            eh, el = halves(core)[i]
            acts = x_held[i].reshape(4 * xn, 4 * SHARE)
            got = dot(acts, weight[pl.ds(el * 4 * SHARE, 4 * SHARE), :]).reshape(4, xn, COLS)
            if i == 0:
                out[0, :, x_rows, cols] = got
                out[1, :, x_rows, cols] = jnp.zeros_like(got)
            else:
                out[eh, :, x_rows, cols] += got


def late_kernel(keep, table, mine, theirs, z2, z3, y2, y3, x2, x3, early, out, z_held, y_held, x_held, total, sems):
    core = table[CORE]
    half = core if keep else 1 - core
    near = jnp.where(half == 0, 0, 3)
    sources = ((near, 0), (1 if keep else 2, 1))
    zn, yn, xn = (PARTS[a][1] for a in "zyx")

    def start(src, dst, which):
        pltpu.make_async_copy(src, dst, sems.at[which]).start()

    def ready(held, which):
        pltpu.make_async_copy(held, held, sems.at[which]).wait()

    for i, part in enumerate((z2, z3)):
        for sx, el in sources:
            start(part.at[:, sx], z_held.at[i, :, :, pl.ds(el * SHARE, SHARE)], 0)
    start(early.at[half], total, 1)
    for i, part in enumerate((y2, y3)):
        for sx, el in sources:
            for zs in range(4):
                start(part.at[sx, zs], y_held.at[i, :, pl.ds((el * 4 + zs) * SHARE, SHARE)], 2)
    for i, part in enumerate((x2, x3)):
        for zs in range(4):
            start(part.at[zs], x_held.at[i, :, :, pl.ds(zs * SHARE, SHARE)], 3)

    z_rows, y_rows, x_rows = rows_of("z"), rows_of("y"), rows_of("x")
    weights = list(zip((mine, theirs), column_slices(core)))
    ready(z_held, 0)
    ready(total, 1)
    for weight, cols in weights:
        got = None
        for i in range(2):
            acts = z_held[i].reshape(4 * zn, 2 * SHARE)
            term = dot(acts[:, :SHARE], weight[pl.ds((2 + i) * SHARE, SHARE), :])
            term += dot(acts[:, SHARE:], weight[pl.ds((6 + i) * SHARE, SHARE), :])
            got = term if got is None else got + term
        total[:, z_rows, cols] += got.reshape(4, zn, COLS)
    ready(y_held, 2)
    for weight, cols in weights:
        acts = y_held[...].reshape(2 * yn, 8 * SHARE)
        total[2:4, y_rows, cols] = dot(acts, weight[...]).reshape(2, yn, COLS)
    ready(x_held, 3)
    for weight, cols in weights:

        def add(i, el):
            acts = x_held[i].reshape(4 * xn, 4 * SHARE)
            total[:, x_rows, cols] += dot(acts, weight[pl.ds(el * 4 * SHARE, 4 * SHARE), :]).reshape(4, xn, COLS)

        if not keep:
            add(0, 1)

        @pl.when(half == 1)
        def _():
            add(1, 0)

    for ys in range(4):
        out[table[SLOT_OFFSET + ys]] = total[ys].astype(out.dtype)


def product(kernel, table, weights, blocks, slots, held, out, more=()):
    vmem, anywhere = pl.BlockSpec(memory_space=pltpu.VMEM), pl.BlockSpec(memory_space=pl.ANY)
    parts = [blocks[axis][s] for axis in "zyx" for s in slots] + list(more)
    work = 2 * out.shape[0] * (2 if out.ndim == 4 else 1)
    return pl.pallas_call(
        kernel,
        in_specs=[pl.BlockSpec(memory_space=pltpu.SMEM)] + [vmem] * 2 + [anywhere] * len(parts),
        out_specs=vmem,
        out_shape=out,
        scratch_shapes=held,
        compiler_params=pltpu.CompilerParams(vmem_limit_bytes=20 * MIB),
        cost_estimate=pl.CostEstimate(
            flops=work * 512 * 4096 * 256, bytes_accessed=(6 + work) * MIB, transcendentals=0
        ),
    )(table, *weights, *parts)


def spread_kernel(table, owner, own, other, *outs):
    for k, out in enumerate(outs):
        section = owner[table[DEST + k]]
        half = jnp.where(section >= 4, 1, 0)
        far = jnp.where(half == table[XH], 0, 1)
        at = (table[Y] + 8 - section) & 3

        @pl.when(far == table[CORE])
        def _():
            out[...] = own[at]

        @pl.when(far != table[CORE])
        def _():
            out[...] = other[at]


def arrange_kernel(table, *refs):
    parts, out, sems = refs[:4], refs[4], refs[5]
    copies = []
    for dz, part in enumerate(parts):
        at = pl.multiple_of(((table[Z] + 4 - dz) & 3) * (2 * COLS), 2 * COLS)
        copies.append(pltpu.make_async_copy(part, out.at[:, pl.ds(at, 2 * COLS)], sems.at[dz]))
        copies[-1].start()
    for copy in copies:
        copy.wait()


def small_call(kernel, scalars, parts, shapes, out_space, scratch=()):
    smem, vmem = pl.BlockSpec(memory_space=pltpu.SMEM), pl.BlockSpec(memory_space=pltpu.VMEM)
    return pl.pallas_call(
        kernel,
        in_specs=[smem] * len(scalars) + [vmem] * len(parts),
        out_specs=[pl.BlockSpec(memory_space=out_space)] * len(shapes),
        out_shape=[jax.ShapeDtypeStruct(shape, jnp.bfloat16) for shape in shapes],
        scratch_shapes=scratch,
        compiler_params=pltpu.CompilerParams(vmem_limit_bytes=16 * MIB),
        cost_estimate=pl.CostEstimate(flops=0, bytes_accessed=2 * MIB, transcendentals=0),
    )(*scalars, *parts)


def other_core(x, y, z, core):
    return linear(x, y, z, 1 - core)


def shards(master, activations, owner):
    f32, bf16 = jnp.float32, jnp.bfloat16
    rows = jnp.asarray(np.array([device_row(i) for i in range(N_DEV)], np.int32))
    me = lax.axis_index("group") * 16 + lax.axis_index("tp")
    table = lax.dynamic_index_in_dim(rows, me, 0, keepdims=False)

    planes = gather_planes({part: activations[None, at : at + n] for part, (at, n) in PARTS.items()})
    blocks = {axis: gather_last(planes[axis], axis) for axis in "zyx"}

    theirs = permute(refit(table, master, THEIRS), other_core)
    mine = refit(table, master, MINE)
    weights = [mine, theirs]

    zn, yn, xn = (PARTS[a][1] for a in "zyx")
    early = product(
        early_kernel,
        table,
        weights,
        blocks,
        (0, 1),
        [
            pltpu.VMEM((2, 8, zn, 2 * SHARE), bf16),
            pltpu.VMEM((2, 2, yn, 8 * SHARE), bf16),
            pltpu.VMEM((2, 4, xn, 4 * SHARE), bf16),
            pltpu.SemaphoreType.DMA((2, 3)),
        ],
        jax.ShapeDtypeStruct((2, 4, 256, 2 * COLS), f32),
    )
    late = [
        pltpu.VMEM((2, 4, zn, 2 * SHARE), bf16),
        pltpu.VMEM((2, yn, 8 * SHARE), bf16),
        pltpu.VMEM((2, 4, xn, 4 * SHARE), bf16),
        pltpu.VMEM((4, 256, 2 * COLS), f32),
        pltpu.SemaphoreType.DMA((4,)),
    ]
    passed, kept = (
        product(
            functools.partial(late_kernel, keep),
            table,
            weights,
            blocks,
            (2, 3),
            late,
            jax.ShapeDtypeStruct((4, 256, 2 * COLS), f32 if keep else bf16),
            (early,),
        )
        for keep in (False, True)
    )
    total = (kept + permute(passed, other_core).astype(f32)).astype(bf16)

    got = {}
    for dy in (2, 1, 3, 0):
        got[dy] = permute(total[dy], lambda x, y, z, c: linear(x + 2 * c, y + dy, z, c))
    own = jnp.stack([got[dy] for dy in range(4)])
    other = permute(own, other_core)

    picked = small_call(spread_kernel, [table, owner], [own, other], [(256, 2 * COLS)] * 4, pltpu.VMEM)
    got = {}
    for dz in (2, 1, 3, 0):
        got[dz] = permute(picked[dz], lambda x, y, z, c: linear(x ^ c, y, z + dz, x % 2))
    got = [got[dz] for dz in range(4)]
    return small_call(arrange_kernel, [table], got, [(256, 8 * COLS)], pltpu.HBM, [pltpu.SemaphoreType.DMA((4,))])[0]


def solution(mesh):
    in_specs = (P(None, ("group", "tp")), P("group", "tp"), P())
    out_specs = P("group", "tp")
    return jax.shard_map(shards, mesh=mesh, in_specs=in_specs, out_specs=out_specs, check_vma=False)
```

```python
import functools

import jax
import jax.numpy as jnp
import numpy as np
from jax import lax
from jax.experimental import pallas as pl
from jax.experimental.pallas import tpu as pltpu
from jax.sharding import PartitionSpec as P

BLOCK = 128
AXES = ("group", "tp")
N_DEV = 128
SHARE = 512
COLS = 256
PARTS = {"z": (0, 64), "y": (64, 64), "x": (128, 64)}
RING_ROWS = 192
REST = 256 - RING_ROWS
ORDER = {"z": "xyz", "y": "zxy", "x": "yzx"}
MIB = 1024 * 1024


def coords(i):
    return i // 64 * 2 + i // 8 % 2, i // 16 % 4, i // 2 % 4, i % 2


def linear(x, y, z, core):
    x, y, z = x % 4, y % 4, z % 4
    return x // 2 * 64 + y * 16 + x % 2 * 8 + z * 2 + core


def permute(value, move):
    return lax.ppermute(value, AXES, [(i, move(*coords(i))) for i in range(N_DEV)])


def offset(slot, at, core):
    step = -1 if (at + core) % 2 else 1
    return (0, step, -step, 2)[slot] % 4


def exchange(value, axis, which):
    def move(x, y, z, core):
        at = {"x": x, "y": y, "z": z}
        at[axis] += offset(which, at[axis], core)
        return linear(at["x"], at["y"], at["z"], core)

    return permute(value, move)


def join_kernel(*refs):
    pairs, outs = refs[:6], refs[6:]
    for i, out in enumerate(outs):
        left, right = pairs[2 * i], pairs[2 * i + 1]
        n = left.shape[0]
        out[:n] = left[...]
        out[n:] = right[...]


def join(pairs):
    vmem = pl.BlockSpec(memory_space=pltpu.VMEM)
    shapes = [(2 * left.shape[0], *left.shape[1:]) for left, _ in pairs]
    size = sum(left.size for left, _ in pairs)
    return pl.pallas_call(
        join_kernel,
        in_specs=[vmem] * 6,
        out_specs=[vmem] * 3,
        out_shape=[jax.ShapeDtypeStruct(shape, jnp.bfloat16) for shape in shapes],
        compiler_params=pltpu.CompilerParams(vmem_limit_bytes=16 * MIB),
        cost_estimate=pl.CostEstimate(flops=0, bytes_accessed=8 * size, transcendentals=0),
    )(*[v for pair in pairs for v in pair])


def gather_planes(blocks):
    for level in range(2):
        for which in (1, 2):
            pairs = {part: (block, exchange(block, ORDER[part][level], which)) for part, block in blocks.items()}
            if level == 0:
                blocks = lax.optimization_barrier({part: jnp.concatenate(pair) for part, pair in pairs.items()})
            else:
                blocks = dict(zip(pairs, join(list(pairs.values()))))
    return blocks


def gather_last(block, axis):
    first = exchange(block, axis, 1)
    if axis != "y":
        first, block = lax.optimization_barrier((first, block))
    second = exchange(block, axis, 2)
    relayed = exchange(first, axis, 2)
    return [v.reshape(4, 4, *v.shape[1:]) for v in (block, first, second, relayed)]


MINE, THEIRS, CORE, SLOT_OFFSET, XH, Y, Z, DEST, WIDTH = 0, 8, 16, 17, 21, 22, 23, 24, 28


def device_row(i):
    x, y, z, core = coords(i)
    xh, xl = x // 2, x % 2

    def chunks(c):
        return [(xl ^ n // 4) * 8 + (z + offset(n % 4, z, c)) % 4 * 2 + c for n in range(8)]

    dest = [(xl ^ core) * 4 + (z + dz) % 4 for dz in range(4)]
    row = chunks(core) + chunks(1 - core) + [core] + [offset(s, y, core) for s in range(4)] + [xh, y, z] + dest
    assert len(row) == WIDTH
    return row


def refit_kernel(first, table, master, out, held, sems):
    copies = []
    for n in range(8):
        at = pl.multiple_of(table[first + n] * SHARE, SHARE)
        copies.append(pltpu.make_async_copy(master.at[pl.ds(at, SHARE)], held.at[n], sems.at[n]))
        copies[-1].start()
    tiles = SHARE // BLOCK
    for n in range(8):
        copies[n].wait()
        amax = jnp.max(jnp.abs(held[n]).reshape(tiles, BLOCK, COLS), axis=1)
        for c in range(COLS // BLOCK):
            cols = slice(c * BLOCK, (c + 1) * BLOCK)
            top = jnp.max(amax[:, cols], axis=1, keepdims=True)
            scales = ((top + 1e-6) / 448.0).astype(jnp.bfloat16).astype(jnp.float32)
            inverses = 1.0 / scales
            for r in range(tiles):
                tile = held[n, r * BLOCK : (r + 1) * BLOCK, cols]
                coded = (tile * inverses[r : r + 1]).astype(jnp.bfloat16)
                value = (coded.astype(jnp.float32) * scales[r : r + 1]).astype(jnp.bfloat16)
                out[n * SHARE + r * BLOCK : n * SHARE + (r + 1) * BLOCK, cols] = value


def refit(table, master, first):
    size = 8 * SHARE * COLS
    return pl.pallas_call(
        functools.partial(refit_kernel, first),
        in_specs=[pl.BlockSpec(memory_space=pltpu.SMEM), pl.BlockSpec(memory_space=pltpu.HBM)],
        out_specs=pl.BlockSpec(memory_space=pltpu.VMEM),
        out_shape=jax.ShapeDtypeStruct((8 * SHARE, COLS), jnp.bfloat16),
        scratch_shapes=[pltpu.VMEM((8, SHARE, COLS), jnp.float32), pltpu.SemaphoreType.DMA((8,))],
        compiler_params=pltpu.CompilerParams(vmem_limit_bytes=44 * MIB),
        cost_estimate=pl.CostEstimate(flops=size * 6, bytes_accessed=size * 6, transcendentals=0),
    )(table, master)


def rows_of(axis):
    at, count = PARTS[axis]
    return pl.ds(at, count)


def dot(a, b):
    return jnp.dot(a, b, preferred_element_type=jnp.float32)


def halves(core):
    return ((0, 0), (core, 1), (1 - core, 1), (1, 0))


def column_slices(core):
    return [pl.ds(pl.multiple_of(c * COLS, COLS), COLS) for c in (core, 1 - core)]


def early_kernel(table, mine, theirs, z0, z1, y0, y1, x0, x1, out, z_held, y_held, x_held, sems):
    core = table[CORE]
    zn, yn, xn = (PARTS[a][1] for a in "zyx")
    for i, (z_part, y_part, x_part) in enumerate(((z0, y0, x0), (z1, y1, x1))):
        for sx, (eh, el) in enumerate(halves(core)):
            cols = pl.ds(el * SHARE, SHARE)
            pltpu.make_async_copy(z_part.at[:, sx], z_held.at[i, pl.ds(eh * 4, 4), :, cols], sems.at[i, 0]).start()
            for zs in range(4):
                cols = pl.ds((el * 4 + zs) * SHARE, SHARE)
                pltpu.make_async_copy(y_part.at[sx, zs], y_held.at[i, eh, :, cols], sems.at[i, 1]).start()
        for zs in range(4):
            cols = pl.ds(zs * SHARE, SHARE)
            pltpu.make_async_copy(x_part.at[zs], x_held.at[i, :, :, cols], sems.at[i, 2]).start()

    z_rows, y_rows, x_rows = rows_of("z"), rows_of("y"), rows_of("x")
    weights = list(zip((mine, theirs), column_slices(core)))
    for i in range(2):
        for which, held in enumerate((z_held, y_held, x_held)):
            pltpu.make_async_copy(held.at[i], held.at[i], sems.at[i, which]).wait()
        for weight, cols in weights:
            for eh in range(2):
                acts = z_held[i, pl.ds(eh * 4, 4)].reshape(4 * zn, 2 * SHARE)
                got = dot(acts[:, :SHARE], weight[pl.ds(i * SHARE, SHARE), :])
                got += dot(acts[:, SHARE:], weight[pl.ds((4 + i) * SHARE, SHARE), :])
                got = got.reshape(4, zn, COLS)
                if i == 0:
                    out[eh, :, z_rows, cols] = got
                else:
                    out[eh, :, z_rows, cols] += got
            acts = y_held[i].reshape(2 * yn, 8 * SHARE)
            out[:, i, y_rows, cols] = dot(acts, weight[...]).reshape(2, yn, COLS)
            eh, el = halves(core)[i]
            acts = x_held[i].reshape(4 * xn, 4 * SHARE)
            got = dot(acts, weight[pl.ds(el * 4 * SHARE, 4 * SHARE), :]).reshape(4, xn, COLS)
            if i == 0:
                out[0, :, x_rows, cols] = got
                out[1, :, x_rows, cols] = jnp.zeros_like(got)
            else:
                out[eh, :, x_rows, cols] += got


def rest_kernel(table, mine, theirs, gathered, out, held, sems):
    core = table[CORE]
    for eh in range(2):
        for ys in range(4):
            group = (table[XH] ^ eh) * 4 + ((table[Y] + table[SLOT_OFFSET + ys]) & 3)
            for n in range(8):
                source = gathered.at[group * 8 + (table[MINE + n] >> 1)]
                pltpu.make_async_copy(source, held.at[eh, ys, :, pl.ds(n * SHARE, SHARE)], sems.at[eh]).start()
    for eh in range(2):
        pltpu.make_async_copy(held.at[eh], held.at[eh], sems.at[eh]).wait()
        acts = held[eh].reshape(4 * REST, 8 * SHARE)
        for weight, cols in zip((mine, theirs), column_slices(core)):
            out[eh, :, :, cols] = dot(acts, weight[...]).reshape(4, REST, COLS)


def late_kernel(keep, table, mine, theirs, z2, z3, y2, y3, x2, x3, early, rest, out, z_held, y_held, x_held, total, sems):
    core = table[CORE]
    half = core if keep else 1 - core
    near = jnp.where(half == 0, 0, 3)
    sources = ((near, 0), (1 if keep else 2, 1))
    zn, yn, xn = (PARTS[a][1] for a in "zyx")

    def start(src, dst, which):
        pltpu.make_async_copy(src, dst, sems.at[which]).start()

    def ready(held, which):
        pltpu.make_async_copy(held, held, sems.at[which]).wait()

    for i, part in enumerate((z2, z3)):
        for sx, el in sources:
            start(part.at[:, sx], z_held.at[i, :, :, pl.ds(el * SHARE, SHARE)], 0)
    start(early.at[half], total.at[:, pl.ds(0, RING_ROWS)], 1)
    start(rest.at[half], total.at[:, pl.ds(RING_ROWS, REST)], 4)
    for i, part in enumerate((y2, y3)):
        for sx, el in sources:
            for zs in range(4):
                start(part.at[sx, zs], y_held.at[i, :, pl.ds((el * 4 + zs) * SHARE, SHARE)], 2)
    for i, part in enumerate((x2, x3)):
        for zs in range(4):
            start(part.at[zs], x_held.at[i, :, :, pl.ds(zs * SHARE, SHARE)], 3)

    z_rows, y_rows, x_rows = rows_of("z"), rows_of("y"), rows_of("x")
    weights = list(zip((mine, theirs), column_slices(core)))
    ready(z_held, 0)
    ready(total.at[:, pl.ds(0, RING_ROWS)], 1)
    for weight, cols in weights:
        got = None
        for i in range(2):
            acts = z_held[i].reshape(4 * zn, 2 * SHARE)
            term = dot(acts[:, :SHARE], weight[pl.ds((2 + i) * SHARE, SHARE), :])
            term += dot(acts[:, SHARE:], weight[pl.ds((6 + i) * SHARE, SHARE), :])
            got = term if got is None else got + term
        total[:, z_rows, cols] += got.reshape(4, zn, COLS)
    ready(y_held, 2)
    for weight, cols in weights:
        acts = y_held[...].reshape(2 * yn, 8 * SHARE)
        total[2:4, y_rows, cols] = dot(acts, weight[...]).reshape(2, yn, COLS)
    ready(x_held, 3)
    for weight, cols in weights:

        def add(i, el):
            acts = x_held[i].reshape(4 * xn, 4 * SHARE)
            total[:, x_rows, cols] += dot(acts, weight[pl.ds(el * 4 * SHARE, 4 * SHARE), :]).reshape(4, xn, COLS)

        if not keep:
            add(0, 1)

        @pl.when(half == 1)
        def _():
            add(1, 0)

    ready(total.at[:, pl.ds(RING_ROWS, REST)], 4)
    for ys in range(4):
        out[table[SLOT_OFFSET + ys]] = total[ys].astype(out.dtype)


def product(kernel, table, weights, blocks, slots, held, out, more=(), vmem_mib=20):
    vmem, anywhere = pl.BlockSpec(memory_space=pltpu.VMEM), pl.BlockSpec(memory_space=pl.ANY)
    parts = [blocks[axis][s] for axis in "zyx" for s in slots] + list(more)
    work = 4 if out.ndim == 4 else 2
    return pl.pallas_call(
        kernel,
        in_specs=[pl.BlockSpec(memory_space=pltpu.SMEM)] + [vmem] * 2 + [anywhere] * len(parts),
        out_specs=vmem,
        out_shape=out,
        scratch_shapes=held,
        compiler_params=pltpu.CompilerParams(vmem_limit_bytes=vmem_mib * MIB),
        cost_estimate=pl.CostEstimate(
            flops=work * 512 * 4096 * 256, bytes_accessed=(6 + work) * MIB, transcendentals=0
        ),
    )(table, *weights, *parts)


def spread_kernel(table, owner, own, other, *outs):
    for k, out in enumerate(outs):
        section = owner[table[DEST + k]]
        half = jnp.where(section >= 4, 1, 0)
        far = jnp.where(half == table[XH], 0, 1)
        at = (table[Y] + 8 - section) & 3

        @pl.when(far == table[CORE])
        def _():
            out[...] = own[at]

        @pl.when(far != table[CORE])
        def _():
            out[...] = other[at]


def arrange_kernel(table, *refs):
    parts, out, sems = refs[:4], refs[4], refs[5]
    copies = []
    for dz, part in enumerate(parts):
        at = pl.multiple_of(((table[Z] + 4 - dz) & 3) * (2 * COLS), 2 * COLS)
        copies.append(pltpu.make_async_copy(part, out.at[:, pl.ds(at, 2 * COLS)], sems.at[dz]))
        copies[-1].start()
    for copy in copies:
        copy.wait()


def small_call(kernel, scalars, parts, shapes, out_space, scratch=()):
    smem, vmem = pl.BlockSpec(memory_space=pltpu.SMEM), pl.BlockSpec(memory_space=pltpu.VMEM)
    return pl.pallas_call(
        kernel,
        in_specs=[smem] * len(scalars) + [vmem] * len(parts),
        out_specs=[pl.BlockSpec(memory_space=out_space)] * len(shapes),
        out_shape=[jax.ShapeDtypeStruct(shape, jnp.bfloat16) for shape in shapes],
        scratch_shapes=scratch,
        compiler_params=pltpu.CompilerParams(vmem_limit_bytes=16 * MIB),
        cost_estimate=pl.CostEstimate(flops=0, bytes_accessed=2 * MIB, transcendentals=0),
    )(*scalars, *parts)


def other_core(x, y, z, core):
    return linear(x, y, z, 1 - core)


def shards(master, activations, owner):
    f32, bf16 = jnp.float32, jnp.bfloat16
    rows = jnp.asarray(np.array([device_row(i) for i in range(N_DEV)], np.int32))
    me = lax.axis_index("group") * 16 + lax.axis_index("tp")
    table = lax.dynamic_index_in_dim(rows, me, 0, keepdims=False)

    same_core = [[i for i in range(N_DEV) if i % 2 == c] for c in range(2)]
    gathered = lax.all_gather(activations[RING_ROWS:], AXES, axis=0, tiled=True, axis_index_groups=same_core)
    gathered = gathered.reshape(N_DEV // 2, REST, SHARE)
    planes = gather_planes({part: activations[None, at : at + n] for part, (at, n) in PARTS.items()})
    blocks = {axis: gather_last(planes[axis], axis) for axis in "zyx"}

    theirs = permute(refit(table, master, THEIRS), other_core)
    mine = refit(table, master, MINE)
    weights = [mine, theirs]

    zn, yn, xn = (PARTS[a][1] for a in "zyx")
    early = product(
        early_kernel,
        table,
        weights,
        blocks,
        (0, 1),
        [
            pltpu.VMEM((2, 8, zn, 2 * SHARE), bf16),
            pltpu.VMEM((2, 2, yn, 8 * SHARE), bf16),
            pltpu.VMEM((2, 4, xn, 4 * SHARE), bf16),
            pltpu.SemaphoreType.DMA((2, 3)),
        ],
        jax.ShapeDtypeStruct((2, 4, RING_ROWS, 2 * COLS), f32),
    )
    rest = product(
        rest_kernel,
        table,
        weights,
        blocks,
        (),
        [pltpu.VMEM((2, 4, REST, 8 * SHARE), bf16), pltpu.SemaphoreType.DMA((2,))],
        jax.ShapeDtypeStruct((2, 4, REST, 2 * COLS), f32),
        (gathered,),
        44,
    )
    late = [
        pltpu.VMEM((2, 4, zn, 2 * SHARE), bf16),
        pltpu.VMEM((2, yn, 8 * SHARE), bf16),
        pltpu.VMEM((2, 4, xn, 4 * SHARE), bf16),
        pltpu.VMEM((4, 256, 2 * COLS), f32),
        pltpu.SemaphoreType.DMA((5,)),
    ]
    passed, kept = (
        product(
            functools.partial(late_kernel, keep),
            table,
            weights,
            blocks,
            (2, 3),
            late,
            jax.ShapeDtypeStruct((4, 256, 2 * COLS), f32 if keep else bf16),
            (early, rest),
        )
        for keep in (False, True)
    )
    total = (kept + permute(passed, other_core).astype(f32)).astype(bf16)

    got = {}
    for dy in (2, 1, 3, 0):
        got[dy] = permute(total[dy], lambda x, y, z, c: linear(x + 2 * c, y + dy, z, c))
    own = jnp.stack([got[dy] for dy in range(4)])
    other = permute(own, other_core)

    picked = small_call(spread_kernel, [table, owner], [own, other], [(256, 2 * COLS)] * 4, pltpu.VMEM)
    got = {}
    for dz in (2, 1, 3, 0):
        got[dz] = permute(picked[dz], lambda x, y, z, c: linear(x ^ c, y, z + dz, x % 2))
    got = [got[dz] for dz in range(4)]
    return small_call(arrange_kernel, [table], got, [(256, 8 * COLS)], pltpu.HBM, [pltpu.SemaphoreType.DMA((4,))])[0]


def solution(mesh):
    in_specs = (P(None, ("group", "tp")), P("group", "tp"), P())
    out_specs = P("group", "tp")
    return jax.shard_map(shards, mesh=mesh, in_specs=in_specs, out_specs=out_specs, check_vma=False)
```

```python
import functools

import jax
import jax.numpy as jnp
import numpy as np
from jax import lax
from jax.experimental import pallas as pl
from jax.experimental.pallas import tpu as pltpu
from jax.sharding import PartitionSpec as P

BLOCK = 128
AXES = ("group", "tp")
N_DEV = 128
SHARE = 512
COLS = 256
HALF = 128
MIB = 1024 * 1024


def coords(i):
    return i // 64 * 2 + i // 8 % 2, i // 16 % 4, i // 2 % 4, i % 2


def linear(x, y, z, core):
    x, y, z = x % 4, y % 4, z % 4
    return x // 2 * 64 + y * 16 + x % 2 * 8 + z * 2 + core


def permute(value, move):
    return lax.ppermute(value, AXES, [(i, move(*coords(i))) for i in range(N_DEV)])


def offset(slot, at, core):
    step = -1 if (at + core) % 2 else 1
    return (0, step, -step, 2)[slot] % 4


def exchange(value, axis, which):
    def move(x, y, z, core):
        at = {"x": x, "y": y, "z": z}
        at[axis] += offset(which, at[axis], core)
        return linear(at["x"], at["y"], at["z"], core)

    return permute(value, move)


def pair_exchange(value, axis, which):
    def move(x, y, z, core):
        at = {"x": x, "y": y, "z": z}
        at[axis] += offset(which, at[axis], 0)
        return linear(at["x"], at["y"], at["z"], core)

    return permute(value, move)


def other_core(x, y, z, core):
    return linear(x, y, z, 1 - core)


def other_chip(x, y, z, core):
    return linear(x ^ 1, y, z, core)


def after(value, *others):
    return lax.optimization_barrier((value, *others))[0]


def gather(activations, core, first_job, second_job):
    came = permute(activations, lambda x, y, z, c: linear(x + 2, y, z, c))
    block = jnp.stack([activations, after(came, first_job)])
    blocks = {"z": block[None, :, :HALF], "y": block[None, :, HALF:]}
    blocks = lax.optimization_barrier(blocks)
    for which in (1, 2):
        blocks = {
            part: jnp.concatenate([v, exchange(v, "y" if part == "z" else "z", which)]) for part, v in blocks.items()
        }
        blocks = lax.optimization_barrier(blocks)
    blocks, second_job = lax.optimization_barrier((blocks, second_job))
    slots, relays = {}, []
    for part, v in blocks.items():
        first = pair_exchange(v, part, 1)
        second = pair_exchange(v, part, 2)
        relays.append(jnp.where(core == 0, first, second))
        slots[part] = [v, first, second, exchange(relays[-1], part, 2)]
    return slots, relays


AWAY, HERE, CORE, Y_SLOT, Z_SLOT, Y_LAST, Z_LAST, XH, Y, Z, DEST, WIDTH = 0, 8, 16, 17, 21, 25, 29, 33, 34, 35, 36, 40


def device_row(i):
    x, y, z, core = coords(i)
    xh, xl = x // 2, x % 2

    def chunks(l, c):
        return [l * 8 + (z + dz) % 4 * 2 + c for dz in range(4)]

    row = chunks(1 - xl, core) + chunks(1 - xl, 1 - core) + chunks(xl, 1 - core) + chunks(xl, core) + [core]
    row += [offset(s, y, core) for s in range(4)] + [offset(s, z, core) for s in range(4)]
    row += [offset(s, y, 0) for s in range(4)] + [offset(s, z, 0) for s in range(4)]
    row += [xh, y, z] + [(xl ^ core) * 4 + (z + dz) % 4 for dz in range(4)]
    assert len(row) == WIDTH
    return row


def refit_kernel(first, table, master, *refs):
    outs, (held, sems) = refs[:-2], refs[-2:]
    copies = []
    for n in range(8):
        at = pl.multiple_of(table[first + n] * SHARE, SHARE)
        copies.append(pltpu.make_async_copy(master.at[pl.ds(at, SHARE)], held.at[n], sems.at[n]))
        copies[-1].start()
    tiles = SHARE // BLOCK
    for n in range(8):
        out = outs[n * len(outs) // 8]
        start = n * SHARE % out.shape[0]
        copies[n].wait()
        amax = jnp.max(jnp.abs(held[n]).reshape(tiles, BLOCK, COLS), axis=1)
        for c in range(COLS // BLOCK):
            cols = slice(c * BLOCK, (c + 1) * BLOCK)
            top = jnp.max(amax[:, cols], axis=1, keepdims=True)
            scales = ((top + 1e-6) / 448.0).astype(jnp.bfloat16).astype(jnp.float32)
            inverses = 1.0 / scales
            for r in range(tiles):
                tile = held[n, r * BLOCK : (r + 1) * BLOCK, cols]
                coded = (tile * inverses[r : r + 1]).astype(jnp.bfloat16)
                value = (coded.astype(jnp.float32) * scales[r : r + 1]).astype(jnp.bfloat16)
                out[start + r * BLOCK : start + (r + 1) * BLOCK, cols] = value


def refit(table, master, first, n_outs):
    size = 8 * SHARE * COLS
    return pl.pallas_call(
        functools.partial(refit_kernel, first),
        in_specs=[pl.BlockSpec(memory_space=pltpu.SMEM), pl.BlockSpec(memory_space=pltpu.HBM)],
        out_specs=[pl.BlockSpec(memory_space=pltpu.VMEM)] * n_outs,
        out_shape=[jax.ShapeDtypeStruct((8 * SHARE // n_outs, COLS), jnp.bfloat16)] * n_outs,
        scratch_shapes=[pltpu.VMEM((8, SHARE, COLS), jnp.float32), pltpu.SemaphoreType.DMA((8,))],
        compiler_params=pltpu.CompilerParams(vmem_limit_bytes=44 * MIB),
        cost_estimate=pl.CostEstimate(flops=size * 6, bytes_accessed=size * 6, transcendentals=0),
    )(table, master)


def dot(a, b):
    return jnp.dot(a, b, preferred_element_type=jnp.float32)


def pieces(core, mine, near, far, cross):
    def cols(at, c):
        return pl.ds(pl.multiple_of(at + c * COLS, COLS), COLS)

    return [(mine, cols(0, core)), (near, cols(0, 1 - core)), (far, cols(2 * COLS, core)), (cross, cols(2 * COLS, 1 - core))]


def chunk(distance):
    if isinstance(distance, int):
        return pl.ds(distance * SHARE, SHARE)
    return pl.ds(pl.multiple_of(distance * SHARE, SHARE), SHARE)


def whole_kernel(table, mine, near, far, cross, y0, y1, y2, kept, passed, held, sems):
    core = table[CORE]
    for i, part in enumerate((y0, y1, y2)):
        for zs in range(4):
            to = held.at[i, :, :, chunk(table[Z_SLOT + zs])]
            pltpu.make_async_copy(part.at[zs], to, sems.at[i]).start()
    for i in range(3):
        pltpu.make_async_copy(held.at[i], held.at[i], sems.at[i]).wait()
        to = (table[Y_LAST + i] + 1) >> 1
        for half, out in ((1 - core, passed), (core, kept)):
            acts = held[i, half]
            for weight, cols in pieces(core, mine, near, far, cross):
                out[to, :, cols] = dot(acts, weight[: 4 * SHARE, :]).astype(out.dtype)


def early_kernel(table, mine, near, far, cross, z0, z1, z2, out, held, sems):
    core = table[CORE]
    for i, part in enumerate((z0, z1, z2)):
        pltpu.make_async_copy(part, held.at[i], sems.at[i]).start()
    for i in range(3):
        pltpu.make_async_copy(held.at[i], held.at[i], sems.at[i]).wait()
    for ys in range(4):
        for weight, cols in pieces(core, mine, near, far, cross):
            got = None
            for i in range(3):
                acts = held[i, ys].reshape(2 * HALF, SHARE)
                term = dot(acts, weight[chunk(table[Z_LAST + i]), :])
                got = term if got is None else got + term
            out[:, table[Y_SLOT + ys], :, cols] = got.reshape(2, HALF, COLS)


def late_kernel(keep, table, mine, near, far, cross, z3, y3, early, out, z_held, y_held, total, sems):
    core = table[CORE]
    half = core if keep else 1 - core

    def start(src, dst, which):
        pltpu.make_async_copy(src, dst, sems.at[which]).start()

    def ready(held, which):
        pltpu.make_async_copy(held, held, sems.at[which]).wait()

    for zs in range(4):
        start(y3.at[zs, half], y_held.at[:, chunk(table[Z_SLOT + zs])], 0)
    start(z3.at[:, half], z_held, 1)
    start(early.at[half], total, 2)
    weights = pieces(core, mine, near, far, cross)
    ready(y_held, 0)
    for weight, cols in weights:
        out[4, :, cols] = dot(y_held[...], weight[: 4 * SHARE, :]).astype(out.dtype)
    ready(z_held, 1)
    ready(total, 2)
    acts = z_held[...].reshape(4 * HALF, SHARE)
    for weight, cols in weights:
        got = dot(acts, weight[chunk(2), :]).reshape(4, HALF, COLS)
        for ys in range(4):
            to = table[Y_SLOT + ys]
            out[to, :, cols] = (total[to, :, cols] + got[ys]).astype(out.dtype)


def product(kernel, table, weights, parts, outs, held, work):
    vmem, anywhere = pl.BlockSpec(memory_space=pltpu.VMEM), pl.BlockSpec(memory_space=pl.ANY)
    return pl.pallas_call(
        kernel,
        in_specs=[pl.BlockSpec(memory_space=pltpu.SMEM)] + [vmem] * 4 + [anywhere] * len(parts),
        out_specs=[vmem] * len(outs),
        out_shape=[jax.ShapeDtypeStruct(shape, t) for shape, t in outs],
        scratch_shapes=held,
        compiler_params=pltpu.CompilerParams(vmem_limit_bytes=20 * MIB),
        cost_estimate=pl.CostEstimate(
            flops=work * 2 * 128 * 2048 * 1024, bytes_accessed=work * MIB, transcendentals=0
        ),
    )(table, *weights, *parts)


def spread_kernel(table, owner, own, other, *outs):
    for k, out in enumerate(outs):
        section = owner[table[DEST + k]]
        half = jnp.where(section >= 4, 1, 0)
        far = jnp.where(half == table[XH], 0, 1)
        at = (table[Y] + 8 - section) & 3

        @pl.when(far == table[CORE])
        def _():
            out[...] = own[at]

        @pl.when(far != table[CORE])
        def _():
            out[...] = other[at]


def arrange_kernel(table, *refs):
    parts, out, sems = refs[:4], refs[4], refs[5]
    copies = []
    for dz, part in enumerate(parts):
        at = pl.multiple_of(((table[Z] + 4 - dz) & 3) * (2 * COLS), 2 * COLS)
        copies.append(pltpu.make_async_copy(part, out.at[:, pl.ds(at, 2 * COLS)], sems.at[dz]))
        copies[-1].start()
    for copy in copies:
        copy.wait()


def small_call(kernel, scalars, parts, shapes, out_space, scratch=()):
    smem, vmem = pl.BlockSpec(memory_space=pltpu.SMEM), pl.BlockSpec(memory_space=pltpu.VMEM)
    return pl.pallas_call(
        kernel,
        in_specs=[smem] * len(scalars) + [vmem] * len(parts),
        out_specs=[pl.BlockSpec(memory_space=out_space)] * len(shapes),
        out_shape=[jax.ShapeDtypeStruct(shape, jnp.bfloat16) for shape in shapes],
        scratch_shapes=scratch,
        compiler_params=pltpu.CompilerParams(vmem_limit_bytes=16 * MIB),
        cost_estimate=pl.CostEstimate(flops=0, bytes_accessed=2 * MIB, transcendentals=0),
    )(*scalars, *parts)


def shards(master, activations, owner):
    f32, bf16 = jnp.float32, jnp.bfloat16
    rows = jnp.asarray(np.array([device_row(i) for i in range(N_DEV)], np.int32))
    me = lax.axis_index("group") * 16 + lax.axis_index("tp")
    table = lax.dynamic_index_in_dim(rows, me, 0, keepdims=False)

    same, swapped = refit(table, master, AWAY, 2)
    swapped = permute(swapped, other_chip)
    slots, relays = gather(activations, lax.axis_index("tp") % 2, same, swapped)
    far = after(permute(after(same, swapped), other_chip), *relays)
    sent, mine = refit(table, master, HERE, 2)
    near = permute(sent, other_core)
    cross = permute(swapped, other_core)
    weights = [mine, near, far, cross]

    wide = 4 * COLS
    kept, passed = product(
        whole_kernel,
        table,
        weights,
        slots["y"][:3],
        [((3, HALF, wide), f32), ((3, HALF, wide), bf16)],
        [pltpu.VMEM((3, 2, HALF, 4 * SHARE), bf16), pltpu.SemaphoreType.DMA((3,))],
        6,
    )
    (early,) = product(
        early_kernel,
        after(table, passed),
        weights,
        slots["z"][:3],
        [((2, 4, HALF, wide), f32)],
        [pltpu.VMEM((3, 4, 2, HALF, SHARE), bf16), pltpu.SemaphoreType.DMA((3,))],
        6,
    )

    def cores_sum(kept, passed):
        both = kept + permute(passed, other_core).astype(f32)
        return both[..., : 2 * COLS], both[..., 2 * COLS :].astype(bf16)

    def chips_sum(own, sent):
        return (own + permute(sent, other_chip).astype(f32)).astype(bf16)

    own, sent = cores_sum(kept, passed)
    late_table = after(table, sent)
    whole = chips_sum(own, sent)
    passed, kept = (
        product(
            functools.partial(late_kernel, keep),
            late_table,
            weights,
            [slots["z"][3], slots["y"][3], early],
            [((5, HALF, wide), f32 if keep else bf16)],
            [
                pltpu.VMEM((4, HALF, SHARE), bf16),
                pltpu.VMEM((HALF, 4 * SHARE), bf16),
                pltpu.VMEM((4, HALF, wide), f32),
                pltpu.SemaphoreType.DMA((3,)),
            ],
            2,
        )[0]
        for keep in (False, True)
    )
    rest = chips_sum(*cores_sum(kept, passed))
    y_rows = (whole[0], whole[1], rest[4], whole[2])
    total = [jnp.concatenate([rest[dy], y_rows[dy]]) for dy in range(4)]

    got = {}
    for dy in (2, 1, 3, 0):
        got[dy] = permute(total[dy], lambda x, y, z, c: linear(x + 2 * c, y + dy, z, c))
    own = jnp.stack([got[dy] for dy in range(4)])
    other = permute(own, other_core)

    picked = small_call(spread_kernel, [table, owner], [own, other], [(256, 2 * COLS)] * 4, pltpu.VMEM)
    got = {}
    for dz in (2, 1, 3, 0):
        got[dz] = permute(picked[dz], lambda x, y, z, c: linear(x ^ c, y, z + dz, x % 2))
    got = [got[dz] for dz in range(4)]
    return small_call(arrange_kernel, [table], got, [(256, 8 * COLS)], pltpu.HBM, [pltpu.SemaphoreType.DMA((4,))])[0]


def solution(mesh):
    in_specs = (P(None, ("group", "tp")), P("group", "tp"), P())
    out_specs = P("group", "tp")
    return jax.shard_map(shards, mesh=mesh, in_specs=in_specs, out_specs=out_specs, check_vma=False)
```

```python
import functools

import jax
import jax.numpy as jnp
import numpy as np
from jax import lax
from jax.experimental import pallas as pl
from jax.experimental.pallas import tpu as pltpu
from jax.sharding import PartitionSpec as P

BLOCK = 128
AXES = ("group", "tp")
N_DEV = 128
SHARE = 512
COLS = 256
HALF = 128
MIB = 1024 * 1024


def coords(i):
    return i // 64 * 2 + i // 8 % 2, i // 16 % 4, i // 2 % 4, i % 2


def linear(x, y, z, core):
    x, y, z = x % 4, y % 4, z % 4
    return x // 2 * 64 + y * 16 + x % 2 * 8 + z * 2 + core


def permute(value, move):
    return lax.ppermute(value, AXES, [(i, move(*coords(i))) for i in range(N_DEV)])


def offset(slot, at, core):
    step = -1 if (at + core) % 2 else 1
    return (0, step, -step, 2)[slot] % 4


def exchange(value, axis, which):
    def move(x, y, z, core):
        at = {"x": x, "y": y, "z": z}
        at[axis] += offset(which, at[axis], core)
        return linear(at["x"], at["y"], at["z"], core)

    return permute(value, move)


def pair_exchange(value, axis, which):
    def move(x, y, z, core):
        at = {"x": x, "y": y, "z": z}
        at[axis] += offset(which, at[axis], 0)
        return linear(at["x"], at["y"], at["z"], core)

    return permute(value, move)


def other_core(x, y, z, core):
    return linear(x, y, z, 1 - core)


def other_chip(x, y, z, core):
    return linear(x ^ 1, y, z, core)


def after(value, *others):
    return lax.optimization_barrier((value, *others))[0]


def gather(activations, core, first_job, second_job):
    came = permute(activations, lambda x, y, z, c: linear(x + 2, y, z, c))
    block = jnp.stack([activations, after(came, first_job)])
    blocks = {"z": block[None, :, :HALF], "y": block[None, :, HALF:]}
    blocks = lax.optimization_barrier(blocks)
    for which in (1, 2):
        blocks = {
            part: jnp.concatenate([v, exchange(v, "y" if part == "z" else "z", which)]) for part, v in blocks.items()
        }
        blocks = lax.optimization_barrier(blocks)
    slots, relays = {}, []
    for part, v in blocks.items():
        first = pair_exchange(v, part, 1)
        second = pair_exchange(v, part, 2)
        relays.append(after(jnp.where(core == 0, first, second), second_job))
        slots[part] = [v, first, second, exchange(relays[-1], part, 2)]
    return slots, relays


AWAY, HERE, CORE, Y_SLOT, Z_SLOT, Y_LAST, Z_LAST, XH, Y, Z, DEST, WIDTH = 0, 8, 16, 17, 21, 25, 29, 33, 34, 35, 36, 40


def device_row(i):
    x, y, z, core = coords(i)
    xh, xl = x // 2, x % 2

    def chunks(l, c):
        return [l * 8 + (z + dz) % 4 * 2 + c for dz in range(4)]

    row = chunks(1 - xl, core) + chunks(1 - xl, 1 - core) + chunks(xl, 1 - core) + chunks(xl, core) + [core]
    row += [offset(s, y, core) for s in range(4)] + [offset(s, z, core) for s in range(4)]
    row += [offset(s, y, 0) for s in range(4)] + [offset(s, z, 0) for s in range(4)]
    row += [xh, y, z] + [(xl ^ core) * 4 + (z + dz) % 4 for dz in range(4)]
    assert len(row) == WIDTH
    return row


def refit_kernel(first, table, master, *refs):
    outs, (held, sems) = refs[:-2], refs[-2:]
    copies = []
    for n in range(8):
        at = pl.multiple_of(table[first + n] * SHARE, SHARE)
        copies.append(pltpu.make_async_copy(master.at[pl.ds(at, SHARE)], held.at[n], sems.at[n]))
        copies[-1].start()
    tiles = SHARE // BLOCK
    for n in range(8):
        out = outs[n * len(outs) // 8]
        start = n * SHARE % out.shape[0]
        copies[n].wait()
        amax = jnp.max(jnp.abs(held[n]).reshape(tiles, BLOCK, COLS), axis=1)
        for c in range(COLS // BLOCK):
            cols = slice(c * BLOCK, (c + 1) * BLOCK)
            top = jnp.max(amax[:, cols], axis=1, keepdims=True)
            scales = ((top + 1e-6) / 448.0).astype(jnp.bfloat16).astype(jnp.float32)
            inverses = 1.0 / scales
            for r in range(tiles):
                tile = held[n, r * BLOCK : (r + 1) * BLOCK, cols]
                coded = (tile * inverses[r : r + 1]).astype(jnp.bfloat16)
                value = (coded.astype(jnp.float32) * scales[r : r + 1]).astype(jnp.bfloat16)
                out[start + r * BLOCK : start + (r + 1) * BLOCK, cols] = value


def refit(table, master, first, n_outs):
    size = 8 * SHARE * COLS
    return pl.pallas_call(
        functools.partial(refit_kernel, first),
        in_specs=[pl.BlockSpec(memory_space=pltpu.SMEM), pl.BlockSpec(memory_space=pltpu.HBM)],
        out_specs=[pl.BlockSpec(memory_space=pltpu.VMEM)] * n_outs,
        out_shape=[jax.ShapeDtypeStruct((8 * SHARE // n_outs, COLS), jnp.bfloat16)] * n_outs,
        scratch_shapes=[pltpu.VMEM((8, SHARE, COLS), jnp.float32), pltpu.SemaphoreType.DMA((8,))],
        compiler_params=pltpu.CompilerParams(vmem_limit_bytes=44 * MIB),
        cost_estimate=pl.CostEstimate(flops=size * 6, bytes_accessed=size * 6, transcendentals=0),
    )(table, master)


def dot(a, b):
    return jnp.dot(a, b, preferred_element_type=jnp.float32)


def pieces(core, mine, near, far, cross):
    def cols(at, c):
        return pl.ds(pl.multiple_of(at + c * COLS, COLS), COLS)

    return [(mine, cols(0, core)), (near, cols(0, 1 - core)), (far, cols(2 * COLS, core)), (cross, cols(2 * COLS, 1 - core))]


def chunk(distance):
    if isinstance(distance, int):
        return pl.ds(distance * SHARE, SHARE)
    return pl.ds(pl.multiple_of(distance * SHARE, SHARE), SHARE)


def early_kernel(table, mine, near, far, cross, y0, y1, y2, z0, z1, z2, kept, passed, out, y_held, z_held, sems):
    core = table[CORE]
    for i, part in enumerate((y0, y1, y2)):
        for zs in range(4):
            to = y_held.at[i, :, :, chunk(table[Z_SLOT + zs])]
            pltpu.make_async_copy(part.at[zs], to, sems.at[i]).start()
    for i, part in enumerate((z0, z1, z2)):
        pltpu.make_async_copy(part, z_held.at[i], sems.at[3 + i]).start()
    weights = pieces(core, mine, near, far, cross)
    for i in range(3):
        pltpu.make_async_copy(y_held.at[i], y_held.at[i], sems.at[i]).wait()
        to = (table[Y_LAST + i] + 1) >> 1
        for half, result in ((1 - core, passed), (core, kept)):
            acts = y_held[i, half]
            for weight, cols in weights:
                result[to, :, cols] = dot(acts, weight[: 4 * SHARE, :]).astype(result.dtype)
    for i in range(3):
        pltpu.make_async_copy(z_held.at[i], z_held.at[i], sems.at[3 + i]).wait()
    for ys in range(4):
        for weight, cols in weights:
            got = None
            for i in range(3):
                acts = z_held[i, ys].reshape(2 * HALF, SHARE)
                term = dot(acts, weight[chunk(table[Z_LAST + i]), :])
                got = term if got is None else got + term
            out[:, table[Y_SLOT + ys], :, cols] = got.reshape(2, HALF, COLS)


def late_kernel(keep, table, mine, near, far, cross, z3, y3, early, out, z_held, y_held, total, sems):
    core = table[CORE]
    half = core if keep else 1 - core

    def start(src, dst, which):
        pltpu.make_async_copy(src, dst, sems.at[which]).start()

    def ready(held, which):
        pltpu.make_async_copy(held, held, sems.at[which]).wait()

    for zs in range(4):
        start(y3.at[zs, half], y_held.at[:, chunk(table[Z_SLOT + zs])], 0)
    start(z3.at[:, half], z_held, 1)
    start(early.at[half], total, 2)
    weights = pieces(core, mine, near, far, cross)
    ready(y_held, 0)
    for weight, cols in weights:
        out[4, :, cols] = dot(y_held[...], weight[: 4 * SHARE, :]).astype(out.dtype)
    ready(z_held, 1)
    ready(total, 2)
    acts = z_held[...].reshape(4 * HALF, SHARE)
    for weight, cols in weights:
        got = dot(acts, weight[chunk(2), :]).reshape(4, HALF, COLS)
        for ys in range(4):
            to = table[Y_SLOT + ys]
            out[to, :, cols] = (total[to, :, cols] + got[ys]).astype(out.dtype)


def product(kernel, table, weights, parts, outs, held, work):
    vmem, anywhere = pl.BlockSpec(memory_space=pltpu.VMEM), pl.BlockSpec(memory_space=pl.ANY)
    return pl.pallas_call(
        kernel,
        in_specs=[pl.BlockSpec(memory_space=pltpu.SMEM)] + [vmem] * 4 + [anywhere] * len(parts),
        out_specs=[vmem] * len(outs),
        out_shape=[jax.ShapeDtypeStruct(shape, t) for shape, t in outs],
        scratch_shapes=held,
        compiler_params=pltpu.CompilerParams(vmem_limit_bytes=20 * MIB),
        cost_estimate=pl.CostEstimate(
            flops=work * 2 * 128 * 2048 * 1024, bytes_accessed=work * MIB, transcendentals=0
        ),
    )(table, *weights, *parts)


def spread_kernel(table, owner, own, other, *outs):
    for k, out in enumerate(outs):
        section = owner[table[DEST + k]]
        half = jnp.where(section >= 4, 1, 0)
        far = jnp.where(half == table[XH], 0, 1)
        at = (table[Y] + 8 - section) & 3

        @pl.when(far == table[CORE])
        def _():
            out[...] = own[at]

        @pl.when(far != table[CORE])
        def _():
            out[...] = other[at]


def arrange_kernel(table, *refs):
    parts, out, sems = refs[:4], refs[4], refs[5]
    copies = []
    for dz, part in enumerate(parts):
        at = pl.multiple_of(((table[Z] + 4 - dz) & 3) * (2 * COLS), 2 * COLS)
        copies.append(pltpu.make_async_copy(part, out.at[:, pl.ds(at, 2 * COLS)], sems.at[dz]))
        copies[-1].start()
    for copy in copies:
        copy.wait()


def small_call(kernel, scalars, parts, shapes, out_space, scratch=()):
    smem, vmem = pl.BlockSpec(memory_space=pltpu.SMEM), pl.BlockSpec(memory_space=pltpu.VMEM)
    return pl.pallas_call(
        kernel,
        in_specs=[smem] * len(scalars) + [vmem] * len(parts),
        out_specs=[pl.BlockSpec(memory_space=out_space)] * len(shapes),
        out_shape=[jax.ShapeDtypeStruct(shape, jnp.bfloat16) for shape in shapes],
        scratch_shapes=scratch,
        compiler_params=pltpu.CompilerParams(vmem_limit_bytes=16 * MIB),
        cost_estimate=pl.CostEstimate(flops=0, bytes_accessed=2 * MIB, transcendentals=0),
    )(*scalars, *parts)


def shards(master, activations, owner):
    f32, bf16 = jnp.float32, jnp.bfloat16
    rows = jnp.asarray(np.array([device_row(i) for i in range(N_DEV)], np.int32))
    me = lax.axis_index("group") * 16 + lax.axis_index("tp")
    table = lax.dynamic_index_in_dim(rows, me, 0, keepdims=False)

    same, swapped = refit(table, master, AWAY, 2)
    swapped = permute(swapped, other_chip)
    slots, relays = gather(activations, lax.axis_index("tp") % 2, same, swapped)
    far = after(permute(after(same, swapped), other_chip), *relays)
    sent, mine = refit(table, master, HERE, 2)
    near = permute(sent, other_core)
    cross = permute(swapped, other_core)
    weights = [mine, near, far, cross]

    wide = 4 * COLS
    kept, passed, early = product(
        early_kernel,
        table,
        weights,
        slots["y"][:3] + slots["z"][:3],
        [((3, HALF, wide), f32), ((3, HALF, wide), bf16), ((2, 4, HALF, wide), f32)],
        [
            pltpu.VMEM((3, 2, HALF, 4 * SHARE), bf16),
            pltpu.VMEM((3, 4, 2, HALF, SHARE), bf16),
            pltpu.SemaphoreType.DMA((6,)),
        ],
        12,
    )

    def cores_sum(kept, passed):
        both = kept + permute(passed, other_core).astype(f32)
        return both[..., : 2 * COLS], both[..., 2 * COLS :].astype(bf16)

    def chips_sum(own, sent):
        return (own + permute(sent, other_chip).astype(f32)).astype(bf16)

    own, sent = cores_sum(kept, passed)
    late_table = after(table, sent)
    whole = chips_sum(own, sent)
    passed, kept = (
        product(
            functools.partial(late_kernel, keep),
            late_table,
            weights,
            [slots["z"][3], slots["y"][3], early],
            [((5, HALF, wide), f32 if keep else bf16)],
            [
                pltpu.VMEM((4, HALF, SHARE), bf16),
                pltpu.VMEM((HALF, 4 * SHARE), bf16),
                pltpu.VMEM((4, HALF, wide), f32),
                pltpu.SemaphoreType.DMA((3,)),
            ],
            2,
        )[0]
        for keep in (False, True)
    )
    rest = chips_sum(*cores_sum(kept, passed))

    def back(rows, dy):
        return permute(rows, lambda x, y, z, c: linear(x + 2 * c, y + dy, z, c))

    first = {dy: back(whole[i], dy) for i, dy in ((1, 1), (2, 3), (0, 0))}
    rest = after(rest, *first.values())
    got = {2: back(jnp.concatenate([rest[2], rest[4]]), 2)}
    for dy in (1, 3, 0):
        got[dy] = jnp.concatenate([back(rest[dy], dy), first[dy]])
    own = jnp.stack([got[dy] for dy in range(4)])
    other = permute(own, other_core)

    picked = small_call(spread_kernel, [table, owner], [own, other], [(256, 2 * COLS)] * 4, pltpu.VMEM)
    got = {}
    for dz in (2, 1, 3, 0):
        got[dz] = permute(picked[dz], lambda x, y, z, c: linear(x ^ c, y, z + dz, x % 2))
    got = [got[dz] for dz in range(4)]
    return small_call(arrange_kernel, [table], got, [(256, 8 * COLS)], pltpu.HBM, [pltpu.SemaphoreType.DMA((4,))])[0]


def solution(mesh):
    in_specs = (P(None, ("group", "tp")), P("group", "tp"), P())
    out_specs = P("group", "tp")
    return jax.shard_map(shards, mesh=mesh, in_specs=in_specs, out_specs=out_specs, check_vma=False)
```

```python
import functools

import jax
import jax.numpy as jnp
import numpy as np
from jax import lax
from jax.experimental import pallas as pl
from jax.experimental.pallas import tpu as pltpu
from jax.sharding import PartitionSpec as P

BLOCK = 128
AXES = ("group", "tp")
N_DEV = 128
SHARE = 512
COLS = 256
HALF = 128
MIB = 1024 * 1024


def coords(i):
    return i // 64 * 2 + i // 8 % 2, i // 16 % 4, i // 2 % 4, i % 2


def linear(x, y, z, core):
    x, y, z = x % 4, y % 4, z % 4
    return x // 2 * 64 + y * 16 + x % 2 * 8 + z * 2 + core


def permute(value, move):
    return lax.ppermute(value, AXES, [(i, move(*coords(i))) for i in range(N_DEV)])


def offset(slot, at, core):
    step = -1 if (at + core) % 2 else 1
    return (0, step, -step, 2)[slot] % 4


def exchange(value, axis, which):
    def move(x, y, z, core):
        at = {"x": x, "y": y, "z": z}
        at[axis] += offset(which, at[axis], core)
        return linear(at["x"], at["y"], at["z"], core)

    return permute(value, move)


def other_core(x, y, z, core):
    return linear(x, y, z, 1 - core)


def other_chip(x, y, z, core):
    return linear(x ^ 1, y, z, core)


def after(value, *others):
    return lax.optimization_barrier((value, *others))[0]


def gather(activations, first_job, second_job, third_job):
    came = permute(activations, lambda x, y, z, c: linear(x + 2, y, z, c))
    block = jnp.stack([activations, after(came, first_job)])
    blocks = {"z": block[None, :, :HALF], "y": block[None, :, HALF:]}
    blocks = lax.optimization_barrier(blocks)
    for which in (1, 2):
        blocks = {
            part: jnp.concatenate([v, exchange(v, "y" if part == "z" else "z", which)]) for part, v in blocks.items()
        }
        blocks = lax.optimization_barrier(blocks)
    blocks, second_job = lax.optimization_barrier((blocks, second_job))
    slots = {}
    for part, v in blocks.items():
        first = exchange(v, part, 1)
        second = exchange(v, part, 2)
        slots[part] = [v, first, second, exchange(after(first, third_job), part, 2)]
    return slots


AWAY, HERE, CORE, Y_SLOT, Z_SLOT, XH, Y, Z, DEST, WIDTH = 0, 8, 16, 17, 21, 25, 26, 27, 28, 32


def device_row(i):
    x, y, z, core = coords(i)
    xh, xl = x // 2, x % 2

    def chunks(l, c):
        return [l * 8 + (z + dz) % 4 * 2 + c for dz in range(4)]

    row = chunks(1 - xl, core) + chunks(1 - xl, 1 - core) + chunks(xl, 1 - core) + chunks(xl, core) + [core]
    row += [offset(s, y, core) for s in range(4)] + [offset(s, z, core) for s in range(4)]
    row += [xh, y, z] + [(xl ^ core) * 4 + (z + dz) % 4 for dz in range(4)]
    assert len(row) == WIDTH
    return row


def refit_kernel(first, table, master, *refs):
    outs, (held, sems) = refs[:-2], refs[-2:]
    copies = []
    for n in range(8):
        at = pl.multiple_of(table[first + n] * SHARE, SHARE)
        copies.append(pltpu.make_async_copy(master.at[pl.ds(at, SHARE)], held.at[n], sems.at[n]))
        copies[-1].start()
    tiles = SHARE // BLOCK
    for n in range(8):
        out = outs[n * len(outs) // 8]
        start = n * SHARE % out.shape[0]
        copies[n].wait()
        amax = jnp.max(jnp.abs(held[n]).reshape(tiles, BLOCK, COLS), axis=1)
        for c in range(COLS // BLOCK):
            cols = slice(c * BLOCK, (c + 1) * BLOCK)
            top = jnp.max(amax[:, cols], axis=1, keepdims=True)
            scales = ((top + 1e-6) / 448.0).astype(jnp.bfloat16).astype(jnp.float32)
            inverses = 1.0 / scales
            for r in range(tiles):
                tile = held[n, r * BLOCK : (r + 1) * BLOCK, cols]
                coded = (tile * inverses[r : r + 1]).astype(jnp.bfloat16)
                value = (coded.astype(jnp.float32) * scales[r : r + 1]).astype(jnp.bfloat16)
                out[start + r * BLOCK : start + (r + 1) * BLOCK, cols] = value


def refit(table, master, first, n_outs):
    size = 8 * SHARE * COLS
    return pl.pallas_call(
        functools.partial(refit_kernel, first),
        in_specs=[pl.BlockSpec(memory_space=pltpu.SMEM), pl.BlockSpec(memory_space=pltpu.HBM)],
        out_specs=[pl.BlockSpec(memory_space=pltpu.VMEM)] * n_outs,
        out_shape=[jax.ShapeDtypeStruct((8 * SHARE // n_outs, COLS), jnp.bfloat16)] * n_outs,
        scratch_shapes=[pltpu.VMEM((8, SHARE, COLS), jnp.float32), pltpu.SemaphoreType.DMA((8,))],
        compiler_params=pltpu.CompilerParams(vmem_limit_bytes=44 * MIB),
        cost_estimate=pl.CostEstimate(flops=size * 6, bytes_accessed=size * 6, transcendentals=0),
    )(table, master)


def dot(a, b):
    return jnp.dot(a, b, preferred_element_type=jnp.float32)


def pieces(core, mine, near, far, cross):
    def cols(at, c):
        return pl.ds(pl.multiple_of(at + c * COLS, COLS), COLS)

    return [(mine, cols(0, core)), (near, cols(0, 1 - core)), (far, cols(2 * COLS, core)), (cross, cols(2 * COLS, 1 - core))]


def product_kernel(part, half_of, table, mine, near, far, cross, *refs):
    slots, (out, held, sems) = refs[:4], refs[4:]
    core = table[CORE]
    half = half_of(core)
    for i, slot in enumerate(slots):
        for k in range(4):
            zs = k if part == "y" else i
            depth = pl.ds(pl.multiple_of(table[Z_SLOT + zs] * SHARE, SHARE), SHARE)
            to = held.at[i if part == "y" else k, :, depth]
            pltpu.make_async_copy(slot.at[k, half], to, sems.at[i]).start()
    for i in range(4):
        pltpu.make_async_copy(held.at[i], held.at[i], sems.at[i]).wait()
    acts = held[...].reshape(4 * HALF, 4 * SHARE)
    for weight, cols in pieces(core, mine, near, far, cross):
        got = jnp.dot(acts, weight[...], preferred_element_type=jnp.float32).reshape(4, HALF, COLS)
        for ys in range(4):
            out[table[Y_SLOT + ys], :, cols] = got[ys].astype(out.dtype)


def product(part, keep, table, weights, slots):
    vmem, anywhere = pl.BlockSpec(memory_space=pltpu.VMEM), pl.BlockSpec(memory_space=pl.ANY)
    return pl.pallas_call(
        functools.partial(product_kernel, part, (lambda core: core) if keep else (lambda core: 1 - core)),
        in_specs=[pl.BlockSpec(memory_space=pltpu.SMEM)] + [vmem] * 4 + [anywhere] * 4,
        out_specs=vmem,
        out_shape=jax.ShapeDtypeStruct((4, HALF, 4 * COLS), jnp.float32 if keep else jnp.bfloat16),
        scratch_shapes=[pltpu.VMEM((4, HALF, 4 * SHARE), jnp.bfloat16), pltpu.SemaphoreType.DMA((4,))],
        compiler_params=pltpu.CompilerParams(vmem_limit_bytes=20 * MIB),
        cost_estimate=pl.CostEstimate(flops=2 * 512 * 2048 * 1024, bytes_accessed=8 * MIB, transcendentals=0),
    )(table, *weights, *slots)


def spread_kernel(table, owner, own, other, *outs):
    for k, out in enumerate(outs):
        section = owner[table[DEST + k]]
        half = jnp.where(section >= 4, 1, 0)
        far = jnp.where(half == table[XH], 0, 1)
        at = (table[Y] + 8 - section) & 3

        @pl.when(far == table[CORE])
        def _():
            out[...] = own[at]

        @pl.when(far != table[CORE])
        def _():
            out[...] = other[at]


def arrange_kernel(table, *refs):
    parts, out, sems = refs[:8], refs[8], refs[9]
    copies = []
    for i, part in enumerate(parts):
        rows, dz = i // 4, i % 4
        at = pl.multiple_of(((table[Z] + 4 - dz) & 3) * (2 * COLS), 2 * COLS)
        to = out.at[pl.ds(rows * HALF, HALF), pl.ds(at, 2 * COLS)]
        copies.append(pltpu.make_async_copy(part, to, sems.at[i]))
        copies[-1].start()
    for copy in copies:
        copy.wait()


def small_call(kernel, scalars, parts, shapes, out_space, scratch=()):
    smem, vmem = pl.BlockSpec(memory_space=pltpu.SMEM), pl.BlockSpec(memory_space=pltpu.VMEM)
    return pl.pallas_call(
        kernel,
        in_specs=[smem] * len(scalars) + [vmem] * len(parts),
        out_specs=[pl.BlockSpec(memory_space=out_space)] * len(shapes),
        out_shape=[jax.ShapeDtypeStruct(shape, jnp.bfloat16) for shape in shapes],
        scratch_shapes=scratch,
        compiler_params=pltpu.CompilerParams(vmem_limit_bytes=16 * MIB),
        cost_estimate=pl.CostEstimate(flops=0, bytes_accessed=2 * MIB, transcendentals=0),
    )(*scalars, *parts)


def shards(master, activations, owner):
    f32, bf16 = jnp.float32, jnp.bfloat16
    rows = jnp.asarray(np.array([device_row(i) for i in range(N_DEV)], np.int32))
    me = lax.axis_index("group") * 16 + lax.axis_index("tp")
    table = lax.dynamic_index_in_dim(rows, me, 0, keepdims=False)

    same, swapped = refit(table, master, AWAY, 2)
    sent, mine = refit(table, master, HERE, 2)
    near = permute(sent, other_core)
    swapped = permute(swapped, other_chip)
    cross = permute(swapped, other_core)
    slots = gather(activations, same, near, cross)
    far = permute(after(same, swapped), other_chip)
    weights = [mine, near, far, cross]
    ready = after(table, slots["z"][3], slots["y"][3])

    def chain(part):
        passed = product(part, False, ready, weights, slots[part])
        kept = product(part, True, ready, weights, slots[part])
        both = kept + permute(passed, other_core).astype(f32)
        came = permute(both[..., 2 * COLS :].astype(bf16), other_chip)
        total = (both[..., : 2 * COLS] + came.astype(f32)).astype(bf16)
        got = {}
        for dy in (2, 1, 3, 0):
            got[dy] = permute(total[dy], lambda x, y, z, c: linear(x + 2 * c, y + dy, z, c))
        own = jnp.stack([got[dy] for dy in range(4)])
        other = permute(own, other_core)
        picked = small_call(spread_kernel, [table, owner], [own, other], [(HALF, 2 * COLS)] * 4, pltpu.VMEM)
        got = {}
        for dz in (2, 1, 3, 0):
            got[dz] = permute(picked[dz], lambda x, y, z, c: linear(x ^ c, y, z + dz, x % 2))
        return [got[dz] for dz in range(4)]

    blocks = chain("y")
    blocks = chain("z") + blocks
    return small_call(
        arrange_kernel, [table], blocks, [(256, 8 * COLS)], pltpu.HBM, [pltpu.SemaphoreType.DMA((8,))]
    )[0]


def solution(mesh):
    in_specs = (P(None, ("group", "tp")), P("group", "tp"), P())
    out_specs = P("group", "tp")
    return jax.shard_map(shards, mesh=mesh, in_specs=in_specs, out_specs=out_specs, check_vma=False)
```

```python
import functools

import jax
import jax.numpy as jnp
import numpy as np
from jax import lax
from jax.experimental import pallas as pl
from jax.experimental.pallas import tpu as pltpu
from jax.sharding import PartitionSpec as P

BLOCK = 128
AXES = ("group", "tp")
N_DEV = 128
SHARE = 512
COLS = 256
HALF = 128
MIB = 1024 * 1024


def coords(i):
    return i // 64 * 2 + i // 8 % 2, i // 16 % 4, i // 2 % 4, i % 2


def linear(x, y, z, core):
    x, y, z = x % 4, y % 4, z % 4
    return x // 2 * 64 + y * 16 + x % 2 * 8 + z * 2 + core


def permute(value, move):
    return lax.ppermute(value, AXES, [(i, move(*coords(i))) for i in range(N_DEV)])


def offset(slot, at, core):
    step = -1 if (at + core) % 2 else 1
    return (0, step, -step, 2)[slot] % 4


def exchange(value, axis, which):
    def move(x, y, z, core):
        at = {"x": x, "y": y, "z": z}
        at[axis] += offset(which, at[axis], core)
        return linear(at["x"], at["y"], at["z"], core)

    return permute(value, move)


def other_core(x, y, z, core):
    return linear(x, y, z, 1 - core)


def other_chip(x, y, z, core):
    return linear(x ^ 1, y, z, core)


def after(value, *others):
    return lax.optimization_barrier((value, *others))[0]


def gather(activations, first_job, second_job, third_job):
    came = permute(activations, lambda x, y, z, c: linear(x + 2, y, z, c))
    block = jnp.stack([activations, after(came, first_job)])
    blocks = {"z": block[None, :, :HALF], "y": block[None, :, HALF:]}
    blocks = lax.optimization_barrier(blocks)
    for which in (1, 2):
        blocks = {
            part: jnp.concatenate([v, exchange(v, "y" if part == "z" else "z", which)]) for part, v in blocks.items()
        }
        blocks = lax.optimization_barrier(blocks)
    blocks, second_job = lax.optimization_barrier((blocks, second_job))
    slots = {}
    for part, v in blocks.items():
        first = exchange(v, part, 1)
        second = exchange(after(v, third_job), part, 2)
        slots[part] = [v, first, second, exchange(after(first, third_job), part, 2)]
    return slots


AWAY, HERE, CORE, Y_SLOT, Z_SLOT, XH, Y, Z, DEST, WIDTH = 0, 8, 16, 17, 21, 25, 26, 27, 28, 32


def device_row(i):
    x, y, z, core = coords(i)
    xh, xl = x // 2, x % 2

    def chunks(l, c):
        return [l * 8 + (z + dz) % 4 * 2 + c for dz in range(4)]

    row = chunks(1 - xl, core) + chunks(1 - xl, 1 - core) + chunks(xl, 1 - core) + chunks(xl, core) + [core]
    row += [offset(s, y, core) for s in range(4)] + [offset(s, z, core) for s in range(4)]
    row += [xh, y, z] + [(xl ^ core) * 4 + (z + dz) % 4 for dz in range(4)]
    assert len(row) == WIDTH
    return row


def refit_kernel(first, table, master, *refs):
    outs, (held, sems) = refs[:-2], refs[-2:]
    copies = []
    for n in range(8):
        at = pl.multiple_of(table[first + n] * SHARE, SHARE)
        copies.append(pltpu.make_async_copy(master.at[pl.ds(at, SHARE)], held.at[n], sems.at[n]))
        copies[-1].start()
    tiles = SHARE // BLOCK
    for n in range(8):
        out = outs[n * len(outs) // 8]
        start = n * SHARE % out.shape[0]
        copies[n].wait()
        amax = jnp.max(jnp.abs(held[n]).reshape(tiles, BLOCK, COLS), axis=1)
        for c in range(COLS // BLOCK):
            cols = slice(c * BLOCK, (c + 1) * BLOCK)
            top = jnp.max(amax[:, cols], axis=1, keepdims=True)
            scales = ((top + 1e-6) / 448.0).astype(jnp.bfloat16).astype(jnp.float32)
            inverses = 1.0 / scales
            for r in range(tiles):
                tile = held[n, r * BLOCK : (r + 1) * BLOCK, cols]
                coded = (tile * inverses[r : r + 1]).astype(jnp.bfloat16)
                value = (coded.astype(jnp.float32) * scales[r : r + 1]).astype(jnp.bfloat16)
                out[start + r * BLOCK : start + (r + 1) * BLOCK, cols] = value


def refit(table, master, first, n_outs):
    size = 8 * SHARE * COLS
    return pl.pallas_call(
        functools.partial(refit_kernel, first),
        in_specs=[pl.BlockSpec(memory_space=pltpu.SMEM), pl.BlockSpec(memory_space=pltpu.HBM)],
        out_specs=[pl.BlockSpec(memory_space=pltpu.VMEM)] * n_outs,
        out_shape=[jax.ShapeDtypeStruct((8 * SHARE // n_outs, COLS), jnp.bfloat16)] * n_outs,
        scratch_shapes=[pltpu.VMEM((8, SHARE, COLS), jnp.float32), pltpu.SemaphoreType.DMA((8,))],
        compiler_params=pltpu.CompilerParams(vmem_limit_bytes=44 * MIB),
        cost_estimate=pl.CostEstimate(flops=size * 6, bytes_accessed=size * 6, transcendentals=0),
    )(table, master)


def dot(a, b):
    return jnp.dot(a, b, preferred_element_type=jnp.float32)


def pieces(core, mine, near, far, cross):
    def cols(at, c):
        return pl.ds(pl.multiple_of(at + c * COLS, COLS), COLS)

    return [(mine, cols(0, core)), (near, cols(0, 1 - core)), (far, cols(2 * COLS, core)), (cross, cols(2 * COLS, 1 - core))]


def product_kernel(part, half_of, table, mine, near, far, cross, *refs):
    slots, (out, held, sems) = refs[:4], refs[4:]
    core = table[CORE]
    half = half_of(core)
    for i, slot in enumerate(slots):
        for k in range(4):
            zs = k if part == "y" else i
            depth = pl.ds(pl.multiple_of(table[Z_SLOT + zs] * SHARE, SHARE), SHARE)
            to = held.at[i if part == "y" else k, :, depth]
            pltpu.make_async_copy(slot.at[k, half], to, sems.at[i]).start()
    for i in range(4):
        pltpu.make_async_copy(held.at[i], held.at[i], sems.at[i]).wait()
    acts = held[...].reshape(4 * HALF, 4 * SHARE)
    for weight, cols in pieces(core, mine, near, far, cross):
        got = jnp.dot(acts, weight[...], preferred_element_type=jnp.float32).reshape(4, HALF, COLS)
        for ys in range(4):
            out[table[Y_SLOT + ys], :, cols] = got[ys].astype(out.dtype)


def product(part, keep, table, weights, slots):
    vmem, anywhere = pl.BlockSpec(memory_space=pltpu.VMEM), pl.BlockSpec(memory_space=pl.ANY)
    return pl.pallas_call(
        functools.partial(product_kernel, part, (lambda core: core) if keep else (lambda core: 1 - core)),
        in_specs=[pl.BlockSpec(memory_space=pltpu.SMEM)] + [vmem] * 4 + [anywhere] * 4,
        out_specs=vmem,
        out_shape=jax.ShapeDtypeStruct((4, HALF, 4 * COLS), jnp.float32 if keep else jnp.bfloat16),
        scratch_shapes=[pltpu.VMEM((4, HALF, 4 * SHARE), jnp.bfloat16), pltpu.SemaphoreType.DMA((4,))],
        compiler_params=pltpu.CompilerParams(vmem_limit_bytes=20 * MIB),
        cost_estimate=pl.CostEstimate(flops=2 * 512 * 2048 * 1024, bytes_accessed=8 * MIB, transcendentals=0),
    )(table, *weights, *slots)


def spread_kernel(table, owner, own, other, *outs):
    for k, out in enumerate(outs):
        section = owner[table[DEST + k]]
        half = jnp.where(section >= 4, 1, 0)
        far = jnp.where(half == table[XH], 0, 1)
        at = (table[Y] + 8 - section) & 3

        @pl.when(far == table[CORE])
        def _():
            out[...] = own[at]

        @pl.when(far != table[CORE])
        def _():
            out[...] = other[at]


def arrange_kernel(table, *refs):
    parts, out, sems = refs[:8], refs[8], refs[9]
    copies = []
    for i, part in enumerate(parts):
        rows, dz = i // 4, i % 4
        at = pl.multiple_of(((table[Z] + 4 - dz) & 3) * (2 * COLS), 2 * COLS)
        to = out.at[pl.ds(rows * HALF, HALF), pl.ds(at, 2 * COLS)]
        copies.append(pltpu.make_async_copy(part, to, sems.at[i]))
        copies[-1].start()
    for copy in copies:
        copy.wait()


def small_call(kernel, scalars, parts, shapes, out_space, scratch=()):
    smem, vmem = pl.BlockSpec(memory_space=pltpu.SMEM), pl.BlockSpec(memory_space=pltpu.VMEM)
    return pl.pallas_call(
        kernel,
        in_specs=[smem] * len(scalars) + [vmem] * len(parts),
        out_specs=[pl.BlockSpec(memory_space=out_space)] * len(shapes),
        out_shape=[jax.ShapeDtypeStruct(shape, jnp.bfloat16) for shape in shapes],
        scratch_shapes=scratch,
        compiler_params=pltpu.CompilerParams(vmem_limit_bytes=16 * MIB),
        cost_estimate=pl.CostEstimate(flops=0, bytes_accessed=2 * MIB, transcendentals=0),
    )(*scalars, *parts)


def shards(master, activations, owner):
    f32, bf16 = jnp.float32, jnp.bfloat16
    rows = jnp.asarray(np.array([device_row(i) for i in range(N_DEV)], np.int32))
    me = lax.axis_index("group") * 16 + lax.axis_index("tp")
    table = lax.dynamic_index_in_dim(rows, me, 0, keepdims=False)

    same, swapped = refit(table, master, AWAY, 2)
    sent, mine = refit(table, master, HERE, 2)
    near = permute(sent, other_core)
    far = permute(same, other_chip)
    swapped = permute(swapped, other_core)
    slots = gather(activations, same, (near, swapped), far)
    cross = permute(after(swapped, far), other_chip)
    weights = [mine, near, far, cross]
    ready = after(table, slots["z"][3], slots["y"][3])

    def chain(part):
        passed = product(part, False, ready, weights, slots[part])
        kept = product(part, True, ready, weights, slots[part])
        both = kept + permute(passed, other_core).astype(f32)
        came = permute(both[..., 2 * COLS :].astype(bf16), other_chip)
        total = (both[..., : 2 * COLS] + came.astype(f32)).astype(bf16)
        got = {}
        for dy in (2, 1, 3, 0):
            got[dy] = permute(total[dy], lambda x, y, z, c: linear(x + 2 * c, y + dy, z, c))
        own = jnp.stack([got[dy] for dy in range(4)])
        other = permute(own, other_core)
        picked = small_call(spread_kernel, [table, owner], [own, other], [(HALF, 2 * COLS)] * 4, pltpu.VMEM)
        got = {}
        for dz in (2, 1, 3, 0):
            got[dz] = permute(picked[dz], lambda x, y, z, c: linear(x ^ c, y, z + dz, x % 2))
        return [got[dz] for dz in range(4)]

    blocks = chain("y")
    blocks = chain("z") + blocks
    return small_call(
        arrange_kernel, [table], blocks, [(256, 8 * COLS)], pltpu.HBM, [pltpu.SemaphoreType.DMA((8,))]
    )[0]


def solution(mesh):
    in_specs = (P(None, ("group", "tp")), P("group", "tp"), P())
    out_specs = P("group", "tp")
    return jax.shard_map(shards, mesh=mesh, in_specs=in_specs, out_specs=out_specs, check_vma=False)
```

```python
import functools

import jax
import jax.numpy as jnp
import numpy as np
from jax import lax
from jax.experimental import pallas as pl
from jax.experimental.pallas import tpu as pltpu
from jax.sharding import PartitionSpec as P

BLOCK = 128
AXES = ("group", "tp")
N_DEV = 128
SHARE = 512
COLS = 256
HALF = 128
MIB = 1024 * 1024


def coords(i):
    return i // 64 * 2 + i // 8 % 2, i // 16 % 4, i // 2 % 4, i % 2


def linear(x, y, z, core):
    x, y, z = x % 4, y % 4, z % 4
    return x // 2 * 64 + y * 16 + x % 2 * 8 + z * 2 + core


def permute(value, move):
    return lax.ppermute(value, AXES, [(i, move(*coords(i))) for i in range(N_DEV)])


def offset(slot, at, core):
    step = -1 if (at + core) % 2 else 1
    return (0, step, -step, 2)[slot] % 4


def exchange(value, axis, which):
    def move(x, y, z, core):
        at = {"x": x, "y": y, "z": z}
        at[axis] += offset(which, at[axis], core)
        return linear(at["x"], at["y"], at["z"], core)

    return permute(value, move)


def other_core(x, y, z, core):
    return linear(x, y, z, 1 - core)


def other_chip(x, y, z, core):
    return linear(x ^ 1, y, z, core)


def after(value, *others):
    return lax.optimization_barrier((value, *others))[0]


def gather(activations, first_job, second_job, third_job):
    came = permute(activations, lambda x, y, z, c: linear(x + 2, y, z, c))
    block = jnp.stack([activations, after(came, first_job)])
    blocks = {"z": block[None, :, :HALF], "y": block[None, :, HALF:]}
    blocks = lax.optimization_barrier(blocks)
    for which in (1, 2):
        blocks = {
            part: jnp.concatenate([v, exchange(v, "y" if part == "z" else "z", which)]) for part, v in blocks.items()
        }
        blocks = lax.optimization_barrier(blocks)
    blocks, second_job = lax.optimization_barrier((blocks, second_job))
    slots = {}
    for part, v in blocks.items():
        first = exchange(v, part, 1)
        second = exchange(after(v, third_job), part, 2)
        slots[part] = [v, first, second, exchange(after(first, third_job), part, 2)]
    return slots


AWAY, HERE, CORE, Y_SLOT, Z_SLOT, XH, Y, Z, DEST, WIDTH = 0, 8, 16, 17, 21, 25, 26, 27, 28, 32


def device_row(i):
    x, y, z, core = coords(i)
    xh, xl = x // 2, x % 2

    def chunks(l, c):
        return [l * 8 + (z + dz) % 4 * 2 + c for dz in range(4)]

    row = chunks(1 - xl, core) + chunks(1 - xl, 1 - core) + chunks(xl, 1 - core) + chunks(xl, core) + [core]
    row += [offset(s, y, core) for s in range(4)] + [offset(s, z, core) for s in range(4)]
    row += [xh, y, z] + [(xl ^ core) * 4 + (z + dz) % 4 for dz in range(4)]
    assert len(row) == WIDTH
    return row


def refit_kernel(first, table, master, *refs):
    outs, (held, sems) = refs[:-2], refs[-2:]
    copies = []
    for n in range(8):
        at = pl.multiple_of(table[first + n] * SHARE, SHARE)
        copies.append(pltpu.make_async_copy(master.at[pl.ds(at, SHARE)], held.at[n], sems.at[n]))
        copies[-1].start()
    tiles = SHARE // BLOCK
    for n in range(8):
        out = outs[n * len(outs) // 8]
        start = n * SHARE % out.shape[0]
        copies[n].wait()
        amax = jnp.max(jnp.abs(held[n]).reshape(tiles, BLOCK, COLS), axis=1)
        for c in range(COLS // BLOCK):
            cols = slice(c * BLOCK, (c + 1) * BLOCK)
            top = jnp.max(amax[:, cols], axis=1, keepdims=True)
            scales = ((top + 1e-6) / 448.0).astype(jnp.bfloat16).astype(jnp.float32)
            inverses = 1.0 / scales
            for r in range(tiles):
                tile = held[n, r * BLOCK : (r + 1) * BLOCK, cols]
                coded = (tile * inverses[r : r + 1]).astype(jnp.bfloat16)
                value = (coded.astype(jnp.float32) * scales[r : r + 1]).astype(jnp.bfloat16)
                out[start + r * BLOCK : start + (r + 1) * BLOCK, cols] = value


def refit(table, master, first, n_outs):
    size = 8 * SHARE * COLS
    return pl.pallas_call(
        functools.partial(refit_kernel, first),
        in_specs=[pl.BlockSpec(memory_space=pltpu.SMEM), pl.BlockSpec(memory_space=pltpu.HBM)],
        out_specs=[pl.BlockSpec(memory_space=pltpu.VMEM)] * n_outs,
        out_shape=[jax.ShapeDtypeStruct((8 * SHARE // n_outs, COLS), jnp.bfloat16)] * n_outs,
        scratch_shapes=[pltpu.VMEM((8, SHARE, COLS), jnp.float32), pltpu.SemaphoreType.DMA((8,))],
        compiler_params=pltpu.CompilerParams(vmem_limit_bytes=44 * MIB),
        cost_estimate=pl.CostEstimate(flops=size * 6, bytes_accessed=size * 6, transcendentals=0),
    )(table, master)


def dot(a, b):
    return jnp.dot(a, b, preferred_element_type=jnp.float32)


def pieces(core, mine, near, far, cross):
    def cols(at, c):
        return pl.ds(pl.multiple_of(at + c * COLS, COLS), COLS)

    return [(mine, cols(0, core)), (near, cols(0, 1 - core)), (far, cols(2 * COLS, core)), (cross, cols(2 * COLS, 1 - core))]


def product_kernel(part, keeps, table, mine, near, far, cross, *refs):
    slots, outs, (held, sems) = refs[:4], refs[4:-2], refs[-2:]
    core = table[CORE]
    for n, keep in enumerate(keeps):
        half = core if keep else 1 - core
        for i, slot in enumerate(slots):
            for k in range(4):
                zs = k if part == "y" else i
                depth = pl.ds(pl.multiple_of(table[Z_SLOT + zs] * SHARE, SHARE), SHARE)
                to = held.at[n, i if part == "y" else k, :, depth]
                pltpu.make_async_copy(slot.at[k, half], to, sems.at[n]).start()
    for n, out in enumerate(outs):
        pltpu.make_async_copy(held.at[n], held.at[n], sems.at[n]).wait()
        acts = held[n].reshape(4 * HALF, 4 * SHARE)
        for weight, cols in pieces(core, mine, near, far, cross):
            got = jnp.dot(acts, weight[...], preferred_element_type=jnp.float32).reshape(4, HALF, COLS)
            for ys in range(4):
                out[table[Y_SLOT + ys], :, cols] = got[ys].astype(out.dtype)


def product(part, keeps, table, weights, slots):
    vmem, anywhere = pl.BlockSpec(memory_space=pltpu.VMEM), pl.BlockSpec(memory_space=pl.ANY)
    n = len(keeps)
    types = [jnp.float32 if keep else jnp.bfloat16 for keep in keeps]
    return pl.pallas_call(
        functools.partial(product_kernel, part, keeps),
        in_specs=[pl.BlockSpec(memory_space=pltpu.SMEM)] + [vmem] * 4 + [anywhere] * 4,
        out_specs=[vmem] * n,
        out_shape=[jax.ShapeDtypeStruct((4, HALF, 4 * COLS), t) for t in types],
        scratch_shapes=[pltpu.VMEM((n, 4, HALF, 4 * SHARE), jnp.bfloat16), pltpu.SemaphoreType.DMA((n,))],
        compiler_params=pltpu.CompilerParams(vmem_limit_bytes=20 * MIB),
        cost_estimate=pl.CostEstimate(flops=n * 2 * 512 * 2048 * 1024, bytes_accessed=n * 8 * MIB, transcendentals=0),
    )(table, *weights, *slots)


def spread_kernel(table, owner, own, other, *outs):
    for k, out in enumerate(outs):
        section = owner[table[DEST + k]]
        half = jnp.where(section >= 4, 1, 0)
        far = jnp.where(half == table[XH], 0, 1)
        at = (table[Y] + 8 - section) & 3

        @pl.when(far == table[CORE])
        def _():
            out[...] = own[at]

        @pl.when(far != table[CORE])
        def _():
            out[...] = other[at]


def arrange_kernel(table, *refs):
    parts, out, sems = refs[:4], refs[4], refs[5]
    copies = []
    for dz, part in enumerate(parts):
        at = pl.multiple_of(((table[Z] + 4 - dz) & 3) * (2 * COLS), 2 * COLS)
        copies.append(pltpu.make_async_copy(part, out.at[:, pl.ds(at, 2 * COLS)], sems.at[dz]))
        copies[-1].start()
    for copy in copies:
        copy.wait()


def small_call(kernel, scalars, parts, shapes, out_space, scratch=()):
    smem, vmem = pl.BlockSpec(memory_space=pltpu.SMEM), pl.BlockSpec(memory_space=pltpu.VMEM)
    return pl.pallas_call(
        kernel,
        in_specs=[smem] * len(scalars) + [vmem] * len(parts),
        out_specs=[pl.BlockSpec(memory_space=out_space)] * len(shapes),
        out_shape=[jax.ShapeDtypeStruct(shape, jnp.bfloat16) for shape in shapes],
        scratch_shapes=scratch,
        compiler_params=pltpu.CompilerParams(vmem_limit_bytes=16 * MIB),
        cost_estimate=pl.CostEstimate(flops=0, bytes_accessed=2 * MIB, transcendentals=0),
    )(*scalars, *parts)


def shards(master, activations, owner):
    f32, bf16 = jnp.float32, jnp.bfloat16
    rows = jnp.asarray(np.array([device_row(i) for i in range(N_DEV)], np.int32))
    me = lax.axis_index("group") * 16 + lax.axis_index("tp")
    table = lax.dynamic_index_in_dim(rows, me, 0, keepdims=False)

    same, swapped = refit(table, master, AWAY, 2)
    sent, mine = refit(table, master, HERE, 2)
    near = permute(sent, other_core)
    far = permute(same, other_chip)
    swapped = permute(swapped, other_core)
    slots = gather(activations, same, (near, swapped), far)
    cross = permute(after(swapped, far), other_chip)
    weights = [mine, near, far, cross]
    ready = after(table, *slots["z"][2:], *slots["y"][2:])

    def summed(passed, kept):
        both = kept + permute(passed, other_core).astype(f32)
        return both[..., : 2 * COLS], both[..., 2 * COLS :].astype(bf16)

    def returned(own, came):
        total = (own + came.astype(f32)).astype(bf16)
        got = {}
        for dy in (2, 1, 3, 0):
            got[dy] = permute(total[dy], lambda x, y, z, c: linear(x + 2 * c, y + dy, z, c))
        return jnp.stack([got[dy] for dy in range(4)])

    (passed,) = product("z", [False], ready, weights, slots["z"])
    (kept,) = product("z", [True], ready, weights, slots["z"])
    first = summed(passed, kept)
    ready = after(ready, first[1])
    (passed,) = product("y", [False], ready, weights, slots["y"])
    (kept,) = product("y", [True], ready, weights, slots["y"])
    second = summed(passed, kept)
    came = permute(first[1], other_chip)
    came_last = permute(after(second[1], came), other_chip)
    own = jnp.concatenate([returned(first[0], came), returned(second[0], came_last)], axis=1)
    other = permute(own, other_core)

    picked = small_call(spread_kernel, [table, owner], [own, other], [(256, 2 * COLS)] * 4, pltpu.VMEM)
    got = {}
    for dz in (2, 1, 3, 0):
        got[dz] = permute(picked[dz], lambda x, y, z, c: linear(x ^ c, y, z + dz, x % 2))
    got = [got[dz] for dz in range(4)]
    return small_call(arrange_kernel, [table], got, [(256, 8 * COLS)], pltpu.HBM, [pltpu.SemaphoreType.DMA((4,))])[0]


def solution(mesh):
    in_specs = (P(None, ("group", "tp")), P("group", "tp"), P())
    out_specs = P("group", "tp")
    return jax.shard_map(shards, mesh=mesh, in_specs=in_specs, out_specs=out_specs, check_vma=False)
```

```python
import functools

import jax
import jax.numpy as jnp
import numpy as np
from jax import lax
from jax.experimental import pallas as pl
from jax.experimental.pallas import tpu as pltpu
from jax.sharding import PartitionSpec as P

BLOCK = 128
AXES = ("group", "tp")
N_DEV = 128
SHARE = 512
COLS = 256
ROWS = {"z": 112, "y": 144}
MIB = 1024 * 1024


def coords(i):
    return i // 64 * 2 + i // 8 % 2, i // 16 % 4, i // 2 % 4, i % 2


def linear(x, y, z, core):
    x, y, z = x % 4, y % 4, z % 4
    return x // 2 * 64 + y * 16 + x % 2 * 8 + z * 2 + core


def permute(value, move):
    return lax.ppermute(value, AXES, [(i, move(*coords(i))) for i in range(N_DEV)])


def offset(slot, at, core):
    step = -1 if (at + core) % 2 else 1
    return (0, step, -step, 2)[slot] % 4


def exchange(value, axis, which):
    def move(x, y, z, core):
        at = {"x": x, "y": y, "z": z}
        at[axis] += offset(which, at[axis], core)
        return linear(at["x"], at["y"], at["z"], core)

    return permute(value, move)


def other_core(x, y, z, core):
    return linear(x, y, z, 1 - core)


def other_chip(x, y, z, core):
    return linear(x ^ 1, y, z, core)


def after(value, *others):
    return lax.optimization_barrier((value, *others))[0]


def gather(activations, jobs):
    came = permute(activations, lambda x, y, z, c: linear(x + 2, y, z, c))
    block = jnp.stack([activations, after(came, *jobs[0])])[None]
    blocks = {"z": block[:, :, : ROWS["z"]], "y": block[:, :, ROWS["z"] :]}
    blocks = lax.optimization_barrier(blocks)
    for which in (1, 2):
        blocks = {
            part: jnp.concatenate([v, exchange(v, "y" if part == "z" else "z", which)]) for part, v in blocks.items()
        }
        blocks = after(blocks, *jobs[which])
    slots = {}
    for part, v in blocks.items():
        first = exchange(v, part, 1)
        second = exchange(v, part, 2)
        slots[part] = [v, first, second, exchange(first, part, 2)]
    return slots


AWAY, HERE, CORE, Y_SLOT, Z_SLOT, XH, Y, Z, DEST, WIDTH = 0, 8, 16, 17, 21, 25, 26, 27, 28, 32


def device_row(i):
    x, y, z, core = coords(i)
    xh, xl = x // 2, x % 2

    def chunks(l, c):
        return [l * 8 + (z + dz) % 4 * 2 + c for dz in range(4)]

    row = chunks(1 - xl, core) + chunks(1 - xl, 1 - core) + chunks(xl, 1 - core) + chunks(xl, core) + [core]
    row += [offset(s, y, core) for s in range(4)] + [offset(s, z, core) for s in range(4)]
    row += [xh, y, z] + [(xl ^ core) * 4 + (z + dz) % 4 for dz in range(4)]
    assert len(row) == WIDTH
    return row


def refit_kernel(first, table, master, *refs):
    outs, (held, sems) = refs[:-2], refs[-2:]
    copies = []
    for n in range(8):
        at = pl.multiple_of(table[first + n] * SHARE, SHARE)
        copies.append(pltpu.make_async_copy(master.at[pl.ds(at, SHARE)], held.at[n], sems.at[n]))
        copies[-1].start()
    tiles = SHARE // BLOCK
    places = [(out, at) for out in outs for at in range(0, out.shape[0], SHARE)]
    for n, (out, start) in enumerate(places):
        copies[n].wait()
        amax = jnp.max(jnp.abs(held[n]).reshape(tiles, BLOCK, COLS), axis=1)
        for c in range(COLS // BLOCK):
            cols = slice(c * BLOCK, (c + 1) * BLOCK)
            top = jnp.max(amax[:, cols], axis=1, keepdims=True)
            scales = ((top + 1e-6) / 448.0).astype(jnp.bfloat16).astype(jnp.float32)
            inverses = 1.0 / scales
            for r in range(tiles):
                tile = held[n, r * BLOCK : (r + 1) * BLOCK, cols]
                coded = (tile * inverses[r : r + 1]).astype(jnp.bfloat16)
                value = (coded.astype(jnp.float32) * scales[r : r + 1]).astype(jnp.bfloat16)
                out[start + r * BLOCK : start + (r + 1) * BLOCK, cols] = value


def refit(table, master, first, counts):
    size = 8 * SHARE * COLS
    return pl.pallas_call(
        functools.partial(refit_kernel, first),
        in_specs=[pl.BlockSpec(memory_space=pltpu.SMEM), pl.BlockSpec(memory_space=pltpu.HBM)],
        out_specs=[pl.BlockSpec(memory_space=pltpu.VMEM)] * len(counts),
        out_shape=[jax.ShapeDtypeStruct((n * SHARE, COLS), jnp.bfloat16) for n in counts],
        scratch_shapes=[pltpu.VMEM((8, SHARE, COLS), jnp.float32), pltpu.SemaphoreType.DMA((8,))],
        compiler_params=pltpu.CompilerParams(vmem_limit_bytes=44 * MIB),
        cost_estimate=pl.CostEstimate(flops=size * 6, bytes_accessed=size * 6, transcendentals=0),
    )(table, master)


def dot(a, b):
    return jnp.dot(a, b, preferred_element_type=jnp.float32)


def pieces(core, mine, near, far, more, cross):
    def cols(at, c):
        return pl.ds(pl.multiple_of(at + c * COLS, COLS), COLS)

    return [
        ((mine,), cols(0, core)),
        ((near,), cols(0, 1 - core)),
        ((far, more), cols(2 * COLS, core)),
        ((cross,), cols(2 * COLS, 1 - core)),
    ]


def product_kernel(part, keep, table, mine, near, far, more, cross, *refs):
    slots, (out, held, sem) = refs[:4], refs[4:]
    core = table[CORE]
    half = core if keep else 1 - core
    for i, slot in enumerate(slots):
        for k in range(4):
            zs = k if part == "y" else i
            depth = pl.ds(pl.multiple_of(table[Z_SLOT + zs] * SHARE, SHARE), SHARE)
            to = held.at[i if part == "y" else k, :, depth]
            pltpu.make_async_copy(slot.at[k, half], to, sem).start()
    pltpu.make_async_copy(held, held, sem).wait()
    acts = held[...].reshape(4 * ROWS[part], 4 * SHARE)
    for weights, cols in pieces(core, mine, near, far, more, cross):
        got, at = None, 0
        for weight in weights:
            term = jnp.dot(
                acts[:, at : at + weight.shape[0]], weight[...], preferred_element_type=jnp.float32
            )
            got, at = term if got is None else got + term, at + weight.shape[0]
        got = got.reshape(4, ROWS[part], COLS)
        for ys in range(4):
            out[table[Y_SLOT + ys], :, cols] = got[ys].astype(out.dtype)


def product(part, keep, table, weights, slots):
    vmem, anywhere = pl.BlockSpec(memory_space=pltpu.VMEM), pl.BlockSpec(memory_space=pl.ANY)
    return pl.pallas_call(
        functools.partial(product_kernel, part, keep),
        in_specs=[pl.BlockSpec(memory_space=pltpu.SMEM)] + [vmem] * 5 + [anywhere] * 4,
        out_specs=vmem,
        out_shape=jax.ShapeDtypeStruct((4, ROWS[part], 4 * COLS), jnp.float32 if keep else jnp.bfloat16),
        scratch_shapes=[pltpu.VMEM((4, ROWS[part], 4 * SHARE), jnp.bfloat16), pltpu.SemaphoreType.DMA],
        compiler_params=pltpu.CompilerParams(vmem_limit_bytes=20 * MIB),
        cost_estimate=pl.CostEstimate(flops=2 * 512 * 2048 * 1024, bytes_accessed=8 * MIB, transcendentals=0),
    )(table, *weights, *slots)


def spread_kernel(table, owner, own, other, *outs):
    for k, out in enumerate(outs):
        section = owner[table[DEST + k]]
        half = jnp.where(section >= 4, 1, 0)
        far = jnp.where(half == table[XH], 0, 1)
        at = (table[Y] + 8 - section) & 3

        @pl.when(far == table[CORE])
        def _():
            out[...] = own[at]

        @pl.when(far != table[CORE])
        def _():
            out[...] = other[at]


def arrange_kernel(table, *refs):
    parts, out, sems = refs[:4], refs[4], refs[5]
    copies = []
    for dz, part in enumerate(parts):
        at = pl.multiple_of(((table[Z] + 4 - dz) & 3) * (2 * COLS), 2 * COLS)
        copies.append(pltpu.make_async_copy(part, out.at[:, pl.ds(at, 2 * COLS)], sems.at[dz]))
        copies[-1].start()
    for copy in copies:
        copy.wait()


def small_call(kernel, scalars, parts, shapes, out_space, scratch=()):
    smem, vmem = pl.BlockSpec(memory_space=pltpu.SMEM), pl.BlockSpec(memory_space=pltpu.VMEM)
    return pl.pallas_call(
        kernel,
        in_specs=[smem] * len(scalars) + [vmem] * len(parts),
        out_specs=[pl.BlockSpec(memory_space=out_space)] * len(shapes),
        out_shape=[jax.ShapeDtypeStruct(shape, jnp.bfloat16) for shape in shapes],
        scratch_shapes=scratch,
        compiler_params=pltpu.CompilerParams(vmem_limit_bytes=16 * MIB),
        cost_estimate=pl.CostEstimate(flops=0, bytes_accessed=2 * MIB, transcendentals=0),
    )(*scalars, *parts)


def shards(master, activations, owner):
    f32, bf16 = jnp.float32, jnp.bfloat16
    rows = jnp.asarray(np.array([device_row(i) for i in range(N_DEV)], np.int32))
    me = lax.axis_index("group") * 16 + lax.axis_index("tp")
    table = lax.dynamic_index_in_dim(rows, me, 0, keepdims=False)

    same, more, swapped = refit(table, master, AWAY, (2, 2, 4))
    sent, mine = refit(table, master, HERE, (4, 4))
    near = permute(sent, other_core)
    swapped = permute(swapped, other_core)
    far = permute(same, other_chip)
    more = permute(after(more, far), other_chip)
    cross = permute(after(swapped, more), other_chip)
    weights = [mine, near, far, more, cross]
    slots = gather(activations, [(same,), (far,), (near, swapped, more)])
    ready = after(table, *slots["z"][2:], *slots["y"][1:3])

    def summed(passed, kept):
        both = kept + permute(passed, other_core).astype(f32)
        return both[..., : 2 * COLS], both[..., 2 * COLS :].astype(bf16)

    def returned(own, came):
        total = (own + came.astype(f32)).astype(bf16)
        got = {}
        for dy in (2, 1, 3, 0):
            got[dy] = permute(total[dy], lambda x, y, z, c: linear(x + 2 * c, y + dy, z, c))
        return jnp.stack([got[dy] for dy in range(4)])

    first = summed(*(product("z", keep, ready, weights, slots["z"]) for keep in (False, True)))
    came = permute(first[1], other_chip)
    ready = after(ready, came)
    second = summed(*(product("y", keep, ready, weights, slots["y"]) for keep in (False, True)))
    came_last = permute(second[1], other_chip)
    z_rows = returned(first[0], came)
    own = jnp.concatenate([z_rows, returned(after(second[0], z_rows), came_last)], axis=1)
    other = permute(own, other_core)

    picked = small_call(spread_kernel, [table, owner], [own, other], [(256, 2 * COLS)] * 4, pltpu.VMEM)
    got = {}
    for dz in (2, 1, 3, 0):
        got[dz] = permute(picked[dz], lambda x, y, z, c: linear(x ^ c, y, z + dz, x % 2))
    got = [got[dz] for dz in range(4)]
    return small_call(arrange_kernel, [table], got, [(256, 8 * COLS)], pltpu.HBM, [pltpu.SemaphoreType.DMA((4,))])[0]


def solution(mesh):
    in_specs = (P(None, ("group", "tp")), P("group", "tp"), P())
    out_specs = P("group", "tp")
    return jax.shard_map(shards, mesh=mesh, in_specs=in_specs, out_specs=out_specs, check_vma=False)
```

```python
import functools

import jax
import jax.numpy as jnp
import numpy as np
from jax import lax
from jax.experimental import pallas as pl
from jax.experimental.pallas import tpu as pltpu
from jax.sharding import PartitionSpec as P

BLOCK = 128
AXES = ("group", "tp")
N_DEV = 128
SHARE = 512
COLS = 256
HALF = 128
MIB = 1024 * 1024


def coords(i):
    return i // 64 * 2 + i // 8 % 2, i // 16 % 4, i // 2 % 4, i % 2


def linear(x, y, z, core):
    x, y, z = x % 4, y % 4, z % 4
    return x // 2 * 64 + y * 16 + x % 2 * 8 + z * 2 + core


def permute(value, move):
    return lax.ppermute(value, AXES, [(i, move(*coords(i))) for i in range(N_DEV)])


def offset(slot, at, core):
    step = -1 if (at + core) % 2 else 1
    return (0, step, -step, 2)[slot] % 4


def exchange(value, axis, which):
    def move(x, y, z, core):
        at = {"x": x, "y": y, "z": z}
        at[axis] += offset(which, at[axis], core)
        return linear(at["x"], at["y"], at["z"], core)

    return permute(value, move)


def other_core(x, y, z, core):
    return linear(x, y, z, 1 - core)


def other_chip(x, y, z, core):
    return linear(x ^ 1, y, z, core)


def after(value, *others):
    return lax.optimization_barrier((value, *others))[0]


def gather(activations, first_job, second_job, third_job):
    came = permute(activations, lambda x, y, z, c: linear(x + 2, y, z, c))
    block = jnp.stack([activations, after(came, first_job)])
    blocks = {"z": block[None, :, :HALF], "y": block[None, :, HALF:]}
    blocks = lax.optimization_barrier(blocks)
    for which in (1, 2):
        blocks = {
            part: jnp.concatenate([v, exchange(v, "y" if part == "z" else "z", which)]) for part, v in blocks.items()
        }
        blocks = lax.optimization_barrier(blocks)
    blocks, second_job = lax.optimization_barrier((blocks, second_job))
    slots = {}
    for part, v in blocks.items():
        first = exchange(v, part, 1)
        second = exchange(after(v, third_job), part, 2)
        slots[part] = [v, first, second, exchange(after(first, third_job), part, 2)]
    return slots


AWAY, HERE, CORE, Y_SLOT, Z_SLOT, XH, Y, Z, DEST, WIDTH = 0, 8, 16, 17, 21, 25, 26, 27, 28, 32


def device_row(i):
    x, y, z, core = coords(i)
    xh, xl = x // 2, x % 2

    def chunks(l, c):
        return [l * 8 + (z + dz) % 4 * 2 + c for dz in range(4)]

    row = chunks(1 - xl, core) + chunks(1 - xl, 1 - core) + chunks(xl, 1 - core) + chunks(xl, core) + [core]
    row += [offset(s, y, core) for s in range(4)] + [offset(s, z, core) for s in range(4)]
    row += [xh, y, z] + [(xl ^ core) * 4 + (z + dz) % 4 for dz in range(4)]
    assert len(row) == WIDTH
    return row


def refit_kernel(first, table, master, *refs):
    outs, (held, sems) = refs[:-2], refs[-2:]
    copies = []
    for n in range(8):
        at = pl.multiple_of(table[first + n] * SHARE, SHARE)
        copies.append(pltpu.make_async_copy(master.at[pl.ds(at, SHARE)], held.at[n], sems.at[n]))
        copies[-1].start()
    tiles = SHARE // BLOCK
    for n in range(8):
        out = outs[n * len(outs) // 8]
        start = n * SHARE % out.shape[0]
        copies[n].wait()
        amax = jnp.max(jnp.abs(held[n]).reshape(tiles, BLOCK, COLS), axis=1)
        for c in range(COLS // BLOCK):
            cols = slice(c * BLOCK, (c + 1) * BLOCK)
            top = jnp.max(amax[:, cols], axis=1, keepdims=True)
            scales = ((top + 1e-6) / 448.0).astype(jnp.bfloat16).astype(jnp.float32)
            inverses = 1.0 / scales
            for r in range(tiles):
                tile = held[n, r * BLOCK : (r + 1) * BLOCK, cols]
                coded = (tile * inverses[r : r + 1]).astype(jnp.bfloat16)
                value = (coded.astype(jnp.float32) * scales[r : r + 1]).astype(jnp.bfloat16)
                out[start + r * BLOCK : start + (r + 1) * BLOCK, cols] = value


def refit(table, master, first, n_outs):
    size = 8 * SHARE * COLS
    return pl.pallas_call(
        functools.partial(refit_kernel, first),
        in_specs=[pl.BlockSpec(memory_space=pltpu.SMEM), pl.BlockSpec(memory_space=pltpu.HBM)],
        out_specs=[pl.BlockSpec(memory_space=pltpu.VMEM)] * n_outs,
        out_shape=[jax.ShapeDtypeStruct((8 * SHARE // n_outs, COLS), jnp.bfloat16)] * n_outs,
        scratch_shapes=[pltpu.VMEM((8, SHARE, COLS), jnp.float32), pltpu.SemaphoreType.DMA((8,))],
        compiler_params=pltpu.CompilerParams(vmem_limit_bytes=44 * MIB),
        cost_estimate=pl.CostEstimate(flops=size * 6, bytes_accessed=size * 6, transcendentals=0),
    )(table, master)


def dot(a, b):
    return jnp.dot(a, b, preferred_element_type=jnp.float32)


def pieces(core, mine, near, far, cross):
    def cols(at, c):
        return pl.ds(pl.multiple_of(at + c * COLS, COLS), COLS)

    return [(mine, cols(0, core)), (near, cols(0, 1 - core)), (far, cols(2 * COLS, core)), (cross, cols(2 * COLS, 1 - core))]


def product_kernel(part, keep, table, mine, near, far, cross, *refs):
    slots, out = refs[:4], refs[4]
    core = table[CORE]
    half = core if keep else 1 - core
    weights = pieces(core, mine, near, far, cross)
    chunks = []
    for n in range(4):
        if part == "y":
            rows = jnp.concatenate([slot[n, half] for slot in slots])
        else:
            rows = slots[n][:, half].reshape(4 * HALF, SHARE)
        chunks.append((rows, pl.ds(pl.multiple_of(table[Z_SLOT + n] * SHARE, SHARE), SHARE)))
    for weight, cols in weights:
        got = None
        for rows, depth in chunks:
            term = jnp.dot(rows, weight[depth, :], preferred_element_type=jnp.float32)
            got = term if got is None else got + term
        got = got.reshape(4, HALF, COLS)
        for ys in range(4):
            out[table[Y_SLOT + ys], :, cols] = got[ys].astype(out.dtype)


def product(part, keep, table, weights, slots):
    vmem = pl.BlockSpec(memory_space=pltpu.VMEM)
    return pl.pallas_call(
        functools.partial(product_kernel, part, keep),
        in_specs=[pl.BlockSpec(memory_space=pltpu.SMEM)] + [vmem] * 8,
        out_specs=vmem,
        out_shape=jax.ShapeDtypeStruct((4, HALF, 4 * COLS), jnp.float32 if keep else jnp.bfloat16),
        compiler_params=pltpu.CompilerParams(vmem_limit_bytes=24 * MIB),
        cost_estimate=pl.CostEstimate(flops=2 * 512 * 2048 * 1024, bytes_accessed=8 * MIB, transcendentals=0),
    )(table, *weights, *slots)


def spread_kernel(table, owner, own, other, *outs):
    for k, out in enumerate(outs):
        section = owner[table[DEST + k]]
        half = jnp.where(section >= 4, 1, 0)
        far = jnp.where(half == table[XH], 0, 1)
        at = (table[Y] + 8 - section) & 3

        @pl.when(far == table[CORE])
        def _():
            out[...] = own[at]

        @pl.when(far != table[CORE])
        def _():
            out[...] = other[at]


def arrange_kernel(table, *refs):
    parts, out, sems = refs[:8], refs[8], refs[9]
    copies = []
    for i, part in enumerate(parts):
        rows, dz = i // 4, i % 4
        at = pl.multiple_of(((table[Z] + 4 - dz) & 3) * (2 * COLS), 2 * COLS)
        to = out.at[pl.ds(rows * HALF, HALF), pl.ds(at, 2 * COLS)]
        copies.append(pltpu.make_async_copy(part, to, sems.at[i]))
        copies[-1].start()
    for copy in copies:
        copy.wait()


def small_call(kernel, scalars, parts, shapes, out_space, scratch=()):
    smem, vmem = pl.BlockSpec(memory_space=pltpu.SMEM), pl.BlockSpec(memory_space=pltpu.VMEM)
    return pl.pallas_call(
        kernel,
        in_specs=[smem] * len(scalars) + [vmem] * len(parts),
        out_specs=[pl.BlockSpec(memory_space=out_space)] * len(shapes),
        out_shape=[jax.ShapeDtypeStruct(shape, jnp.bfloat16) for shape in shapes],
        scratch_shapes=scratch,
        compiler_params=pltpu.CompilerParams(vmem_limit_bytes=16 * MIB),
        cost_estimate=pl.CostEstimate(flops=0, bytes_accessed=2 * MIB, transcendentals=0),
    )(*scalars, *parts)


def shards(master, activations, owner):
    f32, bf16 = jnp.float32, jnp.bfloat16
    rows = jnp.asarray(np.array([device_row(i) for i in range(N_DEV)], np.int32))
    me = lax.axis_index("group") * 16 + lax.axis_index("tp")
    table = lax.dynamic_index_in_dim(rows, me, 0, keepdims=False)

    same, swapped = refit(table, master, AWAY, 2)
    sent, mine = refit(table, master, HERE, 2)
    near = permute(sent, other_core)
    far = permute(same, other_chip)
    swapped = permute(swapped, other_core)
    slots = gather(activations, same, (near, swapped), far)
    cross = permute(after(swapped, far), other_chip)
    weights = [mine, near, far, cross]
    ready = after(table, slots["z"][3], slots["y"][3])

    def chain(part):
        passed = product(part, False, ready, weights, slots[part])
        kept = product(part, True, ready, weights, slots[part])
        both = kept + permute(passed, other_core).astype(f32)
        came = permute(both[..., 2 * COLS :].astype(bf16), other_chip)
        total = (both[..., : 2 * COLS] + came.astype(f32)).astype(bf16)
        got = {}
        for dy in (2, 1, 3, 0):
            got[dy] = permute(total[dy], lambda x, y, z, c: linear(x + 2 * c, y + dy, z, c))
        own = jnp.stack([got[dy] for dy in range(4)])
        other = permute(own, other_core)
        picked = small_call(spread_kernel, [table, owner], [own, other], [(HALF, 2 * COLS)] * 4, pltpu.VMEM)
        got = {}
        for dz in (2, 1, 3, 0):
            got[dz] = permute(picked[dz], lambda x, y, z, c: linear(x ^ c, y, z + dz, x % 2))
        return [got[dz] for dz in range(4)]

    blocks = chain("y")
    blocks = chain("z") + blocks
    return small_call(
        arrange_kernel, [table], blocks, [(256, 8 * COLS)], pltpu.HBM, [pltpu.SemaphoreType.DMA((8,))]
    )[0]


def solution(mesh):
    in_specs = (P(None, ("group", "tp")), P("group", "tp"), P())
    out_specs = P("group", "tp")
    return jax.shard_map(shards, mesh=mesh, in_specs=in_specs, out_specs=out_specs, check_vma=False)
```

```python
import functools

import jax
import jax.numpy as jnp
import numpy as np
from jax import lax
from jax.experimental import pallas as pl
from jax.experimental.pallas import tpu as pltpu
from jax.sharding import PartitionSpec as P

BLOCK = 128
AXES = ("group", "tp")
N_DEV = 128
SHARE = 512
COLS = 256
HALF = 128
MIB = 1024 * 1024


def coords(i):
    return i // 64 * 2 + i // 8 % 2, i // 16 % 4, i // 2 % 4, i % 2


def linear(x, y, z, core):
    x, y, z = x % 4, y % 4, z % 4
    return x // 2 * 64 + y * 16 + x % 2 * 8 + z * 2 + core


def permute(value, move):
    return lax.ppermute(value, AXES, [(i, move(*coords(i))) for i in range(N_DEV)])


def offset(slot, at, core):
    step = -1 if (at + core) % 2 else 1
    return (0, step, -step, 2)[slot] % 4


def exchange(value, axis, which):
    def move(x, y, z, core):
        at = {"x": x, "y": y, "z": z}
        at[axis] += offset(which, at[axis], core)
        return linear(at["x"], at["y"], at["z"], core)

    return permute(value, move)


def other_core(x, y, z, core):
    return linear(x, y, z, 1 - core)


def other_chip(x, y, z, core):
    return linear(x ^ 1, y, z, core)


def after(value, *others):
    return lax.optimization_barrier((value, *others))[0]


def gather(activations, first_job, second_job, third_job):
    came = permute(activations, lambda x, y, z, c: linear(x + 2, y, z, c))
    block = jnp.stack([activations, after(came, first_job)])
    blocks = {"z": block[None, :, :HALF], "y": block[None, :, HALF:]}
    blocks = lax.optimization_barrier(blocks)
    for which in (1, 2):
        blocks = {
            part: jnp.concatenate([v, exchange(v, "y" if part == "z" else "z", which)]) for part, v in blocks.items()
        }
        blocks = lax.optimization_barrier(blocks)
    blocks, second_job = lax.optimization_barrier((blocks, second_job))
    slots = {}
    for part, v in blocks.items():
        first = exchange(v, part, 1)
        second = exchange(after(v, third_job), part, 2)
        slots[part] = [v, first, second, exchange(after(first, third_job), part, 2)]
    return slots


AWAY, HERE, CORE, Y_SLOT, Z_SLOT, XH, Y, Z, DEST, WIDTH = 0, 8, 16, 17, 21, 25, 26, 27, 28, 32


def device_row(i):
    x, y, z, core = coords(i)
    xh, xl = x // 2, x % 2

    def chunks(l, c):
        return [l * 8 + (z + dz) % 4 * 2 + c for dz in range(4)]

    row = chunks(1 - xl, core) + chunks(1 - xl, 1 - core) + chunks(xl, 1 - core) + chunks(xl, core) + [core]
    row += [offset(s, y, core) for s in range(4)] + [offset(s, z, core) for s in range(4)]
    row += [xh, y, z] + [(xl ^ core) * 4 + (z + dz) % 4 for dz in range(4)]
    assert len(row) == WIDTH
    return row


def refit_kernel(first, table, master, *refs):
    outs, (held, sems) = refs[:-2], refs[-2:]
    copies = []
    for n in range(8):
        at = pl.multiple_of(table[first + n] * SHARE, SHARE)
        copies.append(pltpu.make_async_copy(master.at[pl.ds(at, SHARE)], held.at[n], sems.at[n]))
        copies[-1].start()
    tiles = SHARE // BLOCK
    for n in range(8):
        out = outs[n * len(outs) // 8]
        start = n * SHARE % out.shape[0]
        copies[n].wait()
        amax = jnp.max(jnp.abs(held[n]).reshape(tiles, BLOCK, COLS), axis=1)
        for c in range(COLS // BLOCK):
            cols = slice(c * BLOCK, (c + 1) * BLOCK)
            top = jnp.max(amax[:, cols], axis=1, keepdims=True)
            scales = ((top + 1e-6) / 448.0).astype(jnp.bfloat16).astype(jnp.float32)
            inverses = 1.0 / scales
            for r in range(tiles):
                tile = held[n, r * BLOCK : (r + 1) * BLOCK, cols]
                coded = (tile * inverses[r : r + 1]).astype(jnp.bfloat16)
                value = (coded.astype(jnp.float32) * scales[r : r + 1]).astype(jnp.bfloat16)
                out[start + r * BLOCK : start + (r + 1) * BLOCK, cols] = value


def refit(table, master, first, n_outs):
    size = 8 * SHARE * COLS
    return pl.pallas_call(
        functools.partial(refit_kernel, first),
        in_specs=[pl.BlockSpec(memory_space=pltpu.SMEM), pl.BlockSpec(memory_space=pltpu.HBM)],
        out_specs=[pl.BlockSpec(memory_space=pltpu.VMEM)] * n_outs,
        out_shape=[jax.ShapeDtypeStruct((8 * SHARE // n_outs, COLS), jnp.bfloat16)] * n_outs,
        scratch_shapes=[pltpu.VMEM((8, SHARE, COLS), jnp.float32), pltpu.SemaphoreType.DMA((8,))],
        compiler_params=pltpu.CompilerParams(vmem_limit_bytes=44 * MIB),
        cost_estimate=pl.CostEstimate(flops=size * 6, bytes_accessed=size * 6, transcendentals=0),
    )(table, master)


def dot(a, b):
    return jnp.dot(a, b, preferred_element_type=jnp.float32)


def pieces(core, mine, near, far, cross):
    def cols(at, c):
        return pl.ds(pl.multiple_of(at + c * COLS, COLS), COLS)

    return [(mine, cols(0, core)), (near, cols(0, 1 - core)), (far, cols(2 * COLS, core)), (cross, cols(2 * COLS, 1 - core))]


def dot(a, b):
    return jnp.dot(a, b, preferred_element_type=jnp.float32)


def depth_of(table, n):
    return pl.ds(pl.multiple_of(table[Z_SLOT + n] * SHARE, SHARE), SHARE)


EARLY, LATE = (0, 1, 2), 3


def early_kernel(table, mine, near, far, *refs):
    z_slots, y_slots, (z_out, y_out) = refs[:3], refs[3:6], refs[6:]
    for piece, weight in enumerate((mine, near, far)):
        for half in range(2):
            got = None
            for n, slot in zip(EARLY, z_slots):
                term = dot(slot[:, half].reshape(4 * HALF, SHARE), weight[depth_of(table, n), :])
                got = term if got is None else got + term
            z_out[piece, half] = got
            got = None
            for n in range(4):
                term = dot(jnp.concatenate([slot[n, half] for slot in y_slots]), weight[depth_of(table, n), :])
                got = term if got is None else got + term
            y_out[piece, half] = got


def early_product(table, weights, slots):
    vmem = pl.BlockSpec(memory_space=pltpu.VMEM)
    parts = [slots[part][n] for part in "zy" for n in EARLY]
    shapes = [(3, 2, 4 * HALF, COLS), (3, 2, 3 * HALF, COLS)]
    return pl.pallas_call(
        early_kernel,
        in_specs=[pl.BlockSpec(memory_space=pltpu.SMEM)] + [vmem] * 9,
        out_specs=[vmem] * 2,
        out_shape=[jax.ShapeDtypeStruct(shape, jnp.float32) for shape in shapes],
        compiler_params=pltpu.CompilerParams(vmem_limit_bytes=24 * MIB),
        cost_estimate=pl.CostEstimate(flops=5 * 2**30, bytes_accessed=16 * MIB, transcendentals=0),
    )(table, *weights[:3], *parts)


def product_kernel(part, keep, table, mine, near, far, cross, *refs):
    slots, early, out = refs[:4], refs[4], refs[5]
    core = table[CORE]
    half = core if keep else 1 - core

    def rows(n, some):
        if part == "y":
            return jnp.concatenate([slots[i][n, half] for i in some])
        return slots[n][:, half].reshape(4 * HALF, SHARE)

    for piece, (weight, cols) in enumerate(pieces(core, mine, near, far, cross)):
        last = piece == 3
        some = EARLY + (LATE,) if last else (LATE,)
        got = None
        for n in range(4) if part == "y" else some:
            term = dot(rows(n, some), weight[depth_of(table, n), :])
            got = term if got is None else got + term
        if not last and part == "z":
            got += early[piece, half]
        for ys in range(4):
            if last or part == "z":
                value = got[ys * HALF : (ys + 1) * HALF]
            elif ys == LATE:
                value = got
            else:
                value = early[piece, half, pl.ds(EARLY.index(ys) * HALF, HALF)]
            out[table[Y_SLOT + ys], :, cols] = value.astype(out.dtype)


def product(part, keep, table, weights, slots, early):
    vmem = pl.BlockSpec(memory_space=pltpu.VMEM)
    return pl.pallas_call(
        functools.partial(product_kernel, part, keep),
        in_specs=[pl.BlockSpec(memory_space=pltpu.SMEM)] + [vmem] * 9,
        out_specs=vmem,
        out_shape=jax.ShapeDtypeStruct((4, HALF, 4 * COLS), jnp.float32 if keep else jnp.bfloat16),
        compiler_params=pltpu.CompilerParams(vmem_limit_bytes=24 * MIB),
        cost_estimate=pl.CostEstimate(flops=2**30, bytes_accessed=8 * MIB, transcendentals=0),
    )(table, *weights, *slots, early)


def spread_kernel(table, owner, own, other, *outs):
    for k, out in enumerate(outs):
        section = owner[table[DEST + k]]
        half = jnp.where(section >= 4, 1, 0)
        far = jnp.where(half == table[XH], 0, 1)
        at = (table[Y] + 8 - section) & 3

        @pl.when(far == table[CORE])
        def _():
            out[...] = own[at]

        @pl.when(far != table[CORE])
        def _():
            out[...] = other[at]


def arrange_kernel(table, *refs):
    parts, out, sems = refs[:8], refs[8], refs[9]
    copies = []
    for i, part in enumerate(parts):
        rows, dz = i // 4, i % 4
        at = pl.multiple_of(((table[Z] + 4 - dz) & 3) * (2 * COLS), 2 * COLS)
        to = out.at[pl.ds(rows * HALF, HALF), pl.ds(at, 2 * COLS)]
        copies.append(pltpu.make_async_copy(part, to, sems.at[i]))
        copies[-1].start()
    for copy in copies:
        copy.wait()


def small_call(kernel, scalars, parts, shapes, out_space, scratch=()):
    smem, vmem = pl.BlockSpec(memory_space=pltpu.SMEM), pl.BlockSpec(memory_space=pltpu.VMEM)
    return pl.pallas_call(
        kernel,
        in_specs=[smem] * len(scalars) + [vmem] * len(parts),
        out_specs=[pl.BlockSpec(memory_space=out_space)] * len(shapes),
        out_shape=[jax.ShapeDtypeStruct(shape, jnp.bfloat16) for shape in shapes],
        scratch_shapes=scratch,
        compiler_params=pltpu.CompilerParams(vmem_limit_bytes=16 * MIB),
        cost_estimate=pl.CostEstimate(flops=0, bytes_accessed=2 * MIB, transcendentals=0),
    )(*scalars, *parts)


def shards(master, activations, owner):
    f32, bf16 = jnp.float32, jnp.bfloat16
    rows = jnp.asarray(np.array([device_row(i) for i in range(N_DEV)], np.int32))
    me = lax.axis_index("group") * 16 + lax.axis_index("tp")
    table = lax.dynamic_index_in_dim(rows, me, 0, keepdims=False)

    same, swapped = refit(table, master, AWAY, 2)
    sent, mine = refit(table, master, HERE, 2)
    near = permute(sent, other_core)
    far = permute(same, other_chip)
    swapped = permute(swapped, other_core)
    slots = gather(activations, same, (near, swapped), far)
    cross = permute(after(swapped, far), other_chip)
    weights = [mine, near, far, cross]
    early = dict(zip("zy", early_product(table, weights, slots)))
    ready = after(table, slots["z"][LATE], slots["y"][LATE])

    def chain(part):
        passed = product(part, False, ready, weights, slots[part], early[part])
        kept = product(part, True, ready, weights, slots[part], early[part])
        both = kept + permute(passed, other_core).astype(f32)
        came = permute(both[..., 2 * COLS :].astype(bf16), other_chip)
        total = (both[..., : 2 * COLS] + came.astype(f32)).astype(bf16)
        got = {}
        for dy in (2, 1, 3, 0):
            got[dy] = permute(total[dy], lambda x, y, z, c: linear(x + 2 * c, y + dy, z, c))
        own = jnp.stack([got[dy] for dy in range(4)])
        other = permute(own, other_core)
        picked = small_call(spread_kernel, [table, owner], [own, other], [(HALF, 2 * COLS)] * 4, pltpu.VMEM)
        got = {}
        for dz in (2, 1, 3, 0):
            got[dz] = permute(picked[dz], lambda x, y, z, c: linear(x ^ c, y, z + dz, x % 2))
        return [got[dz] for dz in range(4)]

    blocks = chain("y")
    blocks = chain("z") + blocks
    return small_call(
        arrange_kernel, [table], blocks, [(256, 8 * COLS)], pltpu.HBM, [pltpu.SemaphoreType.DMA((8,))]
    )[0]


def solution(mesh):
    in_specs = (P(None, ("group", "tp")), P("group", "tp"), P())
    out_specs = P("group", "tp")
    return jax.shard_map(shards, mesh=mesh, in_specs=in_specs, out_specs=out_specs, check_vma=False)
```

```python
import functools

import jax
import jax.numpy as jnp
import numpy as np
from jax import lax
from jax.experimental import pallas as pl
from jax.experimental.pallas import tpu as pltpu
from jax.sharding import PartitionSpec as P

BLOCK = 128
AXES = ("group", "tp")
N_DEV = 128
SHARE = 512
COLS = 256
HALF = 128
MIB = 1024 * 1024


def coords(i):
    return i // 64 * 2 + i // 8 % 2, i // 16 % 4, i // 2 % 4, i % 2


def linear(x, y, z, core):
    x, y, z = x % 4, y % 4, z % 4
    return x // 2 * 64 + y * 16 + x % 2 * 8 + z * 2 + core


def permute(value, move):
    return lax.ppermute(value, AXES, [(i, move(*coords(i))) for i in range(N_DEV)])


def offset(slot, at, core):
    step = -1 if (at + core) % 2 else 1
    return (0, step, -step, 2)[slot] % 4


def exchange(value, axis, which):
    def move(x, y, z, core):
        at = {"x": x, "y": y, "z": z}
        at[axis] += offset(which, at[axis], core)
        return linear(at["x"], at["y"], at["z"], core)

    return permute(value, move)


def other_core(x, y, z, core):
    return linear(x, y, z, 1 - core)


def other_chip(x, y, z, core):
    return linear(x ^ 1, y, z, core)


def after(value, *others):
    return lax.optimization_barrier((value, *others))[0]


def gather(activations, first_job, second_job, third_job):
    came = permute(activations, lambda x, y, z, c: linear(x + 2, y, z, c))
    block = jnp.stack([activations, after(came, first_job)])
    blocks = {"z": block[None, :, :HALF], "y": block[None, :, HALF:]}
    blocks = lax.optimization_barrier(blocks)
    for which in (1, 2):
        blocks = {
            part: jnp.concatenate([v, exchange(v, "y" if part == "z" else "z", which)]) for part, v in blocks.items()
        }
        blocks = lax.optimization_barrier(blocks)
    blocks, second_job = lax.optimization_barrier((blocks, second_job))
    slots = {}
    for part, v in blocks.items():
        first = exchange(v, part, 1)
        second = exchange(after(v, third_job), part, 2)
        slots[part] = [v, first, second, exchange(after(first, third_job), part, 2)]
    return slots


AWAY, HERE, CORE, Y_SLOT, Z_SLOT, XH, Y, Z, DEST, WIDTH = 0, 8, 16, 17, 21, 25, 26, 27, 28, 32


def device_row(i):
    x, y, z, core = coords(i)
    xh, xl = x // 2, x % 2

    def chunks(l, c):
        return [l * 8 + (z + dz) % 4 * 2 + c for dz in range(4)]

    row = chunks(1 - xl, core) + chunks(1 - xl, 1 - core) + chunks(xl, 1 - core) + chunks(xl, core) + [core]
    row += [offset(s, y, core) for s in range(4)] + [offset(s, z, core) for s in range(4)]
    row += [xh, y, z] + [(xl ^ core) * 4 + (z + dz) % 4 for dz in range(4)]
    assert len(row) == WIDTH
    return row


def refit_kernel(first, table, master, *refs):
    outs, (held, sems) = refs[:-2], refs[-2:]
    copies = []
    for n in range(8):
        at = pl.multiple_of(table[first + n] * SHARE, SHARE)
        copies.append(pltpu.make_async_copy(master.at[pl.ds(at, SHARE)], held.at[n], sems.at[n]))
        copies[-1].start()
    tiles = SHARE // BLOCK
    for n in range(8):
        out = outs[n * len(outs) // 8]
        start = n * SHARE % out.shape[0]
        copies[n].wait()
        amax = jnp.max(jnp.abs(held[n]).reshape(tiles, BLOCK, COLS), axis=1)
        for c in range(COLS // BLOCK):
            cols = slice(c * BLOCK, (c + 1) * BLOCK)
            top = jnp.max(amax[:, cols], axis=1, keepdims=True)
            scales = ((top + 1e-6) / 448.0).astype(jnp.bfloat16).astype(jnp.float32)
            inverses = 1.0 / scales
            for r in range(tiles):
                tile = held[n, r * BLOCK : (r + 1) * BLOCK, cols]
                coded = (tile * inverses[r : r + 1]).astype(jnp.bfloat16)
                value = (coded.astype(jnp.float32) * scales[r : r + 1]).astype(jnp.bfloat16)
                out[start + r * BLOCK : start + (r + 1) * BLOCK, cols] = value


def refit(table, master, first, n_outs):
    size = 8 * SHARE * COLS
    return pl.pallas_call(
        functools.partial(refit_kernel, first),
        in_specs=[pl.BlockSpec(memory_space=pltpu.SMEM), pl.BlockSpec(memory_space=pltpu.HBM)],
        out_specs=[pl.BlockSpec(memory_space=pltpu.VMEM)] * n_outs,
        out_shape=[jax.ShapeDtypeStruct((8 * SHARE // n_outs, COLS), jnp.bfloat16)] * n_outs,
        scratch_shapes=[pltpu.VMEM((8, SHARE, COLS), jnp.float32), pltpu.SemaphoreType.DMA((8,))],
        compiler_params=pltpu.CompilerParams(vmem_limit_bytes=44 * MIB),
        cost_estimate=pl.CostEstimate(flops=size * 6, bytes_accessed=size * 6, transcendentals=0),
    )(table, master)


def dot(a, b):
    return jnp.dot(a, b, preferred_element_type=jnp.float32)


def pieces(core, mine, near, far, cross):
    def cols(at, c):
        return pl.ds(pl.multiple_of(at + c * COLS, COLS), COLS)

    return [(mine, cols(0, core)), (near, cols(0, 1 - core)), (far, cols(2 * COLS, core)), (cross, cols(2 * COLS, 1 - core))]


def dot(a, b):
    return jnp.dot(a, b, preferred_element_type=jnp.float32)


def depth_of(table, n):
    return pl.ds(pl.multiple_of(table[Z_SLOT + n] * SHARE, SHARE), SHARE)


EARLY, LATE = (0, 1, 2), 3


def early_kernel(count, table, *refs):
    weights, z_slots, y_slots, (z_out, y_out) = refs[:count], refs[count : count + 3], refs[count + 3 : -2], refs[-2:]
    for piece, weight in enumerate(weights):
        for half in range(2):
            got = None
            for n, slot in zip(EARLY, z_slots):
                term = dot(slot[:, half].reshape(4 * HALF, SHARE), weight[depth_of(table, n), :])
                got = term if got is None else got + term
            z_out[piece, half] = got
            got = None
            for n in range(4):
                term = dot(jnp.concatenate([slot[n, half] for slot in y_slots]), weight[depth_of(table, n), :])
                got = term if got is None else got + term
            y_out[piece, half] = got


def early_product(table, weights, slots):
    vmem = pl.BlockSpec(memory_space=pltpu.VMEM)
    parts = [slots[part][n] for part in "zy" for n in EARLY]
    count = len(weights)
    shapes = [(count, 2, 4 * HALF, COLS), (count, 2, 3 * HALF, COLS)]
    return pl.pallas_call(
        functools.partial(early_kernel, count),
        in_specs=[pl.BlockSpec(memory_space=pltpu.SMEM)] + [vmem] * (count + 6),
        out_specs=[vmem] * 2,
        out_shape=[jax.ShapeDtypeStruct(shape, jnp.float32) for shape in shapes],
        compiler_params=pltpu.CompilerParams(vmem_limit_bytes=24 * MIB),
        cost_estimate=pl.CostEstimate(flops=count * 2**30, bytes_accessed=16 * MIB, transcendentals=0),
    )(table, *weights, *parts)


def product_kernel(part, keep, table, mine, near, far, cross, *refs):
    slot, first, last, out = refs
    core = table[CORE]
    half = core if keep else 1 - core
    for piece, (weight, cols) in enumerate(pieces(core, mine, near, far, cross)):
        early = first.at[piece, half] if piece < 3 else last.at[0, half]
        if part == "z":
            got = early[...] + dot(slot[:, half].reshape(4 * HALF, SHARE), weight[depth_of(table, LATE), :])
            values = [got[ys * HALF : (ys + 1) * HALF] for ys in range(4)]
        else:
            got = None
            for n in range(4):
                term = dot(slot[n, half], weight[depth_of(table, n), :])
                got = term if got is None else got + term
            values = [early[pl.ds(n * HALF, HALF)] for n in range(3)] + [got]
        for ys in range(4):
            out[table[Y_SLOT + ys], :, cols] = values[ys].astype(out.dtype)


def product(part, keep, table, weights, slot, early):
    vmem = pl.BlockSpec(memory_space=pltpu.VMEM)
    return pl.pallas_call(
        functools.partial(product_kernel, part, keep),
        in_specs=[pl.BlockSpec(memory_space=pltpu.SMEM)] + [vmem] * 7,
        out_specs=vmem,
        out_shape=jax.ShapeDtypeStruct((4, HALF, 4 * COLS), jnp.float32 if keep else jnp.bfloat16),
        compiler_params=pltpu.CompilerParams(vmem_limit_bytes=24 * MIB),
        cost_estimate=pl.CostEstimate(flops=2**29, bytes_accessed=8 * MIB, transcendentals=0),
    )(table, *weights, slot, *early)


def spread_kernel(table, owner, own, other, *outs):
    for k, out in enumerate(outs):
        section = owner[table[DEST + k]]
        half = jnp.where(section >= 4, 1, 0)
        far = jnp.where(half == table[XH], 0, 1)
        at = (table[Y] + 8 - section) & 3

        @pl.when(far == table[CORE])
        def _():
            out[...] = own[at]

        @pl.when(far != table[CORE])
        def _():
            out[...] = other[at]


def arrange_kernel(table, *refs):
    parts, out, sems = refs[:8], refs[8], refs[9]
    copies = []
    for i, part in enumerate(parts):
        rows, dz = i // 4, i % 4
        at = pl.multiple_of(((table[Z] + 4 - dz) & 3) * (2 * COLS), 2 * COLS)
        to = out.at[pl.ds(rows * HALF, HALF), pl.ds(at, 2 * COLS)]
        copies.append(pltpu.make_async_copy(part, to, sems.at[i]))
        copies[-1].start()
    for copy in copies:
        copy.wait()


def small_call(kernel, scalars, parts, shapes, out_space, scratch=()):
    smem, vmem = pl.BlockSpec(memory_space=pltpu.SMEM), pl.BlockSpec(memory_space=pltpu.VMEM)
    return pl.pallas_call(
        kernel,
        in_specs=[smem] * len(scalars) + [vmem] * len(parts),
        out_specs=[pl.BlockSpec(memory_space=out_space)] * len(shapes),
        out_shape=[jax.ShapeDtypeStruct(shape, jnp.bfloat16) for shape in shapes],
        scratch_shapes=scratch,
        compiler_params=pltpu.CompilerParams(vmem_limit_bytes=16 * MIB),
        cost_estimate=pl.CostEstimate(flops=0, bytes_accessed=2 * MIB, transcendentals=0),
    )(*scalars, *parts)


def shards(master, activations, owner):
    f32, bf16 = jnp.float32, jnp.bfloat16
    rows = jnp.asarray(np.array([device_row(i) for i in range(N_DEV)], np.int32))
    me = lax.axis_index("group") * 16 + lax.axis_index("tp")
    table = lax.dynamic_index_in_dim(rows, me, 0, keepdims=False)

    same, swapped = refit(table, master, AWAY, 2)
    sent, mine = refit(table, master, HERE, 2)
    near = permute(sent, other_core)
    far = permute(same, other_chip)
    swapped = permute(swapped, other_core)
    slots = gather(activations, same, (near, swapped), far)
    cross = permute(after(swapped, far), other_chip)
    weights = [mine, near, far, cross]
    early = early_product(table, weights[:3], slots)
    early = dict(zip("zy", zip(early, early_product(after(table, *early), weights[3:], slots))))
    ready = after(table, slots["z"][LATE], slots["y"][LATE])

    def chain(part):
        passed = product(part, False, ready, weights, slots[part][LATE], early[part])
        kept = product(part, True, ready, weights, slots[part][LATE], early[part])
        both = kept + permute(passed, other_core).astype(f32)
        came = permute(both[..., 2 * COLS :].astype(bf16), other_chip)
        total = (both[..., : 2 * COLS] + came.astype(f32)).astype(bf16)
        got = {}
        for dy in (2, 1, 3, 0):
            got[dy] = permute(total[dy], lambda x, y, z, c: linear(x + 2 * c, y + dy, z, c))
        own = jnp.stack([got[dy] for dy in range(4)])
        other = permute(own, other_core)
        picked = small_call(spread_kernel, [table, owner], [own, other], [(HALF, 2 * COLS)] * 4, pltpu.VMEM)
        got = {}
        for dz in (2, 1, 3, 0):
            got[dz] = permute(picked[dz], lambda x, y, z, c: linear(x ^ c, y, z + dz, x % 2))
        return [got[dz] for dz in range(4)]

    blocks = chain("y")
    blocks = chain("z") + blocks
    return small_call(
        arrange_kernel, [table], blocks, [(256, 8 * COLS)], pltpu.HBM, [pltpu.SemaphoreType.DMA((8,))]
    )[0]


def solution(mesh):
    in_specs = (P(None, ("group", "tp")), P("group", "tp"), P())
    out_specs = P("group", "tp")
    return jax.shard_map(shards, mesh=mesh, in_specs=in_specs, out_specs=out_specs, check_vma=False)
```

```python
import functools

import jax
import jax.numpy as jnp
import numpy as np
from jax import lax
from jax.experimental import pallas as pl
from jax.experimental.pallas import tpu as pltpu
from jax.sharding import PartitionSpec as P

BLOCK = 128
AXES = ("group", "tp")
N_DEV = 128
SHARE = 512
COLS = 256
HALF = 128
MIB = 1024 * 1024


def coords(i):
    return i // 64 * 2 + i // 8 % 2, i // 16 % 4, i // 2 % 4, i % 2


def linear(x, y, z, core):
    x, y, z = x % 4, y % 4, z % 4
    return x // 2 * 64 + y * 16 + x % 2 * 8 + z * 2 + core


def permute(value, move):
    return lax.ppermute(value, AXES, [(i, move(*coords(i))) for i in range(N_DEV)])


def offset(slot, at, core):
    step = -1 if (at + core) % 2 else 1
    return (0, step, -step, 2)[slot] % 4


def exchange(value, axis, which):
    def move(x, y, z, core):
        at = {"x": x, "y": y, "z": z}
        at[axis] += offset(which, at[axis], core)
        return linear(at["x"], at["y"], at["z"], core)

    return permute(value, move)


def other_core(x, y, z, core):
    return linear(x, y, z, 1 - core)


def other_chip(x, y, z, core):
    return linear(x ^ 1, y, z, core)


def after(value, *others):
    return lax.optimization_barrier((value, *others))[0]


def gather(activations, first_job, second_job, third_job):
    came = permute(activations, lambda x, y, z, c: linear(x + 2, y, z, c))
    block = jnp.stack([activations, after(came, *first_job)])
    blocks = {"z": block[None, :, :HALF], "y": block[None, :, HALF:]}
    blocks = lax.optimization_barrier(blocks)
    for which in (1, 2):
        blocks = {
            part: jnp.concatenate([v, exchange(v, "y" if part == "z" else "z", which)]) for part, v in blocks.items()
        }
        blocks = lax.optimization_barrier(blocks)
    blocks, second_job = lax.optimization_barrier((blocks, second_job))
    slots = {}
    for part, v in blocks.items():
        first = exchange(v, part, 1)
        second = exchange(after(v, third_job), part, 2)
        slots[part] = [v, first, second, exchange(after(first, third_job), part, 2)]
    return slots


AWAY, HERE, CORE, Y_SLOT, Z_SLOT, XH, Y, Z, DEST, WIDTH = 0, 8, 16, 17, 21, 25, 26, 27, 28, 32


def device_row(i):
    x, y, z, core = coords(i)
    xh, xl = x // 2, x % 2

    def chunks(l, c):
        return [l * 8 + (z + dz) % 4 * 2 + c for dz in range(4)]

    row = chunks(1 - xl, core) + chunks(1 - xl, 1 - core) + chunks(xl, 1 - core) + chunks(xl, core) + [core]
    row += [offset(s, y, core) for s in range(4)] + [offset(s, z, core) for s in range(4)]
    row += [xh, y, z] + [(xl ^ core) * 4 + (z + dz) % 4 for dz in range(4)]
    assert len(row) == WIDTH
    return row


def refit_kernel(first, table, master, *refs):
    outs, (held, sems) = refs[:-2], refs[-2:]
    copies = []
    for n in range(8):
        at = pl.multiple_of(table[first + n] * SHARE, SHARE)
        copies.append(pltpu.make_async_copy(master.at[pl.ds(at, SHARE)], held.at[n], sems.at[n]))
        copies[-1].start()
    tiles = SHARE // BLOCK
    for n in range(8):
        out = outs[n * len(outs) // 8]
        start = n * SHARE % out.shape[0]
        copies[n].wait()
        amax = jnp.max(jnp.abs(held[n]).reshape(tiles, BLOCK, COLS), axis=1)
        for c in range(COLS // BLOCK):
            cols = slice(c * BLOCK, (c + 1) * BLOCK)
            top = jnp.max(amax[:, cols], axis=1, keepdims=True)
            scales = ((top + 1e-6) / 448.0).astype(jnp.bfloat16).astype(jnp.float32)
            inverses = 1.0 / scales
            for r in range(tiles):
                tile = held[n, r * BLOCK : (r + 1) * BLOCK, cols]
                coded = (tile * inverses[r : r + 1]).astype(jnp.bfloat16)
                value = (coded.astype(jnp.float32) * scales[r : r + 1]).astype(jnp.bfloat16)
                out[start + r * BLOCK : start + (r + 1) * BLOCK, cols] = value


def refit(table, master, first, n_outs):
    size = 8 * SHARE * COLS
    return pl.pallas_call(
        functools.partial(refit_kernel, first),
        in_specs=[pl.BlockSpec(memory_space=pltpu.SMEM), pl.BlockSpec(memory_space=pltpu.HBM)],
        out_specs=[pl.BlockSpec(memory_space=pltpu.VMEM)] * n_outs,
        out_shape=[jax.ShapeDtypeStruct((8 * SHARE // n_outs, COLS), jnp.bfloat16)] * n_outs,
        scratch_shapes=[pltpu.VMEM((8, SHARE, COLS), jnp.float32), pltpu.SemaphoreType.DMA((8,))],
        compiler_params=pltpu.CompilerParams(vmem_limit_bytes=44 * MIB),
        cost_estimate=pl.CostEstimate(flops=size * 6, bytes_accessed=size * 6, transcendentals=0),
    )(table, master)


def dot(a, b):
    return jnp.dot(a, b, preferred_element_type=jnp.float32)


def pieces(core, mine, near, far, cross):
    def cols(at, c):
        return pl.ds(pl.multiple_of(at + c * COLS, COLS), COLS)

    return [(mine, cols(0, core)), (near, cols(0, 1 - core)), (far, cols(2 * COLS, core)), (cross, cols(2 * COLS, 1 - core))]


def dot(a, b):
    return jnp.dot(a, b, preferred_element_type=jnp.float32)


def depth_of(table, n):
    return pl.ds(pl.multiple_of(table[Z_SLOT + n] * SHARE, SHARE), SHARE)


EARLY, LATE = (0, 1, 2), 3


def early_kernel(count, table, *refs):
    weights, z_slots, y_slots, (z_out, y_out) = refs[:count], refs[count : count + 3], refs[count + 3 : -2], refs[-2:]
    for piece, weight in enumerate(weights):
        for half in range(2):
            got = None
            for n, slot in zip(EARLY, z_slots):
                term = dot(slot[:, half].reshape(4 * HALF, SHARE), weight[depth_of(table, n), :])
                got = term if got is None else got + term
            z_out[piece, half] = got
            got = None
            for n in range(4):
                term = dot(jnp.concatenate([slot[n, half] for slot in y_slots]), weight[depth_of(table, n), :])
                got = term if got is None else got + term
            y_out[piece, half] = got


def early_product(table, weights, slots):
    vmem = pl.BlockSpec(memory_space=pltpu.VMEM)
    parts = [slots[part][n] for part in "zy" for n in EARLY]
    count = len(weights)
    shapes = [(count, 2, 4 * HALF, COLS), (count, 2, 3 * HALF, COLS)]
    return pl.pallas_call(
        functools.partial(early_kernel, count),
        in_specs=[pl.BlockSpec(memory_space=pltpu.SMEM)] + [vmem] * (count + 6),
        out_specs=[vmem] * 2,
        out_shape=[jax.ShapeDtypeStruct(shape, jnp.float32) for shape in shapes],
        compiler_params=pltpu.CompilerParams(vmem_limit_bytes=24 * MIB),
        cost_estimate=pl.CostEstimate(flops=count * 2**30, bytes_accessed=16 * MIB, transcendentals=0),
    )(table, *weights, *parts)


def product_kernel(part, keep, table, mine, near, far, cross, *refs):
    slot, first, last, out = refs
    core = table[CORE]
    half = core if keep else 1 - core
    for piece, (weight, cols) in enumerate(pieces(core, mine, near, far, cross)):
        early = first.at[piece, half] if piece < 3 else last.at[0, half]
        if part == "z":
            got = early[...] + dot(slot[:, half].reshape(4 * HALF, SHARE), weight[depth_of(table, LATE), :])
            values = [got[ys * HALF : (ys + 1) * HALF] for ys in range(4)]
        else:
            got = None
            for n in range(4):
                term = dot(slot[n, half], weight[depth_of(table, n), :])
                got = term if got is None else got + term
            values = [early[pl.ds(n * HALF, HALF)] for n in range(3)] + [got]
        for ys in range(4):
            out[table[Y_SLOT + ys], :, cols] = values[ys].astype(out.dtype)


def product(part, keep, table, weights, slot, early):
    vmem = pl.BlockSpec(memory_space=pltpu.VMEM)
    return pl.pallas_call(
        functools.partial(product_kernel, part, keep),
        in_specs=[pl.BlockSpec(memory_space=pltpu.SMEM)] + [vmem] * 7,
        out_specs=vmem,
        out_shape=jax.ShapeDtypeStruct((4, HALF, 4 * COLS), jnp.float32 if keep else jnp.bfloat16),
        compiler_params=pltpu.CompilerParams(vmem_limit_bytes=24 * MIB),
        cost_estimate=pl.CostEstimate(flops=2**29, bytes_accessed=8 * MIB, transcendentals=0),
    )(table, *weights, slot, *early)


def spread_kernel(table, owner, own, other, *outs):
    for k, out in enumerate(outs):
        section = owner[table[DEST + k]]
        half = jnp.where(section >= 4, 1, 0)
        far = jnp.where(half == table[XH], 0, 1)
        at = (table[Y] + 8 - section) & 3

        @pl.when(far == table[CORE])
        def _():
            out[...] = own[at]

        @pl.when(far != table[CORE])
        def _():
            out[...] = other[at]


def arrange_kernel(table, *refs):
    parts, out, sems = refs[:8], refs[8], refs[9]
    copies = []
    for i, part in enumerate(parts):
        rows, dz = i // 4, i % 4
        at = pl.multiple_of(((table[Z] + 4 - dz) & 3) * (2 * COLS), 2 * COLS)
        to = out.at[pl.ds(rows * HALF, HALF), pl.ds(at, 2 * COLS)]
        copies.append(pltpu.make_async_copy(part, to, sems.at[i]))
        copies[-1].start()
    for copy in copies:
        copy.wait()


def small_call(kernel, scalars, parts, shapes, out_space, scratch=()):
    smem, vmem = pl.BlockSpec(memory_space=pltpu.SMEM), pl.BlockSpec(memory_space=pltpu.VMEM)
    return pl.pallas_call(
        kernel,
        in_specs=[smem] * len(scalars) + [vmem] * len(parts),
        out_specs=[pl.BlockSpec(memory_space=out_space)] * len(shapes),
        out_shape=[jax.ShapeDtypeStruct(shape, jnp.bfloat16) for shape in shapes],
        scratch_shapes=scratch,
        compiler_params=pltpu.CompilerParams(vmem_limit_bytes=16 * MIB),
        cost_estimate=pl.CostEstimate(flops=0, bytes_accessed=2 * MIB, transcendentals=0),
    )(*scalars, *parts)


def shards(master, activations, owner):
    f32, bf16 = jnp.float32, jnp.bfloat16
    rows = jnp.asarray(np.array([device_row(i) for i in range(N_DEV)], np.int32))
    me = lax.axis_index("group") * 16 + lax.axis_index("tp")
    table = lax.dynamic_index_in_dim(rows, me, 0, keepdims=False)

    same, swapped = refit(table, master, AWAY, 2)
    sent, mine = refit(table, master, HERE, 2)
    near = permute(sent, other_core)
    far = permute(same, other_chip)
    swapped = permute(swapped, other_core)
    slots = gather(activations, (same, mine), (near, swapped), far)
    cross = permute(after(swapped, far), other_chip)
    weights = [mine, near, far, cross]
    early = early_product(table, weights[:3], slots)
    early = dict(zip("zy", zip(early, early_product(after(table, *early), weights[3:], slots))))
    ready = after(table, slots["z"][LATE], slots["y"][LATE])

    def chain(part):
        passed = product(part, False, ready, weights, slots[part][LATE], early[part])
        kept = product(part, True, ready, weights, slots[part][LATE], early[part])
        both = kept + permute(passed, other_core).astype(f32)
        came = permute(both[..., 2 * COLS :].astype(bf16), other_chip)
        total = (both[..., : 2 * COLS] + came.astype(f32)).astype(bf16)
        got = {}
        for dy in (2, 1, 3, 0):
            got[dy] = permute(total[dy], lambda x, y, z, c: linear(x + 2 * c, y + dy, z, c))
        own = jnp.stack([got[dy] for dy in range(4)])
        other = permute(own, other_core)
        picked = small_call(spread_kernel, [table, owner], [own, other], [(HALF, 2 * COLS)] * 4, pltpu.VMEM)
        got = {}
        for dz in (2, 1, 3, 0):
            got[dz] = permute(picked[dz], lambda x, y, z, c: linear(x ^ c, y, z + dz, x % 2))
        return [got[dz] for dz in range(4)]

    blocks = chain("y")
    blocks = chain("z") + blocks
    return small_call(
        arrange_kernel, [table], blocks, [(256, 8 * COLS)], pltpu.HBM, [pltpu.SemaphoreType.DMA((8,))]
    )[0]


def solution(mesh):
    in_specs = (P(None, ("group", "tp")), P("group", "tp"), P())
    out_specs = P("group", "tp")
    return jax.shard_map(shards, mesh=mesh, in_specs=in_specs, out_specs=out_specs, check_vma=False)
```

```python
import functools

import jax
import jax.numpy as jnp
import numpy as np
from jax import lax
from jax.experimental import pallas as pl
from jax.experimental.pallas import tpu as pltpu
from jax.sharding import PartitionSpec as P

BLOCK = 128
AXES = ("group", "tp")
N_DEV = 128
SHARE = 512
COLS = 256
HALF = 128
MIB = 1024 * 1024


def coords(i):
    return i // 64 * 2 + i // 8 % 2, i // 16 % 4, i // 2 % 4, i % 2


def linear(x, y, z, core):
    x, y, z = x % 4, y % 4, z % 4
    return x // 2 * 64 + y * 16 + x % 2 * 8 + z * 2 + core


def permute(value, move):
    return lax.ppermute(value, AXES, [(i, move(*coords(i))) for i in range(N_DEV)])


def offset(slot, at, core):
    step = -1 if (at + core) % 2 else 1
    return (0, step, -step, 2)[slot] % 4


def exchange(value, axis, which):
    def move(x, y, z, core):
        at = {"x": x, "y": y, "z": z}
        at[axis] += offset(which, at[axis], core)
        return linear(at["x"], at["y"], at["z"], core)

    return permute(value, move)


def other_core(x, y, z, core):
    return linear(x, y, z, 1 - core)


def other_chip(x, y, z, core):
    return linear(x ^ 1, y, z, core)


def after(value, *others):
    return lax.optimization_barrier((value, *others))[0]


def gather(activations, first_job, second_job, third_job):
    came = permute(activations, lambda x, y, z, c: linear(x + 2, y, z, c))
    block = jnp.stack([activations, after(came, first_job)])
    blocks = {"z": block[None, :, :HALF], "y": block[None, :, HALF:]}
    blocks = lax.optimization_barrier(blocks)
    for which in (1, 2):
        blocks = {
            part: jnp.concatenate([v, exchange(v, "y" if part == "z" else "z", which)]) for part, v in blocks.items()
        }
        blocks = lax.optimization_barrier(blocks)
    blocks, second_job = lax.optimization_barrier((blocks, second_job))
    slots = {}
    for part, v in blocks.items():
        first = exchange(v, part, 1)
        second = exchange(after(v, third_job), part, 2)
        slots[part] = [v, first, second, exchange(after(first, third_job), part, 2)]
    return slots


AWAY, HERE, CORE, Y_SLOT, Z_SLOT, XH, Y, Z, DEST, WIDTH = 0, 8, 16, 17, 21, 25, 26, 27, 28, 32


def device_row(i):
    x, y, z, core = coords(i)
    xh, xl = x // 2, x % 2

    def chunks(l, c):
        return [l * 8 + (z + dz) % 4 * 2 + c for dz in range(4)]

    row = chunks(1 - xl, core) + chunks(1 - xl, 1 - core) + chunks(xl, 1 - core) + chunks(xl, core) + [core]
    row += [offset(s, y, core) for s in range(4)] + [offset(s, z, core) for s in range(4)]
    row += [xh, y, z] + [(xl ^ core) * 4 + (z + dz) % 4 for dz in range(4)]
    assert len(row) == WIDTH
    return row


def refit_kernel(first, table, master, *refs):
    outs, (held, sems) = refs[:-2], refs[-2:]
    copies = []
    for n in range(8):
        at = pl.multiple_of(table[first + n] * SHARE, SHARE)
        copies.append(pltpu.make_async_copy(master.at[pl.ds(at, SHARE)], held.at[n], sems.at[n]))
        copies[-1].start()
    tiles = SHARE // BLOCK
    for n in range(8):
        out = outs[n * len(outs) // 8]
        start = n * SHARE % out.shape[0]
        copies[n].wait()
        amax = jnp.max(jnp.abs(held[n]).reshape(tiles, BLOCK, COLS), axis=1)
        for c in range(COLS // BLOCK):
            cols = slice(c * BLOCK, (c + 1) * BLOCK)
            top = jnp.max(amax[:, cols], axis=1, keepdims=True)
            scales = ((top + 1e-6) / 448.0).astype(jnp.bfloat16).astype(jnp.float32)
            inverses = 1.0 / scales
            for r in range(tiles):
                tile = held[n, r * BLOCK : (r + 1) * BLOCK, cols]
                coded = (tile * inverses[r : r + 1]).astype(jnp.bfloat16)
                value = (coded.astype(jnp.float32) * scales[r : r + 1]).astype(jnp.bfloat16)
                out[start + r * BLOCK : start + (r + 1) * BLOCK, cols] = value


def refit(table, master, first, n_outs):
    size = 8 * SHARE * COLS
    return pl.pallas_call(
        functools.partial(refit_kernel, first),
        in_specs=[pl.BlockSpec(memory_space=pltpu.SMEM), pl.BlockSpec(memory_space=pltpu.HBM)],
        out_specs=[pl.BlockSpec(memory_space=pltpu.VMEM)] * n_outs,
        out_shape=[jax.ShapeDtypeStruct((8 * SHARE // n_outs, COLS), jnp.bfloat16)] * n_outs,
        scratch_shapes=[pltpu.VMEM((8, SHARE, COLS), jnp.float32), pltpu.SemaphoreType.DMA((8,))],
        compiler_params=pltpu.CompilerParams(vmem_limit_bytes=44 * MIB),
        cost_estimate=pl.CostEstimate(flops=size * 6, bytes_accessed=size * 6, transcendentals=0),
    )(table, master)


def dot(a, b):
    return jnp.dot(a, b, preferred_element_type=jnp.float32)


def pieces(core, mine, near, far, cross):
    def cols(at, c):
        return pl.ds(pl.multiple_of(at + c * COLS, COLS), COLS)

    return [(mine, cols(0, core)), (near, cols(0, 1 - core)), (far, cols(2 * COLS, core)), (cross, cols(2 * COLS, 1 - core))]


def dot(a, b):
    return jnp.dot(a, b, preferred_element_type=jnp.float32)


def depth_of(table, n):
    return pl.ds(pl.multiple_of(table[Z_SLOT + n] * SHARE, SHARE), SHARE)


EARLY, LATE = (0, 1, 2), 3


def early_kernel(count, table, *refs):
    weights, z_slots, y_slots, (z_out, y_out) = refs[:count], refs[count : count + 3], refs[count + 3 : -2], refs[-2:]
    for piece, weight in enumerate(weights):
        for half in range(2):
            got = None
            for n, slot in zip(EARLY, z_slots):
                term = dot(slot[:, half].reshape(4 * HALF, SHARE), weight[depth_of(table, n), :])
                got = term if got is None else got + term
            z_out[piece, half] = got
            got = None
            for n in range(4):
                term = dot(jnp.concatenate([slot[n, half] for slot in y_slots]), weight[depth_of(table, n), :])
                got = term if got is None else got + term
            y_out[piece, half] = got


def early_product(table, weights, slots):
    vmem = pl.BlockSpec(memory_space=pltpu.VMEM)
    parts = [slots[part][n] for part in "zy" for n in EARLY]
    count = len(weights)
    shapes = [(count, 2, 4 * HALF, COLS), (count, 2, 3 * HALF, COLS)]
    return pl.pallas_call(
        functools.partial(early_kernel, count),
        in_specs=[pl.BlockSpec(memory_space=pltpu.SMEM)] + [vmem] * (count + 6),
        out_specs=[vmem] * 2,
        out_shape=[jax.ShapeDtypeStruct(shape, jnp.float32) for shape in shapes],
        compiler_params=pltpu.CompilerParams(vmem_limit_bytes=24 * MIB),
        cost_estimate=pl.CostEstimate(flops=count * 2**30, bytes_accessed=16 * MIB, transcendentals=0),
    )(table, *weights, *parts)


def product_kernel(part, keep, table, mine, near, far, cross, *refs):
    slot, first, last, out = refs
    core = table[CORE]
    half = core if keep else 1 - core
    for piece, (weight, cols) in enumerate(pieces(core, mine, near, far, cross)):
        early = first.at[piece, half] if piece < 3 else last.at[0, half]
        if part == "z":
            got = early[...] + dot(slot[:, half].reshape(4 * HALF, SHARE), weight[depth_of(table, LATE), :])
            values = [got[ys * HALF : (ys + 1) * HALF] for ys in range(4)]
        else:
            got = None
            for n in range(4):
                term = dot(slot[n, half], weight[depth_of(table, n), :])
                got = term if got is None else got + term
            values = [early[pl.ds(n * HALF, HALF)] for n in range(3)] + [got]
        for ys in range(4):
            out[table[Y_SLOT + ys], :, cols] = values[ys].astype(out.dtype)


def product(part, keep, table, weights, slot, early):
    vmem = pl.BlockSpec(memory_space=pltpu.VMEM)
    return pl.pallas_call(
        functools.partial(product_kernel, part, keep),
        in_specs=[pl.BlockSpec(memory_space=pltpu.SMEM)] + [vmem] * 7,
        out_specs=vmem,
        out_shape=jax.ShapeDtypeStruct((4, HALF, 4 * COLS), jnp.float32 if keep else jnp.bfloat16),
        compiler_params=pltpu.CompilerParams(vmem_limit_bytes=24 * MIB),
        cost_estimate=pl.CostEstimate(flops=2**29, bytes_accessed=8 * MIB, transcendentals=0),
    )(table, *weights, slot, *early)


def spread_kernel(table, owner, own, other, *outs):
    for k, out in enumerate(outs):
        section = owner[table[DEST + k]]
        half = jnp.where(section >= 4, 1, 0)
        far = jnp.where(half == table[XH], 0, 1)
        at = (table[Y] + 8 - section) & 3

        @pl.when(far == table[CORE])
        def _():
            out[...] = own[at]

        @pl.when(far != table[CORE])
        def _():
            out[...] = other[at]


def arrange_kernel(table, *refs):
    parts, out, sems = refs[:4], refs[4], refs[5]
    copies = []
    for dz, part in enumerate(parts):
        at = pl.multiple_of(((table[Z] + 4 - dz) & 3) * (2 * COLS), 2 * COLS)
        copies.append(pltpu.make_async_copy(part, out.at[:, pl.ds(at, 2 * COLS)], sems.at[dz]))
        copies[-1].start()
    for copy in copies:
        copy.wait()


def small_call(kernel, scalars, parts, shapes, out_space, scratch=()):
    smem, vmem = pl.BlockSpec(memory_space=pltpu.SMEM), pl.BlockSpec(memory_space=pltpu.VMEM)
    return pl.pallas_call(
        kernel,
        in_specs=[smem] * len(scalars) + [vmem] * len(parts),
        out_specs=[pl.BlockSpec(memory_space=out_space)] * len(shapes),
        out_shape=[jax.ShapeDtypeStruct(shape, jnp.bfloat16) for shape in shapes],
        scratch_shapes=scratch,
        compiler_params=pltpu.CompilerParams(vmem_limit_bytes=16 * MIB),
        cost_estimate=pl.CostEstimate(flops=0, bytes_accessed=2 * MIB, transcendentals=0),
    )(*scalars, *parts)


def shards(master, activations, owner):
    f32, bf16 = jnp.float32, jnp.bfloat16
    rows = jnp.asarray(np.array([device_row(i) for i in range(N_DEV)], np.int32))
    me = lax.axis_index("group") * 16 + lax.axis_index("tp")
    table = lax.dynamic_index_in_dim(rows, me, 0, keepdims=False)

    same, swapped = refit(table, master, AWAY, 2)
    sent, mine = refit(table, master, HERE, 2)
    near = permute(sent, other_core)
    far = permute(same, other_chip)
    swapped = permute(swapped, other_core)
    slots = gather(activations, same, (near, swapped), far)
    cross = permute(after(swapped, far), other_chip)
    weights = [mine, near, far, cross]
    early = early_product(table, weights[:3], slots)
    early = dict(zip("zy", zip(early, early_product(after(table, *early), weights[3:], slots))))
    ready = after(table, slots["z"][LATE], slots["y"][LATE])

    def chain(part):
        passed = product(part, False, ready, weights, slots[part][LATE], early[part])
        kept = product(part, True, ready, weights, slots[part][LATE], early[part])
        both = kept + permute(passed, other_core).astype(f32)
        came = permute(both[..., 2 * COLS :].astype(bf16), other_chip)
        total = (both[..., : 2 * COLS] + came.astype(f32)).astype(bf16)
        got = {}
        for dy in (2, 1, 3, 0):
            got[dy] = permute(total[dy], lambda x, y, z, c: linear(x + 2 * c, y + dy, z, c))
        own = jnp.stack([got[dy] for dy in range(4)])
        return own

    own = chain("y")
    own = jnp.concatenate([chain("z"), own], axis=1)
    other = permute(own, other_core)

    picked = small_call(spread_kernel, [table, owner], [own, other], [(256, 2 * COLS)] * 4, pltpu.VMEM)
    got = {}
    for dz in (2, 1, 3, 0):
        got[dz] = permute(picked[dz], lambda x, y, z, c: linear(x ^ c, y, z + dz, x % 2))
    got = [got[dz] for dz in range(4)]
    return small_call(arrange_kernel, [table], got, [(256, 8 * COLS)], pltpu.HBM, [pltpu.SemaphoreType.DMA((4,))])[0]


def solution(mesh):
    in_specs = (P(None, ("group", "tp")), P("group", "tp"), P())
    out_specs = P("group", "tp")
    return jax.shard_map(shards, mesh=mesh, in_specs=in_specs, out_specs=out_specs, check_vma=False)
```
